32 devices in a mesh: seq: 2 (over x), rows: 4 (over z), col: 4 (over y, core).
Axes of the slice: x: 2, y: 2, z: 4, core: 2. Of those that a mesh axis runs over, the one named last changes fastest.
Arguments:
- tokens: bfloat16 [16, 512, 768], P(('rows', 'col'), 'seq'), may hold values from -6 to 6
- lengths: int32 [16, 4], P(('rows', 'col')), may hold values from 1 to 320, 512 in all within a row
- qkv_weight: bfloat16 [2, 3, 768, 768], replicated, may hold values from -0.21875 to 0.21875
- out_weight: bfloat16 [2, 768, 768], replicated, may hold values from -0.875 to 0.875
- rel_table: bfloat16 [2, 512, 768], replicated, may hold values from -5 to 5
- ffn_in: bfloat16 [2, 768, 3072], P(None, None, 'col'), may hold values from -0.21875 to 0.21875
- ffn_out: bfloat16 [2, 768, 3072], P(None, None, 'col'), may hold values from -0.109375 to 0.109375
- norm_params: float32 [2, 4, 768], replicated, may hold values from -0.8 to 1.4, as said below
- cotangent: bfloat16 [16, 512, 768], P(('rows', 'col'), 'seq'), may hold values from -6 to 6
Outputs:
- output: float32 [16, 512, 768], P(('rows', 'col'), 'seq')
- input_grad: float32 [16, 512, 768], P(('rows', 'col'), 'seq')
- grad_qkv: float32 [2, 3, 768, 768], P(None, None, ('seq', 'rows'), 'col')
- grad_out: float32 [2, 768, 768], P(None, ('seq', 'rows'), 'col')
- grad_rel: float32 [2, 512, 768], P(None, ('seq', 'rows'), 'col')
- grad_ffn_in: float32 [2, 768, 3072], P(None, ('seq', 'rows'), 'col')
- grad_ffn_out: float32 [2, 768, 3072], P(None, ('seq', 'rows'), 'col')
- grad_norms: float32 [2, 4, 768], P(None, 'col', ('seq', 'rows'))
The draws below stay inside these ranges and needn't reach their ends.
Inputs may be any that keep to these rules, and one draw needn't show every extreme that they name: Each row's 4 document lengths sum to 512, and the longest of each row has exactly 320 tokens. `norm_params`: rows 0 and 2 of each layer are gains, rows 1 and 3 biases.
All inputs are finite; a program needn't handle non-finite values.
Results may differ from the reference program's by a relative error of at most 0.03.
Values may be sent and summed in bfloat16 or wider, within the bound.
No kernel may reach another device: no remote copies, remote signals or barrier semaphores. Data moves between devices by JAX's collectives and lax.ppermute only.
A program may use at most 256 MiB of HBM per device.

```python
import math
import jax
import jax.numpy as jnp
import numpy as np
from jax import lax

D = 768
HEADS = 12
HEAD_DIM = 64
FF = 3072
SPAN = 256
MAX_REL = 512
L = 512
DOCS = 4
DOC_MOST = 320
ROWS = 16


def draw_norm_params(key, part):
    key = jax.random.fold_in(key, 7)
    values = jax.random.uniform(key, (2, 4, D), jnp.float32)
    kind_rows = lax.broadcasted_iota(jnp.int32, (2, 4, D), 1) % 2
    gain_rows = 0.6 + 0.8 * values
    biases = 1.6 * values - 0.8
    return jnp.where(kind_rows == 0, gain_rows, biases)


def block_levels(own_key, extent, shards, smallest, top_value):
    def one(axis_at, parts):
        draws = jax.random.uniform(jax.random.fold_in(jax.random.fold_in(own_key, 6), axis_at), (parts,), jnp.float32, smallest / len(shards), top_value / len(shards))
        return jnp.repeat(jnp.exp(draws), extent[axis_at] // parts).reshape((-1,) + (1,) * (len(extent) - axis_at - 1))

    level = one(*shards[0])
    for cut in shards[1:]:
        level = level * one(*cut)
    return level


def length_profile(number_of, total, reach, lean):
    loads = [(1 << 20) // math.isqrt(rank ** lean) + 1 for rank in range(2, number_of + 1)]
    rest, holding = total - reach - (number_of - 1), [1] * (number_of - 1)
    while rest > 0:
        candidates = [i for i in range(number_of - 1) if holding[i] < reach]
        pool, left = sum([loads[i] for i in candidates]), rest
        for i in candidates:
            addition = min(reach - holding[i], max(1, left * loads[i] // pool), rest)
            holding[i] = holding[i] + addition
            rest = rest - addition
    return np.array([reach] + holding)


def uneven(own_key, count, total, bound, lean):
    if count == 2:
        one = jax.random.randint(own_key, (), max(1, total - bound), min(bound, total - 1) + 1)
        return jnp.stack([one, total - one])
    tallies = jnp.asarray(length_profile(count, total, bound, lean), jnp.int32)
    pairs = (count - 1) // 2
    giver, sink = tallies[1:1 + 2 * pairs:2], tallies[2:2 + 2 * pairs:2]
    room = jnp.minimum(giver - 1, bound - sink)
    shifted = jax.random.randint(jax.random.fold_in(own_key, 1), (pairs,), 0, 1 << 20) % (room + 1)
    tallies = tallies.at[1:1 + 2 * pairs:2].set(giver - shifted).at[2:2 + 2 * pairs:2].set(sink + shifted)
    return tallies[jax.random.permutation(jax.random.fold_in(own_key, 2), count)]


def centred(stream_key, shape, scale, bound, pieces=(), kind=jnp.bfloat16):
    drawn = jax.random.normal(stream_key, shape, jnp.float32) * scale
    if len(pieces) > 0:
        drawn = block_levels(stream_key, shape, pieces, -0.22, 0.18) * drawn
    return jnp.clip(drawn, min=-bound, max=bound).astype(kind)


def setup_inputs(seed: int = 0) -> dict:
    keys = jax.random.split(jax.random.key(seed), 10)
    return {
        "tokens": centred(keys[0], (ROWS, L, D), 1.0, 6.0, ((0, 16), (1, 2))),
        "lengths": jax.vmap(lambda own: uneven(own, DOCS, L, DOC_MOST, 0))(jax.random.split(keys[1], ROWS)).reshape((ROWS, DOCS)).astype(jnp.int32),
        "qkv_weight": centred(keys[2], (2, 3, D, D), D ** -0.5, 0.21875),
        "out_weight": centred(keys[3], (2, D, D), (D // 16) ** -0.5, 0.875),
        "rel_table": centred(keys[4], (2, 2 * SPAN, D), 1.0, 5.0),
        "ffn_in": centred(keys[5], (2, D, FF), D ** -0.5, 0.21875, ((2, 4),)),
        "ffn_out": centred(keys[6], (2, D, FF), FF ** -0.5, 0.109375, ((2, 4),)),
        "norm_params": draw_norm_params(jax.random.fold_in(keys[9], 71), 0),
        "cotangent": centred(keys[8], (ROWS, L, D), 1.0, 6.0, ((0, 16), (1, 2))),
    }


@jax.custom_vjp
def low(v):
    return lax.optimization_barrier(v.astype(jnp.bfloat16)).astype(jnp.float32)

@jax.custom_vjp
def low_back(v):
    return v

def low_keep(v):
    return (low(v), None)

def low_pass(kept, grad):
    return (grad,)

def back_keep(v):
    return (v, None)

def back_low(kept, grad):
    return (low(grad),)
low.defvjp(low_keep, low_pass)
low_back.defvjp(back_keep, back_low)
HIGHEST = lax.Precision.HIGHEST
NEGATIVE = -1000000000.0
EPSILON = 1e-07

def bucket_matrix(length, span_size, max_relative):
    relative = np.arange(length)[:, None] - np.arange(length)[None, :]
    middle = span_size // 2
    absolute = np.where((relative < middle) & (relative > -middle), middle - 1, np.abs(relative))
    log_position = np.ceil(np.log(absolute / middle) / np.log((max_relative - 1) / middle) * (middle - 1)) + middle
    bucket = np.where(absolute <= middle, relative, log_position * np.sign(relative))
    return np.clip(bucket + span_size, 0, 2 * span_size - 1).astype(np.int32)

def layer_norm(stream, gain_row, bias_row):
    row_mean = lax.optimization_barrier(jnp.mean(stream, axis=-1, keepdims=True))
    centered = stream - row_mean
    row_var = lax.optimization_barrier(jnp.mean(centered * centered, axis=-1, keepdims=True))
    return centered * lax.rsqrt(row_var + EPSILON) * gain_row + bias_row

def both_ways(values):
    return low_back(low(values))

def encoder_layer(stream, same_doc, bucket_rows, qkv, w_out, rel, w_in, w_down, norm_rows):
    groups = stream.shape[0]
    score_scale = (3.0 * HEAD_DIM) ** (-0.5)
    flat_in = low(stream)
    projected = jnp.einsum('gld,cde->cgle', flat_in, qkv, precision=HIGHEST)
    queries = both_ways(projected[0]).reshape(groups, L, HEADS, HEAD_DIM)
    keys_all = both_ways(projected[1]).reshape(groups, L, HEADS, HEAD_DIM)
    values_all = both_ways(projected[2]).reshape(groups, L, HEADS, HEAD_DIM)
    rel_low = low(rel)
    pos_query = low(jnp.dot(rel_low, qkv[0], precision=HIGHEST)).reshape(2 * SPAN, HEADS, HEAD_DIM)
    pos_key = low(jnp.dot(rel_low, qkv[1], precision=HIGHEST)).reshape(2 * SPAN, HEADS, HEAD_DIM)
    content = jnp.einsum('gihe,gjhe->ghij', queries, keys_all, precision=HIGHEST)
    content_pos_all = jnp.einsum('gihe,bhe->ghib', queries, pos_key, precision=HIGHEST)
    content_pos = jnp.take_along_axis(content_pos_all, jnp.broadcast_to(bucket_rows, content.shape), axis=3)
    pos_content_all = jnp.einsum('gjhe,bhe->ghjb', keys_all, pos_query, precision=HIGHEST)
    pos_content = jnp.swapaxes(jnp.take_along_axis(pos_content_all, jnp.broadcast_to(bucket_rows, content.shape), axis=3), 2, 3)
    scores = low_back(jnp.where(same_doc, (content + content_pos + pos_content) * score_scale, NEGATIVE))
    soft_rows = jax.nn.softmax(scores, axis=-1)
    attended = jnp.einsum('ghij,gjhe->gihe', low(soft_rows), values_all, precision=HIGHEST)
    attended = both_ways(attended.reshape(groups, L, D))
    branch = low_back(jnp.einsum('gld,de->gle', attended, w_out, precision=HIGHEST))
    middle_state = layer_norm(stream + branch, norm_rows[0], norm_rows[1])
    ffn_rows = low(middle_state)
    hidden = low_back(jnp.einsum('gld,df->glf', ffn_rows, w_in, precision=HIGHEST))
    activated = low(jax.nn.gelu(hidden, approximate=False))
    ffn_branch = low_back(jnp.einsum('glf,df->gld', activated, w_down, precision=HIGHEST))
    return layer_norm(middle_state + ffn_branch, norm_rows[2], norm_rows[3])

def reference(tokens, lengths, qkv_weight, out_weight, rel_table, ffn_in, ffn_out, norm_params, cotangent):
    group_rows = 4
    params = tuple((item.astype(jnp.float32) for item in (qkv_weight, out_weight, rel_table, ffn_in, ffn_out, norm_params)))
    bucket_rows = jnp.asarray(bucket_matrix(L, SPAN, MAX_REL))
    count_groups = tokens.shape[0] // group_rows

    def one_group(totals, group_items):
        block_rows, block_lengths, block_cot = group_items
        doc_ends = jnp.cumsum(block_lengths, axis=1)
        positions = jnp.arange(L, dtype=jnp.int32)
        doc_ids = lax.optimization_barrier(jnp.sum((positions[None, :, None] >= doc_ends[:, None, :]).astype(jnp.int32), axis=2))
        same_doc = (doc_ids[:, :, None] == doc_ids[:, None, :])[:, None]

        def forward(stream, weights):
            qkv, w_out, rel, w_in, w_down, norm_rows = weights
            for layer_num in range(2):
                stream = encoder_layer(stream, same_doc, bucket_rows, qkv[layer_num], w_out[layer_num], rel[layer_num], w_in[layer_num], w_down[layer_num], norm_rows[layer_num])
            return stream
        result, pull_back = jax.vjp(forward, block_rows.astype(jnp.float32), params)
        d_stream, d_params = pull_back(block_cot.astype(jnp.float32))
        totals = jax.tree.map(jnp.add, totals, d_params)
        return (totals, (result, d_stream))
    zeros_init = jax.tree.map(jnp.zeros_like, params)
    totals, (results, d_inputs) = lax.scan(one_group, zeros_init, (tokens.reshape(count_groups, group_rows, L, D), lengths.reshape(count_groups, group_rows, DOCS), cotangent.reshape(count_groups, group_rows, L, D)))
    return (results.reshape(tokens.shape), d_inputs.reshape(tokens.shape), totals[0], totals[1], totals[2], totals[3], totals[4], totals[5])
```

```python
import functools
import jax
import jax.numpy as jnp
import numpy as np
from jax import lax
from jax.experimental import pallas as pl
from jax.experimental.pallas import tpu as pltpu
from jax.sharding import PartitionSpec as P

HEAD_DIM = 64
SPAN = 256
MAX_REL = 512
WIDE = 640
HALF = 320
BF = jnp.bfloat16
F32 = jnp.float32
SCALE = (3.0 * HEAD_DIM) ** (-0.5)
LOG2E = 1.4426950408889634

NT = (((1,), (1,)), ((), ()))
NN = (((1,), (0,)), ((), ()))
TN = (((0,), (0,)), ((), ()))

def dot(a, b, dims=NN):
    return lax.dot_general(a, b, dims, preferred_element_type=F32)

def bucket_table():
    r = HALF - np.arange(WIDE)
    middle = SPAN // 2
    a = np.where((r < middle) & (r > -middle), middle - 1, np.abs(r))
    logp = np.ceil(np.log(a / middle) / np.log((MAX_REL - 1) / middle) * (middle - 1)) + middle
    b = np.where(a <= middle, r, logp * np.sign(r))
    b = np.clip(b + SPAN, 0, 2 * SPAN - 1).astype(np.int32)
    return (b[:, None] == np.arange(2 * SPAN)[None, :]).astype(np.float32)

def fwd_kernel(ends_ref, x_ref, w_ref, pe_ref, rev_ref, o_ref, sv_ref, p_ref, bt_ref, sb_ref, *, length, blk):
    e1, e2, e3 = ends_ref[0], ends_ref[1], ends_ref[2]
    qkv = dot(x_ref[...], w_ref[0]).astype(BF)
    q, k, v = qkv[:, :128], qkv[:, 128:256], qkv[:, 256:]
    sv_ref[0, :, :128] = q
    sb_ref[...] = qkv
    sv_ref[0, :, 128:] = dot(rev_ref[...], qkv[:, 128:]).astype(BF)
    lane = lax.broadcasted_iota(jnp.int32, (1, 128), 1)
    posj = lax.broadcasted_iota(jnp.int32, (1, length), 1)
    idj = (posj >= e1).astype(jnp.int32) + (posj >= e2).astype(jnp.int32) + (posj >= e3).astype(jnp.int32)
    for h in range(2):
        own = (lane < 64) if h == 0 else (lane >= 64)
        kh = jnp.where(own, sb_ref[:, 128:256], jnp.zeros((), BF))
        for b in range(length // blk):
            sl = slice(b * blk, (b + 1) * blk)
            t2 = dot(kh[sl], pe_ref[0, 0], NT)
            t2 = pltpu.roll(t2, (b * blk + HALF) % WIDE, 1, stride=1, stride_axis=0)
            bt_ref[:, sl] = t2[:, :length].T
        for b in range(length // blk):
            sl = slice(b * blk, (b + 1) * blk)
            qb = jnp.where(own, sb_ref[sl, :128], jnp.zeros((), BF))
            t1 = dot(qb, pe_ref[0, 1], NT)
            t1 = pltpu.roll(t1, (b * blk + HALF) % WIDE, 1, stride=1, stride_axis=0)
            s = dot(qb, sb_ref[:, 128:256], NT) + t1[:, :length] + bt_ref[sl, :]
            posi = lax.broadcasted_iota(jnp.int32, (blk, 1), 0) + b * blk
            idi = (posi >= e1).astype(jnp.int32) + (posi >= e2).astype(jnp.int32) + (posi >= e3).astype(jnp.int32)
            s = jnp.where(idi == idj, s, -1e30)
            m = jnp.max(s, axis=1, keepdims=True)
            e = jnp.exp2((s - m) * (SCALE * LOG2E))
            p = (e * (1.0 / jnp.sum(e, axis=1, keepdims=True))).astype(BF)
            o = dot(p, sb_ref[:, 256:])
            if h == 0:
                o_ref[sl, :] = o.astype(BF)
            else:
                o_ref[sl, :] = jnp.where(own, o.astype(BF), o_ref[sl, :])
            p_ref[h, sl, :] = dot(p, rev_ref[...]).astype(BF)

def attn_fwd(ends, x, w, pe, rev):
    length = x.shape[0]
    model = x.shape[1]
    pairs = w.shape[0]
    return pl.pallas_call(
        functools.partial(fwd_kernel, length=length, blk=128),
        out_shape=(
            jax.ShapeDtypeStruct((length, pairs * 128), BF),
            jax.ShapeDtypeStruct((pairs, length, 384), BF),
            jax.ShapeDtypeStruct((2 * pairs, length, length), BF),
        ),
        grid_spec=pltpu.PrefetchScalarGridSpec(
            num_scalar_prefetch=1,
            grid=(pairs,),
            in_specs=[
                pl.BlockSpec((length, model), lambda g, e: (0, 0)),
                pl.BlockSpec((1, model, 384), lambda g, e: (g, 0, 0)),
                pl.BlockSpec((1, 2, WIDE, 128), lambda g, e: (g, 0, 0, 0)),
                pl.BlockSpec((length, length), lambda g, e: (0, 0)),
            ],
            out_specs=(
                pl.BlockSpec((length, 128), lambda g, e: (0, g)),
                pl.BlockSpec((1, length, 384), lambda g, e: (g, 0, 0)),
                pl.BlockSpec((2, length, length), lambda g, e: (g, 0, 0)),
            ),
            scratch_shapes=[pltpu.VMEM((length, length), F32), pltpu.VMEM((length, 384), BF)],
        ),
        compiler_params=pltpu.CompilerParams(vmem_limit_bytes=48 << 20),
        name="attention",
    )(ends, x, w, pe, rev)


def bwd_kernel(drb_ref, wo_ref, sv_ref, p_ref, pe_ref, rev_ref, wt_ref, dq_ref, dpe_ref, dx_ref, dt_ref, u_ref, acc_ref, *, length, blk):
    g = pl.program_id(0)
    lane = lax.broadcasted_iota(jnp.int32, (1, 128), 1)
    zero = jnp.zeros((), BF)
    dO = dot(drb_ref[...], wo_ref[...], NT).astype(BF)
    q = sv_ref[0, :, :128]
    dOT, qT, krT = dO.T, q.T, sv_ref[0, :, 128:256].T
    nb = length // blk
    for h in range(2):
        own = (lane < 64) if h == 0 else (lane >= 64)
        hs = slice(64 * h, 64 * h + 64)
        krh = jnp.where(own, sv_ref[0, :, 128:256], zero)
        pkh = jnp.where(own, pe_ref[0, 1], zero)
        for b in range(nb):
            sl = slice(b * blk, (b + 1) * blk)
            dOb = jnp.where(own, dO[sl], zero)
            da = dot(dOb, sv_ref[0, :, 256:], NT)
            p = p_ref[h, sl, :].astype(F32)
            delta = jnp.sum(p * da, axis=1, keepdims=True)
            ds = p * (da - delta)
            dsb = ds.astype(BF)
            ds = dsb.astype(F32)
            dt_ref[:, sl] = ds.T
            u = jnp.concatenate([ds, jnp.zeros((blk, WIDE - length), F32)], axis=1)
            u = pltpu.roll(u, (b * blk + WIDE - 192) % WIDE, 1, stride=1, stride_axis=0).astype(BF)
            u_ref[sl, :] = u
            r = dot(dsb, krh) + dot(u, pkh)
            if h == 0:
                acc_ref[sl, :128] = r
            else:
                acc_ref[sl, :128] = acc_ref[sl, :128] + r
        dpe_ref[0, 1, hs, :] = dot(qT[hs], u_ref[...])
        acc_ref[:, 256:384] = (acc_ref[:, 256:384] if h else 0.0) + dot(p_ref[h], jnp.where(own, dO, zero), TN)
        qh = jnp.where(own, q, zero)
        pqh = jnp.where(own, pe_ref[0, 0], zero)
        for b in range(nb):
            sl = slice(b * blk, (b + 1) * blk)
            z = dt_ref[sl, :]
            w = jnp.concatenate([z, jnp.zeros((blk, WIDE - length), F32)], axis=1)
            w = pltpu.roll(w, (b * blk + WIDE - 191) % WIDE, 1, stride=1, stride_axis=0).astype(BF)
            u_ref[sl, :] = w
            r = dot(z.astype(BF), qh) + dot(w, pqh)
            if h == 0:
                acc_ref[sl, 128:256] = r
            else:
                acc_ref[sl, 128:256] = acc_ref[sl, 128:256] + r
        dpe_ref[0, 0, hs, :] = dot(krT[hs], u_ref[...])
    dq = (acc_ref[:, :128] * SCALE).astype(BF)
    dk = (acc_ref[:, 128:256] * SCALE).astype(BF)
    dv = acc_ref[:, 256:384].astype(BF)
    dkv = dot(rev_ref[...], jnp.concatenate([dk, dv], axis=1)).astype(BF)
    dqkv = jnp.concatenate([dq, dkv], axis=1)
    dq_ref[0] = dqkv
    part = dot(dqkv, wt_ref[0], NT)
    @pl.when(g == 0)
    def _():
        dx_ref[...] = part
    @pl.when(g > 0)
    def _():
        dx_ref[...] = dx_ref[...] + part

def attn_bwd(drb, wo, saved, probs, pe, rev, w):
    length, model = drb.shape
    pairs = w.shape[0]
    return pl.pallas_call(
        functools.partial(bwd_kernel, length=length, blk=128),
        out_shape=(
            jax.ShapeDtypeStruct((pairs, length, 384), BF),
            jax.ShapeDtypeStruct((pairs, 2, 128, WIDE), F32),
            jax.ShapeDtypeStruct((length, model), F32),
        ),
        grid=(pairs,),
        in_specs=[
            pl.BlockSpec((length, model), lambda g: (0, 0)),
            pl.BlockSpec((128, model), lambda g: (g, 0)),
            pl.BlockSpec((1, length, 384), lambda g: (g, 0, 0)),
            pl.BlockSpec((2, length, length), lambda g: (g, 0, 0)),
            pl.BlockSpec((1, 2, WIDE, 128), lambda g: (g, 0, 0, 0)),
            pl.BlockSpec((length, length), lambda g: (0, 0)),
            pl.BlockSpec((1, model, 384), lambda g: (g, 0, 0)),
        ],
        out_specs=(
            pl.BlockSpec((1, length, 384), lambda g: (g, 0, 0)),
            pl.BlockSpec((1, 2, 128, WIDE), lambda g: (g, 0, 0, 0)),
            pl.BlockSpec((length, model), lambda g: (0, 0)),
        ),
        scratch_shapes=[pltpu.VMEM((length, length), F32), pltpu.VMEM((length, WIDE), BF), pltpu.VMEM((length, 384), F32)],
        compiler_params=pltpu.CompilerParams(vmem_limit_bytes=48 << 20),
        name="attention_grad",
    )(drb, wo, saved, probs, pe, rev, w)

EPSILON = 1e-07


def layer_norm(stream, gain_row, bias_row):
    row_mean = jnp.mean(stream, axis=-1, keepdims=True)
    centered = stream - row_mean
    row_var = jnp.mean(centered * centered, axis=-1, keepdims=True)
    return centered * lax.rsqrt(row_var + EPSILON) * gain_row + bias_row


def norm_back(state, gain_row, bias_row, d_result):
    unused_out, pull_back = jax.vjp(layer_norm, state, gain_row, bias_row)
    return pull_back(d_result)


def gelu_slope(hidden):
    cumulative = 0.5 * (1.0 + lax.erf(hidden * 0.7071067811865476))
    density = jnp.exp(-0.5 * hidden * hidden) * 0.3989422804014327
    return cumulative + hidden * density


class Wires:
    def __init__(self):
        self.seqs = lax.axis_size("seq")
        self.rows = lax.axis_size("rows")
        self.cols = lax.axis_size("col")
        self.seq = lax.axis_index("seq")
        self.row = lax.axis_index("rows")
        self.col = lax.axis_index("col")
        self.core = self.col % 2

    def send(self, array, target):
        pairs = []
        for s in range(self.seqs):
            for r in range(self.rows):
                for c in range(self.cols):
                    t = target(s, r, c)
                    if t is not None:
                        pairs.append(((s * self.rows + r) * self.cols + c, (t[0] * self.rows + t[1]) * self.cols + t[2]))
        return lax.ppermute(array, ("seq", "rows", "col"), pairs)

    def turn(self, array):
        return self.send(array, lambda s, r, c: (c % 2, r, c - c % 2 + s))

    def core_swap(self, array):
        return self.send(array, lambda s, r, c: (s, r, c ^ 1))

    def in_order(self, own, other, axis):
        first = self.core == 0
        return jnp.concatenate([jnp.where(first, own, other), jnp.where(first, other, own)], axis=axis)


def ffn_forward(middle_state, w_in, w_down):
    ffn_rows = middle_state.astype(BF)
    gathered = lax.all_gather(ffn_rows, "col", axis=0, tiled=True)
    hidden = jnp.dot(gathered, w_in, preferred_element_type=F32)
    activated = jax.nn.gelu(hidden, approximate=False).astype(BF)
    part = jnp.einsum("tf,df->td", activated, w_down, preferred_element_type=F32).astype(BF)
    branch = lax.psum_scatter(part, "col", scatter_dimension=0, tiled=True).astype(F32)
    return branch, gathered


def ffn_backward(d_rows, source_rows, w_in, w_down):
    cot_rows = lax.all_gather(d_rows, "col", axis=0, tiled=True)
    hidden = jnp.dot(source_rows, w_in, preferred_element_type=F32)
    activated = jax.nn.gelu(hidden, approximate=False).astype(BF)
    d_hidden = (jnp.dot(cot_rows, w_down, preferred_element_type=F32) * gelu_slope(hidden)).astype(BF)
    grad_down = jnp.einsum("td,tf->df", cot_rows, activated, preferred_element_type=F32)
    grad_in = jnp.einsum("td,tf->df", source_rows, d_hidden, preferred_element_type=F32)
    part = jnp.einsum("tf,df->td", d_hidden, w_in, preferred_element_type=F32).astype(BF)
    d_middle = lax.psum_scatter(part, "col", scatter_dimension=0, tiled=True).astype(F32)
    return d_middle, grad_in, grad_down


def per_device(tokens, lengths, qkv_weight, out_weight, rel_table, ffn_in, ffn_out, norm_params, cotangent):
    wires = Wires()
    core = wires.core
    local, model = tokens.shape[1:]
    length = 2 * local
    layers = qkv_weight.shape[0]
    half = model // 2
    block = model // wires.cols
    pairs = half // 128
    table = jnp.asarray(bucket_table(), BF)
    rev = jnp.asarray(np.eye(length)[::-1], BF)
    start = wires.turn(tokens[0])
    ends = jnp.cumsum(wires.turn(lengths)[0])
    d_final = wires.turn(cotangent[0])

    def own_blocks(array, axis, which):
        shape = array.shape
        cut = array.reshape(shape[:axis] + (wires.cols // 2, 2, block) + shape[axis + 1:])
        cut = lax.dynamic_index_in_dim(cut, which, axis + 1, keepdims=False)
        return cut.reshape(shape[:axis] + (half,) + shape[axis + 1:])

    qkv_own = own_blocks(qkv_weight, 3, core)
    out_own = own_blocks(out_weight, 1, core)
    out_other = own_blocks(out_weight, 1, 1 - core)
    w_pairs = qkv_own.reshape(layers, 3, model, pairs, 128).transpose(0, 3, 2, 1, 4).reshape(layers, pairs, model, 384)
    pos = jnp.einsum("nbd,ncde->ncbe", rel_table, qkv_own[:, :2], preferred_element_type=F32).astype(BF)
    ext = jnp.einsum("ub,ncbe->ncue", table, pos, preferred_element_type=F32).astype(BF)
    pe_fwd = ext.reshape(layers, 2, WIDE, pairs, 128).transpose(0, 3, 1, 2, 4)
    ext_b = jnp.einsum("ub,nbe->nue", table[::-1], pos[:, 1], preferred_element_type=F32).astype(BF)
    pe_bwd = jnp.stack([ext[:, 0], ext_b], axis=1).reshape(layers, 2, WIDE, pairs, 128).transpose(0, 3, 1, 2, 4)

    stream = start.astype(F32)
    kept = []
    for n in range(layers):
        norm_rows = norm_params[n]
        x_own = stream.astype(BF)
        x_full = wires.in_order(x_own, wires.core_swap(x_own), 0)
        o_own, saved, probs = attn_fwd(ends, x_full, w_pairs[n], pe_fwd[n], rev)
        o_other = wires.core_swap(o_own)
        o_mine = lax.dynamic_slice_in_dim(o_own, core * local, local, 0)
        o_rest = lax.dynamic_slice_in_dim(o_other, core * local, local, 0)
        branch = dot(o_mine, out_own[n]) + dot(o_rest, out_other[n])
        resid = stream + branch
        middle = layer_norm(resid, norm_rows[0], norm_rows[1])
        ffn_branch, gathered = ffn_forward(middle, ffn_in[n], ffn_out[n])
        pre_norm = middle + ffn_branch
        stream = layer_norm(pre_norm, norm_rows[2], norm_rows[3])
        kept.append((x_full, o_own, o_other, saved, probs, resid, gathered, pre_norm))
    output = wires.turn(stream)
    d_stream = d_final.astype(F32)
    grads = [None] * layers
    chunks = wires.seqs * wires.rows
    for n in reversed(range(layers)):
        norm_rows = norm_params[n]
        x_full, o_own, o_other, saved, probs, resid, gathered, pre_norm = kept[n]
        d_pre, d_gain_two, d_bias_two = norm_back(pre_norm, norm_rows[2], norm_rows[3], d_stream)
        d_middle, grad_in, grad_down = ffn_backward(d_pre.astype(BF), gathered, ffn_in[n], ffn_out[n])
        d_resid, d_gain_one, d_bias_one = norm_back(resid, norm_rows[0], norm_rows[1], d_pre + d_middle)
        d_branch = d_resid.astype(BF)
        d_branch_full = wires.in_order(d_branch, wires.core_swap(d_branch), 0)
        d_qkv, d_ext, d_x = attn_bwd(d_branch_full, out_own[n], saved, probs, pe_bwd[n], rev, w_pairs[n])
        d_mine = lax.dynamic_slice_in_dim(d_x, core * local, local, 0)
        d_theirs = lax.dynamic_slice_in_dim(d_x, (1 - core) * local, local, 0)
        d_stream = d_resid + d_mine + wires.core_swap(d_theirs.astype(BF)).astype(F32)

        g_qkv = jnp.einsum("ld,plce->cdpe", x_full, d_qkv.reshape(pairs, length, 3, 128), preferred_element_type=F32)
        g_qkv = g_qkv.reshape(3, model, half)
        d_ext = (d_ext * SCALE).astype(BF)
        d_pq = jnp.einsum("peu,ub->peb", d_ext[:, 0], table, preferred_element_type=F32).astype(BF).reshape(half, -1)
        d_pk = jnp.einsum("peu,ub->peb", d_ext[:, 1], table[::-1], preferred_element_type=F32).astype(BF).reshape(half, -1)
        g_pos = jnp.stack([
            jnp.einsum("bd,eb->de", rel_table[n], d_pq, preferred_element_type=F32),
            jnp.einsum("bd,eb->de", rel_table[n], d_pk, preferred_element_type=F32),
        ])
        g_qkv = jnp.concatenate([g_qkv[:2] + g_pos, g_qkv[2:]], axis=0)
        g_rel = jnp.einsum("eb,de->bd", d_pq, qkv_own[n, 0], preferred_element_type=F32)
        g_rel = g_rel + jnp.einsum("eb,de->bd", d_pk, qkv_own[n, 1], preferred_element_type=F32)
        g_rel = own_blocks(g_rel, 1, core) + wires.core_swap(own_blocks(g_rel, 1, 1 - core).astype(BF)).astype(F32)
        d_cols = own_blocks(d_branch_full, 1, core)
        g_out_own = jnp.einsum("ld,le->de", o_own, d_cols, preferred_element_type=F32)
        g_out_other = jnp.einsum("ld,le->de", o_other, d_cols, preferred_element_type=F32)
        two = wires.cols // 2
        g_out = wires.in_order(
            g_out_own.reshape(two, 1, block, half), g_out_other.reshape(two, 1, block, half), 1
        ).reshape(model, half)
        def cut(array):
            lead = array.shape[:-2]
            count = array.shape[-2] // chunks
            array = array.astype(BF).reshape(lead + (chunks, count, two, block))
            nl = len(lead)
            array = jnp.moveaxis(array, (nl, nl + 2), (0, 1))
            return array.reshape(chunks, two, -1, block)

        packed = jnp.concatenate([cut(g_qkv), cut(g_out), cut(g_rel)], axis=2)
        packed = lax.psum_scatter(
            packed, "col", scatter_dimension=1, tiled=False,
            axis_index_groups=[[k, k + 2] for k in range(2)],
        )
        packed = lax.psum_scatter(packed, ("seq", "rows"), scatter_dimension=0, tiled=False).astype(F32)
        c1 = model // chunks
        q_part, o_part, r_part = packed[: 3 * c1], packed[3 * c1 : 4 * c1], packed[4 * c1 :]
        ffn = jnp.stack([grad_in, grad_down]).astype(BF)
        ffn = lax.psum_scatter(ffn, ("seq", "rows"), scatter_dimension=1, tiled=True).astype(F32)
        norms = jnp.stack([d_gain_one, d_bias_one, d_gain_two, d_bias_two])
        grads[n] = (q_part.reshape(3, c1, block), o_part, r_part, ffn[0], ffn[1], norms)
    d_input = wires.turn(d_stream)
    stacked = [jnp.stack([grads[n][k] for n in range(layers)]) for k in range(6)]
    norms = lax.psum(stacked[5], ("seq", "rows", "col"))
    norms = lax.dynamic_slice_in_dim(norms, wires.col, 1, 1)
    width = model // chunks
    norms = lax.dynamic_slice_in_dim(norms, (wires.seq * wires.rows + wires.row) * width, width, 2)
    return (output[None], d_input[None], stacked[0], stacked[1], stacked[2], stacked[3], stacked[4], norms)


def solution(mesh):
    placed = (
        P(("rows", "col"), "seq", None),
        P(("rows", "col"), None),
        P(),
        P(),
        P(),
        P(None, None, "col"),
        P(None, None, "col"),
        P(),
        P(("rows", "col"), "seq", None),
    )
    return jax.shard_map(
        per_device,
        mesh=mesh,
        in_specs=placed,
        out_specs=(
            P(("rows", "col"), "seq", None),
            P(("rows", "col"), "seq", None),
            P(None, None, ("seq", "rows"), "col"),
            P(None, ("seq", "rows"), "col"),
            P(None, ("seq", "rows"), "col"),
            P(None, ("seq", "rows"), "col"),
            P(None, ("seq", "rows"), "col"),
            P(None, "col", ("seq", "rows")),
        ),
        check_vma=False,
    )
```

```python
import functools

import jax
import jax.numpy as jnp
import numpy as np
from jax import lax
from jax.experimental import pallas as pl
from jax.experimental.pallas import tpu as pltpu
from jax.sharding import PartitionSpec as P

HEAD_DIM = 64
SPAN = 256
MAX_REL = 512
WIDE = 640
HALF = 320
EPSILON = 1e-07
SCALE = (3.0 * HEAD_DIM) ** (-0.5)
LOG2E = 1.4426950408889634
BF = jnp.bfloat16
F32 = jnp.float32
NT = (((1,), (1,)), ((), ()))
NN = (((1,), (0,)), ((), ()))
TN = (((0,), (0,)), ((), ()))
VMEM_LIMIT = 56 << 20


def dot(a, b, dims=NN):
    return lax.dot_general(a, b, dims, preferred_element_type=F32)


def bucket_table():
    relative = HALF - np.arange(WIDE)
    middle = SPAN // 2
    absolute = np.where((relative < middle) & (relative > -middle), middle - 1, np.abs(relative))
    log_position = np.ceil(np.log(absolute / middle) / np.log((MAX_REL - 1) / middle) * (middle - 1)) + middle
    bucket = np.where(absolute <= middle, relative, log_position * np.sign(relative))
    bucket = np.clip(bucket + SPAN, 0, 2 * SPAN - 1).astype(np.int32)
    return (bucket[:, None] == np.arange(2 * SPAN)[None, :]).astype(np.float32)


def assemble(target, own, other, core, count):
    target[pl.ds(pl.multiple_of(core * count, count), count), :] = own[...]
    target[pl.ds(pl.multiple_of((1 - core) * count, count), count), :] = other[...]


def half_of(head):
    lane = lax.broadcasted_iota(jnp.int32, (1, 128), 1)
    return (lane < HEAD_DIM) if head == 0 else (lane >= HEAD_DIM)


def doc_number(position, meta_ref):
    total = jnp.zeros(position.shape, jnp.int32)
    for k in range(3):
        total = total + (position >= meta_ref[k]).astype(jnp.int32)
    return total


def skew(values, base):
    return pltpu.roll(values, base % WIDE, 1, stride=1, stride_axis=0)


def attention_kernel(meta_ref, own_ref, other_ref, w_ref, pe_ref, rev_ref, o_ref, sv_ref, p_ref, x_ref, bt_ref, sb_ref, *, length, blk):
    core = meta_ref[3]

    @pl.when(pl.program_id(0) == 0)
    def _():
        assemble(x_ref, own_ref, other_ref, core, length // 2)

    qkv = dot(x_ref[...], w_ref[0]).astype(BF)
    sv_ref[0, :, :128] = qkv[:, :128]
    sb_ref[...] = qkv
    sv_ref[0, :, 128:] = dot(rev_ref[...], qkv[:, 128:]).astype(BF)
    zero = jnp.zeros((), BF)
    ids_j = doc_number(lax.broadcasted_iota(jnp.int32, (1, length), 1), meta_ref)
    for h in range(2):
        own = half_of(h)
        for b in range(length // blk):
            sl = slice(b * blk, (b + 1) * blk)
            kb = jnp.where(own, sb_ref[sl, 128:256], zero)
            t2 = skew(dot(kb, pe_ref[0, 0], NT), b * blk + HALF)
            bt_ref[:, sl] = t2[:, :length].T
        for b in range(length // blk):
            sl = slice(b * blk, (b + 1) * blk)
            qb = jnp.where(own, sb_ref[sl, :128], zero)
            t1 = skew(dot(qb, pe_ref[0, 1], NT), b * blk + HALF)
            s = dot(qb, sb_ref[:, 128:256], NT) + t1[:, :length] + bt_ref[sl, :]
            ids_i = doc_number(lax.broadcasted_iota(jnp.int32, (blk, 1), 0) + b * blk, meta_ref)
            s = jnp.where(ids_i == ids_j, s, -1e30)
            e = jnp.exp2((s - jnp.max(s, axis=1, keepdims=True)) * (SCALE * LOG2E))
            p = (e * (1.0 / jnp.sum(e, axis=1, keepdims=True))).astype(BF)
            o = dot(p, sb_ref[:, 256:]).astype(BF)
            if h == 0:
                o_ref[sl, :] = o
            else:
                o_ref[sl, :] = jnp.where(own, o, o_ref[sl, :])
            p_ref[h, sl, :] = dot(p, rev_ref[...]).astype(BF)


def attention(meta, own, other, w, pe, rev):
    count, model = own.shape
    length = 2 * count
    pairs = w.shape[0]
    whole = lambda *shape: pl.BlockSpec(shape, lambda g, m: (0,) * len(shape))
    return pl.pallas_call(
        functools.partial(attention_kernel, length=length, blk=128),
        out_shape=(
            jax.ShapeDtypeStruct((length, pairs * 128), BF),
            jax.ShapeDtypeStruct((pairs, length, 384), BF),
            jax.ShapeDtypeStruct((2 * pairs, length, length), BF),
        ),
        grid_spec=pltpu.PrefetchScalarGridSpec(
            num_scalar_prefetch=1,
            grid=(pairs,),
            in_specs=[
                whole(count, model),
                whole(count, model),
                pl.BlockSpec((1, model, 384), lambda g, m: (g, 0, 0)),
                pl.BlockSpec((1, 2, WIDE, 128), lambda g, m: (g, 0, 0, 0)),
                whole(length, length),
            ],
            out_specs=(
                pl.BlockSpec((length, 128), lambda g, m: (0, g)),
                pl.BlockSpec((1, length, 384), lambda g, m: (g, 0, 0)),
                pl.BlockSpec((2, length, length), lambda g, m: (g, 0, 0)),
            ),
            scratch_shapes=[
                pltpu.VMEM((length, model), BF),
                pltpu.VMEM((length, length), F32),
                pltpu.VMEM((length, 384), BF),
            ],
        ),
        compiler_params=pltpu.CompilerParams(vmem_limit_bytes=VMEM_LIMIT),
        name="attention",
    )(meta, own, other, w, pe, rev)


def attention_grad_kernel(
    meta_ref, own_ref, other_ref, wo_ref, sv_ref, p_ref, pe_ref, rev_ref, w_ref,
    dqkv_ref, dpe_ref, mine_ref, theirs_ref, drb_ref, dt_ref, u_ref, acc_ref, dx_ref, *, length, blk,
):
    g = pl.program_id(0)
    core = meta_ref[3]
    count = length // 2

    @pl.when(g == 0)
    def _():
        assemble(drb_ref, own_ref, other_ref, core, count)

    zero = jnp.zeros((), BF)
    pad = jnp.zeros((blk, WIDE - length), F32)
    d_o = dot(drb_ref[...], wo_ref[...], NT).astype(BF)
    q = sv_ref[0, :, :128]
    q_t, kr_t = q.T, sv_ref[0, :, 128:256].T
    for h in range(2):
        own = half_of(h)
        hs = slice(HEAD_DIM * h, HEAD_DIM * (h + 1))
        krh = jnp.where(own, sv_ref[0, :, 128:256], zero)
        pkh = jnp.where(own, pe_ref[0, 1], zero)
        d_oh = jnp.where(own, d_o, zero)
        for b in range(length // blk):
            sl = slice(b * blk, (b + 1) * blk)
            da = dot(d_oh[sl], sv_ref[0, :, 256:], NT)
            p = p_ref[h, sl, :].astype(F32)
            ds = (p * (da - jnp.sum(p * da, axis=1, keepdims=True))).astype(BF)
            wide = ds.astype(F32)
            dt_ref[:, sl] = wide.T
            u = skew(jnp.concatenate([wide, pad], axis=1), b * blk + WIDE - 192).astype(BF)
            u_ref[sl, :] = u
            r = dot(ds, krh) + dot(u, pkh)
            acc_ref[sl, :128] = r if h == 0 else acc_ref[sl, :128] + r
        dpe_ref[0, 1, hs, :] = (dot(q_t[hs], u_ref[...]) * SCALE).astype(BF)
        r = dot(p_ref[h], d_oh, TN)
        acc_ref[:, 256:] = r if h == 0 else acc_ref[:, 256:] + r
        qh = jnp.where(own, q, zero)
        pqh = jnp.where(own, pe_ref[0, 0], zero)
        for b in range(length // blk):
            sl = slice(b * blk, (b + 1) * blk)
            z = dt_ref[sl, :]
            u = skew(jnp.concatenate([z, pad], axis=1), b * blk + WIDE - 191).astype(BF)
            u_ref[sl, :] = u
            r = dot(z.astype(BF), qh) + dot(u, pqh)
            acc_ref[sl, 128:256] = r if h == 0 else acc_ref[sl, 128:256] + r
        dpe_ref[0, 0, hs, :] = (dot(kr_t[hs], u_ref[...]) * SCALE).astype(BF)
    dq = (acc_ref[:, :128] * SCALE).astype(BF)
    dk = (acc_ref[:, 128:256] * SCALE).astype(BF)
    dv = acc_ref[:, 256:].astype(BF)
    dkv = dot(rev_ref[...], jnp.concatenate([dk, dv], axis=1)).astype(BF)
    dqkv = jnp.concatenate([dq, dkv], axis=1)
    dqkv_ref[0] = dqkv
    part = dot(dqkv, w_ref[0], NT)

    @pl.when(g == 0)
    def _():
        dx_ref[...] = part

    @pl.when(g > 0)
    def _():
        dx_ref[...] = dx_ref[...] + part

    @pl.when(g == pl.num_programs(0) - 1)
    def _():
        mine_ref[...] = dx_ref[pl.ds(pl.multiple_of(core * count, count), count), :]
        theirs_ref[...] = dx_ref[pl.ds(pl.multiple_of((1 - core) * count, count), count), :].astype(BF)


def attention_grad(meta, own, other, wo, saved, probs, pe, rev, w):
    count, model = own.shape
    length = 2 * count
    pairs = w.shape[0]
    whole = lambda *shape: pl.BlockSpec(shape, lambda g, m: (0,) * len(shape))
    return pl.pallas_call(
        functools.partial(attention_grad_kernel, length=length, blk=128),
        out_shape=(
            jax.ShapeDtypeStruct((pairs, length, 384), BF),
            jax.ShapeDtypeStruct((pairs, 2, 128, WIDE), BF),
            jax.ShapeDtypeStruct((count, model), F32),
            jax.ShapeDtypeStruct((count, model), BF),
        ),
        grid_spec=pltpu.PrefetchScalarGridSpec(
            num_scalar_prefetch=1,
            grid=(pairs,),
            in_specs=[
                whole(count, model),
                whole(count, model),
                pl.BlockSpec((128, model), lambda g, m: (g, 0)),
                pl.BlockSpec((1, length, 384), lambda g, m: (g, 0, 0)),
                pl.BlockSpec((2, length, length), lambda g, m: (g, 0, 0)),
                pl.BlockSpec((1, 2, WIDE, 128), lambda g, m: (g, 0, 0, 0)),
                whole(length, length),
                pl.BlockSpec((1, model, 384), lambda g, m: (g, 0, 0)),
            ],
            out_specs=(
                pl.BlockSpec((1, length, 384), lambda g, m: (g, 0, 0)),
                pl.BlockSpec((1, 2, 128, WIDE), lambda g, m: (g, 0, 0, 0)),
                whole(count, model),
                whole(count, model),
            ),
            scratch_shapes=[
                pltpu.VMEM((length, model), BF),
                pltpu.VMEM((length, length), F32),
                pltpu.VMEM((length, WIDE), BF),
                pltpu.VMEM((length, 384), F32),
                pltpu.VMEM((length, model), F32),
            ],
        ),
        compiler_params=pltpu.CompilerParams(vmem_limit_bytes=VMEM_LIMIT),
        name="attention_grad",
    )(meta, own, other, wo, saved, probs, pe, rev, w)


def weight_copies(layer, refs, scratch, sems, meta_ref):
    shards = []
    for s in range(4):
        group = []
        for m in range(2):
            own, core_own, near, far, core_near, core_far = refs[m]
            place = scratch.at[m, s]
            if s < 2:
                group.append(((own if s == 0 else core_own).at[layer], place))
            else:
                first, second = (near, far) if s == 2 else (core_near, core_far)
                rows = first.shape[0]
                one = pl.multiple_of(meta_ref[4] * rows, rows)
                two = pl.multiple_of((1 - meta_ref[4]) * rows, rows)
                group.append((first, place.at[pl.ds(one, rows)]))
                group.append((second, place.at[pl.ds(two, rows)]))
        shards.append(group)
    copies, k = [], 0
    for group in shards:
        made = []
        for source, target in group:
            made.append(pltpu.make_async_copy(source, target, sems.at[k]))
            k += 1
        copies.append(made)
    return copies


COPIES = 12


def row_norm(state, gain, bias):
    centered = state - jnp.mean(state, axis=1, keepdims=True)
    inverse = lax.rsqrt(jnp.mean(centered * centered, axis=1, keepdims=True) + EPSILON)
    return centered * inverse * gain + bias


def row_norm_grad(state, gain, d_result):
    centered = state - jnp.mean(state, axis=1, keepdims=True)
    inverse = lax.rsqrt(jnp.mean(centered * centered, axis=1, keepdims=True) + EPSILON)
    unit = centered * inverse
    d_unit = d_result * gain
    d_state = inverse * (
        d_unit
        - jnp.mean(d_unit, axis=1, keepdims=True)
        - unit * jnp.mean(d_unit * unit, axis=1, keepdims=True)
    )
    return d_state, jnp.sum(d_result * unit, axis=0, keepdims=True), jnp.sum(d_result, axis=0, keepdims=True)


def tokens_kernel(meta_ref, own_ref, other_ref, x_ref, wo_own_ref, wo_other_ref, norm_ref, *rest, layer, chunk):
    wires, rest = rest[:12], rest[12:]
    y_ref, yb_ref, mb_ref, resid_ref, pre_ref, slope_ref, scratch, sems = rest
    copies = weight_copies(layer, (wires[:6], wires[6:]), scratch, sems, meta_ref)
    for group in copies:
        for item in group:
            item.start()
    resid = x_ref[...].astype(F32) + dot(own_ref[...], wo_own_ref[...]) + dot(other_ref[...], wo_other_ref[...])
    resid_ref[...] = resid
    middle = row_norm(resid, norm_ref[0:1, :], norm_ref[1:2, :])
    mb = middle.astype(BF)
    mb_ref[...] = mb
    pre_ref[...] = middle
    hidden = scratch.shape[3]
    for s in range(4):
        for item in copies[s]:
            item.wait()
        for c in range(hidden // chunk):
            cols = slice(c * chunk, (c + 1) * chunk)
            h = dot(mb, scratch[0, s, :, cols])
            cumulative = 0.5 * (1.0 + lax.erf(h * 0.7071067811865476))
            density = jnp.exp(-0.5 * h * h) * 0.3989422804014327
            slope_ref[:, s * hidden + c * chunk : s * hidden + (c + 1) * chunk] = (cumulative + h * density).astype(BF)
            act = (h * cumulative).astype(BF)
            pre_ref[...] = pre_ref[...] + dot(act, scratch[1, s, :, cols], NT)
    y = row_norm(pre_ref[...], norm_ref[2:3, :], norm_ref[3:4, :])
    y_ref[...] = y
    yb_ref[...] = y.astype(BF)


def token_step(meta, layer, o_own, o_other, x, wo_own, wo_other, norms, wires):
    count, model = x.shape
    half = o_own.shape[1]
    hidden = wires[0].shape[2]
    whole = lambda *shape: pl.BlockSpec(shape, lambda g, m: (0,) * len(shape))
    mine = pl.BlockSpec((count, half), lambda g, m: (m[3], 0))
    hbm = pl.BlockSpec(memory_space=pl.ANY)
    return pl.pallas_call(
        functools.partial(tokens_kernel, layer=layer, chunk=384),
        out_shape=(
            jax.ShapeDtypeStruct((count, model), F32),
            jax.ShapeDtypeStruct((count, model), BF),
            jax.ShapeDtypeStruct((count, model), BF),
            jax.ShapeDtypeStruct((count, model), F32),
            jax.ShapeDtypeStruct((count, model), F32),
            jax.ShapeDtypeStruct((count, 4 * hidden), BF),
        ),
        grid_spec=pltpu.PrefetchScalarGridSpec(
            num_scalar_prefetch=1,
            grid=(1,),
            in_specs=[mine, mine, whole(count, model), whole(half, model), whole(half, model), whole(4, model)] + [hbm] * 12,
            out_specs=(
                whole(count, model), whole(count, model), whole(count, model), whole(count, model), whole(count, model),
                whole(count, 4 * hidden),
            ),
            scratch_shapes=[pltpu.VMEM((2, 4, model, hidden), BF), pltpu.SemaphoreType.DMA((COPIES,))],
        ),
        compiler_params=pltpu.CompilerParams(vmem_limit_bytes=VMEM_LIMIT),
        name="token_step",
    )(meta, o_own, o_other, x, wo_own, wo_other, norms, *wires)


def tokens_grad_kernel(meta_ref, *rest, layer, chunk, parts):
    ups, rest = rest[:parts], rest[parts:]
    pre_ref, resid_ref, slope_ref, norm_ref, *rest = rest
    wires, rest = rest[:12], rest[12:]
    df_ref, dr_ref, drb_ref, dn_ref, scratch, sems, dm_ref = rest
    copies = weight_copies(layer, (wires[:6], wires[6:]), scratch, sems, meta_ref)
    for group in copies:
        for item in group:
            item.start()
    dy = ups[0][...].astype(F32)
    for item in ups[1:]:
        dy = dy + item[...].astype(F32)
    dz, dg2, db2 = row_norm_grad(pre_ref[...], norm_ref[2:3, :], dy)
    df = dz.astype(BF)
    df_ref[...] = df
    dm_ref[...] = dz
    hidden = scratch.shape[3]
    for s in range(4):
        for item in copies[s]:
            item.wait()
        for c in range(hidden // chunk):
            cols = slice(c * chunk, (c + 1) * chunk)
            slope = slope_ref[:, s * hidden + c * chunk : s * hidden + (c + 1) * chunk].astype(F32)
            dh = (dot(df, scratch[1, s, :, cols]) * slope).astype(BF)
            dm_ref[...] = dm_ref[...] + dot(dh, scratch[0, s, :, cols], NT)
    dr, dg1, db1 = row_norm_grad(resid_ref[...], norm_ref[0:1, :], dm_ref[...])
    dr_ref[...] = dr
    drb_ref[...] = dr.astype(BF)
    dn_ref[0:1, :] = dg1
    dn_ref[1:2, :] = db1
    dn_ref[2:3, :] = dg2
    dn_ref[3:4, :] = db2


def token_grad(meta, layer, ups, pre, resid, slope, norms, wires):
    count, model = pre.shape
    hidden = wires[0].shape[2]
    whole = lambda *shape: pl.BlockSpec(shape, lambda g, m: (0,) * len(shape))
    hbm = pl.BlockSpec(memory_space=pl.ANY)
    return pl.pallas_call(
        functools.partial(tokens_grad_kernel, layer=layer, chunk=384, parts=len(ups)),
        out_shape=(
            jax.ShapeDtypeStruct((count, model), BF),
            jax.ShapeDtypeStruct((count, model), F32),
            jax.ShapeDtypeStruct((count, model), BF),
            jax.ShapeDtypeStruct((4, model), F32),
        ),
        grid_spec=pltpu.PrefetchScalarGridSpec(
            num_scalar_prefetch=1,
            grid=(1,),
            in_specs=[whole(count, model)] * len(ups)
            + [whole(count, model), whole(count, model), whole(count, 4 * hidden), whole(4, model)]
            + [hbm] * 12,
            out_specs=(whole(count, model), whole(count, model), whole(count, model), whole(4, model)),
            scratch_shapes=[
                pltpu.VMEM((2, 4, model, hidden), BF),
                pltpu.SemaphoreType.DMA((COPIES,)),
                pltpu.VMEM((count, model), F32),
            ],
        ),
        compiler_params=pltpu.CompilerParams(vmem_limit_bytes=VMEM_LIMIT),
        name="token_grad",
    )(meta, *ups, pre, resid, slope, norms, *wires)


def hidden_grad_kernel(m_ref, d_ref, wi_ref, wd_ref, g_ref, mt_ref, dt_ref):
    @pl.when(pl.program_id(0) == 0)
    def _():
        mt_ref[...] = m_ref[...].T
        dt_ref[...] = d_ref[...].T

    h = dot(m_ref[...], wi_ref[0])
    cumulative = 0.5 * (1.0 + lax.erf(h * 0.7071067811865476))
    density = jnp.exp(-0.5 * h * h) * 0.3989422804014327
    act = (h * cumulative).astype(BF)
    dh = (dot(d_ref[...], wd_ref[0]) * (cumulative + h * density)).astype(BF)
    g_ref[0] = dot(mt_ref[...], dh).astype(BF)
    g_ref[1] = dot(dt_ref[...], act).astype(BF)


def hidden_grad(layer, rows, d_rows, w_in, w_down):
    count, model = rows.shape
    hidden = w_in.shape[2]
    chunk = 256
    whole = lambda *shape: pl.BlockSpec(shape, lambda g: (0,) * len(shape))
    return pl.pallas_call(
        hidden_grad_kernel,
        out_shape=jax.ShapeDtypeStruct((2, model, hidden), BF),
        grid=(hidden // chunk,),
        in_specs=[
            whole(count, model),
            whole(count, model),
            pl.BlockSpec((1, model, chunk), lambda g: (layer, 0, g)),
            pl.BlockSpec((1, model, chunk), lambda g: (layer, 0, g)),
        ],
        out_specs=pl.BlockSpec((2, model, chunk), lambda g: (0, 0, g)),
        scratch_shapes=[pltpu.VMEM((model, count), BF), pltpu.VMEM((model, count), BF)],
        compiler_params=pltpu.CompilerParams(vmem_limit_bytes=VMEM_LIMIT),
        name="hidden_grad",
    )(rows, d_rows, w_in, w_down)


def turned(values):
    return pltpu.roll(values.astype(F32), HEAD_DIM, 1).astype(values.dtype)


def split_heads(tiles, y):
    return (tiles[0], tiles[1]) if y == 0 else (tiles[2], tiles[1])


def projection_grad_kernel(
    meta_ref, x_own_ref, x_other_ref, dqkv_ref, o_own_ref, o_other_ref, d_own_ref, d_other_ref, dpe_ref, table_ref, rel_ref,
    w_ref, dn_ref, g_ref, send_ref, x_ref, d_ref, left_ref, out_ref, right_ref, *, length, chunks, pairs,
):
    core = meta_ref[3]
    count = length // 2
    model = x_ref.shape[1]
    buckets = rel_ref.shape[0]
    low = half_of(0)
    zero = jnp.zeros((), BF)
    assemble(x_ref, x_own_ref, x_other_ref, core, count)
    assemble(d_ref, d_own_ref, d_other_ref, core, count)
    left_ref[:, :length] = x_ref[...].T
    left_ref[:, length:] = rel_ref[...].T
    block = model // 4
    at_core = lambda y, k: 2 * block * y + block * k
    for y in range(2):
        for k in range(2):
            rows = slice(at_core(y, k), at_core(y, k) + block)
            here = slice(block * y, block * (y + 1))
            own, other = o_own_ref[:, here].T, o_other_ref[:, here].T
            out_ref[rows, :] = jnp.where(core == k, own, other)
    d_pos = []
    for c in range(2):
        tiles = []
        for p in range(pairs):
            folded = dot(dpe_ref[p, c], table_ref[c])
            tiles.append(folded.T.astype(BF))
        d_pos.append(tiles)
    per = model // chunks
    first_core = core == 0
    for y in range(2):
        cut = lambda c, tiles=None: split_heads([dqkv_ref[p, :, 128 * c : 128 * (c + 1)] for p in range(pairs)], y)
        (qf, qr), (kf, kr), (vf, vr) = cut(0), cut(1), cut(2)
        (pqf, pqr), (pkf, pkr) = split_heads(d_pos[0], y), split_heads(d_pos[1], y)
        if y == 0:
            mix = jnp.where(low, qr, turned(kr))
            pmix = jnp.where(low, pqr, turned(pkr))
            vmix = jnp.where(low, vr, zero)
        else:
            mix = jnp.where(low, turned(qr), kr)
            pmix = jnp.where(low, turned(pqr), pkr)
            vmix = jnp.where(low, turned(vr), zero)
        base = 2 * block * y
        t0, t1, t2 = (d_ref[:, base + 128 * k : base + 128 * (k + 1)] for k in range(3))
        of = jnp.where(first_core, t0, t2)
        om = jnp.where(low, zero, jnp.where(first_core, turned(t1), t1))
        right_ref[:length, 0:128] = qf
        right_ref[:length, 128:256] = kf
        right_ref[:length, 256:384] = mix
        right_ref[length:, 0:128] = pqf
        right_ref[length:, 128:256] = pkf
        right_ref[length:, 256:384] = pmix
        one = dot(left_ref[...], right_ref[...])
        two = dot(left_ref[:, :length], jnp.concatenate([vf, vmix], axis=1))
        three = dot(out_ref[...], jnp.concatenate([om, of], axis=1))
        for n in range(chunks):
            rows = slice(n * per, (n + 1) * per)
            g_ref[y, n, :per, 0:384] = one[rows].astype(BF)
            g_ref[y, n, :per, 384:512] = two[rows, :128].astype(BF)
            g_ref[y, n, :per, 512:640] = (two[rows, 128:] + three[rows, :128]).astype(BF)
            g_ref[y, n, :per, 640:768] = three[rows, 128:].astype(BF)
    back = jnp.zeros((buckets, model), F32)
    for p in range(pairs):
        for c in range(2):
            back = back + dot(d_pos[c][p], w_ref[p, :, 128 * c : 128 * (c + 1)], NT)
    share = buckets // chunks
    tall = share // 2
    kinds = dn_ref[...]
    for y in range(2):
        base = 2 * block * y
        t0, t1, t2 = (back[:, base + 128 * k : base + 128 * (k + 1)] for k in range(3))
        t1t = pltpu.roll(t1, HEAD_DIM, 1)
        for target, flag in ((0, first_core), (1, jnp.logical_not(first_core))):
            full = jnp.where(flag, t0, t2).astype(BF)
            rest = jnp.where(low, jnp.where(flag, t1, t1t), 0.0).astype(BF)
            norm = jnp.where(flag, kinds[2 * y : 2 * y + 1, :], kinds[2 * y + 1 : 2 * y + 2, :])
            for n in range(chunks):
                place = g_ref.at[y, n, pl.ds(per, tall)] if target == 0 else send_ref.at[y, n]
                for k in range(2):
                    rows = slice(n * share + k * tall, n * share + (k + 1) * tall)
                    place[:, 256 * k : 256 * k + 128] = full[rows]
                    place[:, 256 * k + 128 : 256 * k + 256] = rest[rows]
                place[:, 512:768] = jnp.zeros((tall, 256), BF)
        for target, flag in ((0, first_core), (1, jnp.logical_not(first_core))):
            norm = jnp.where(flag, kinds[2 * y : 2 * y + 1, :], kinds[2 * y + 1 : 2 * y + 2, :])
            norm = jnp.broadcast_to(norm, (16, model)).astype(BF)
            for n in range(chunks):
                piece = norm[:, n * per : (n + 1) * per]
                if target == 0:
                    g_ref[y, n, per : per + 16, 512 : 512 + per] = piece
                else:
                    send_ref[y, n, 0:16, 512 : 512 + per] = piece


def projection_grad(meta, x_own, x_other, dqkv, o_own, o_other, d_own, d_other, dpe, tables, rel, w, dn, chunks):
    count, model = x_own.shape
    length = 2 * count
    pairs = w.shape[0]
    buckets = rel.shape[0]
    per, tall = model // chunks, buckets // chunks // 2
    args = (x_own, x_other, dqkv, o_own, o_other, d_own, d_other, dpe, tables, rel, w, dn)
    whole = lambda shape: pl.BlockSpec(shape, lambda g, m: (0,) * len(shape))
    return pl.pallas_call(
        functools.partial(projection_grad_kernel, length=length, chunks=chunks, pairs=pairs),
        out_shape=(
            jax.ShapeDtypeStruct((2, chunks, per + tall, model), BF),
            jax.ShapeDtypeStruct((2, chunks, tall, model), BF),
        ),
        grid_spec=pltpu.PrefetchScalarGridSpec(
            num_scalar_prefetch=1,
            grid=(1,),
            in_specs=[whole(a.shape) for a in args],
            out_specs=(whole((2, chunks, per + tall, model)), whole((2, chunks, tall, model))),
            scratch_shapes=[
                pltpu.VMEM((length, model), BF),
                pltpu.VMEM((length, model), BF),
                pltpu.VMEM((model, length + buckets), BF),
                pltpu.VMEM((model, length), BF),
                pltpu.VMEM((length + buckets, 384), BF),
            ],
        ),
        compiler_params=pltpu.CompilerParams(vmem_limit_bytes=VMEM_LIMIT),
        name="projection_grad",
    )(meta, *args)


class Wires:
    def __init__(self):
        self.seqs, self.rows, self.cols = (lax.axis_size(name) for name in ("seq", "rows", "col"))
        self.seq, self.row, self.col = (lax.axis_index(name) for name in ("seq", "rows", "col"))
        self.core, self.y = self.col % 2, self.col // 2

    def send(self, array, target):
        pairs = []
        for s in range(self.seqs):
            for r in range(self.rows):
                for c in range(self.cols):
                    t = target(s, r, c)
                    pairs.append(((s * self.rows + r) * self.cols + c, (t[0] * self.rows + t[1]) * self.cols + t[2]))
        return lax.ppermute(array, ("seq", "rows", "col"), pairs)

    def turn(self, array):
        return self.send(array, lambda s, r, c: (c % 2, r, c - c % 2 + s))

    def to_core(self, array):
        return self.send(array, lambda s, r, c: (s, r, c ^ 1))

    def to_y(self, array):
        return self.send(array, lambda s, r, c: (s, r, c ^ 2))

    def to_seq(self, array):
        return self.send(array, lambda s, r, c: (1 - s, r, c))

    def to_row(self, array, bit):
        return self.send(array, lambda s, r, c: (s, r ^ (1 << bit), c))


def halve(array, axis, count, bit, mine, send):
    shape = array.shape
    low = 1 << bit
    cut = array.reshape(shape[:axis] + (count // (2 * low), 2, low) + shape[axis + 1 :])
    keep = lax.dynamic_index_in_dim(cut, mine, axis + 1, keepdims=False)
    give = lax.dynamic_index_in_dim(cut, 1 - mine, axis + 1, keepdims=False)
    got = send(give)
    total = (keep.astype(F32) + got.astype(F32)).astype(array.dtype)
    return total.reshape(shape[:axis] + (count // 2,) + shape[axis + 1 :])


def bits_of(count):
    return count.bit_length() - 1


def reduce_rows(array, axis, wires):
    count = array.shape[axis]
    array = halve(array, axis, count, bits_of(count) - 1, wires.seq, wires.to_seq)
    bit = 0
    while array.shape[axis] > 1:
        array = halve(array, axis, array.shape[axis], 0, (wires.row >> bit) & 1, functools.partial(wires.to_row, bit=bit))
        bit += 1
    return lax.squeeze(array, (axis,))


def reduce_projection(packed, extra, wires, parts):
    tall = extra.shape[2]
    packed = packed + jnp.pad(extra, ((0, 0), (0, 0), (packed.shape[2] - tall, 0), (0, 0)))
    width = packed.shape[3] // parts
    done = []
    for k in range(parts):
        piece = lax.slice_in_dim(packed, k * width, (k + 1) * width, axis=3)
        steps = ["y", "seq"] if k % 2 == 0 else ["seq", "y"]
        for step in steps:
            if step == "y":
                piece = halve(piece, 0, 2, 0, wires.y, wires.to_y)
            else:
                piece = halve(piece, 1, 8, 2, wires.seq, wires.to_seq)
        done.append(piece)
    whole = jnp.concatenate(done, axis=3)[0]
    low = bits_of(wires.rows) - 2
    for k in range(2):
        bit = low + k
        whole = halve(whole, 0, whole.shape[0], 0, (wires.row >> bit) & 1, functools.partial(wires.to_row, bit=bit))
    whole = whole[0]
    main, tail = whole[:-tall], whole[-tall:]
    rel = jnp.concatenate([tail[:, :256], tail[:, 256:512]], axis=0)
    norm = tail[0, 512 : 512 + main.shape[0]]
    if low > 0:
        for bit in reversed(range(low)):
            mine, send = (wires.row >> bit) & 1, functools.partial(wires.to_row, bit=bit)
            main, rel, norm = (
                halve(a.reshape((2, a.shape[0] // 2) + a.shape[1:]), 0, 2, 0, mine, send)[0] for a in (main, rel, norm)
            )
    return main, rel, norm


def unpack(main, rel, wires):
    t = [main[:, 128 * k : 128 * (k + 1)] for k in range(6)]
    full = [t[0], t[1], t[3], t[5]]
    rest = [t[2][:, :64], t[2][:, 64:], t[4][:, :64], t[4][:, 64:]]
    out = []
    for k in range(4):
        head = wires.y == 0 if k < 3 else wires.core == 0
        out.append(jnp.where(head, jnp.concatenate([full[k], rest[k]], 1), jnp.concatenate([rest[k], full[k]], 1)))
    rel = jnp.where(
        wires.core == 0,
        jnp.concatenate([rel[:, :128], rel[:, 128:192]], 1),
        jnp.concatenate([rel[:, 128:192], rel[:, :128]], 1),
    )
    return [item.astype(F32) for item in out], rel.astype(F32)


def after(array, earlier):
    return lax.optimization_barrier((array, earlier))[0]


def per_device(tokens, lengths, qkv_weight, out_weight, rel_table, ffn_in, ffn_out, norm_params, cotangent):
    wires = Wires()
    core = wires.core
    count, model = tokens.shape[1:]
    length = 2 * count
    layers = qkv_weight.shape[0]
    half, block = model // 2, model // wires.cols
    pairs = half // 128
    table_np = bucket_table()
    table = jnp.asarray(table_np, BF)
    tables = jnp.asarray(np.stack([table_np, table_np[::-1]]), BF)
    rev = jnp.asarray(np.eye(length)[::-1], BF)
    start = wires.turn(tokens[0])
    ends = jnp.cumsum(wires.turn(lengths)[0]).astype(jnp.int32)
    meta = jnp.concatenate([ends[:3], core[None], wires.seq[None]]).astype(jnp.int32)

    weights = (ffn_in, ffn_out)
    core_own = [wires.to_core(w) for w in weights]
    rows = model // 2
    last = start
    wire_args = []
    for n in range(layers):
        args = []
        for m in range(2):
            piece = lax.dynamic_slice_in_dim(weights[m][n], wires.seq * rows, rows, 0)
            near = wires.to_y(after(piece, last) if n + m else piece)
            far = wires.to_seq(near)
            last = near
            args += [weights[m], core_own[m], near, far, wires.to_core(near), wires.to_core(far)]
        wire_args.append(args)
    d_final = wires.turn(after(cotangent[0], last))

    def own_blocks(array, axis, which):
        shape = array.shape
        cut = array.reshape(shape[:axis] + (wires.cols // 2, 2, block) + shape[axis + 1 :])
        cut = lax.dynamic_index_in_dim(cut, which, axis + 1, keepdims=False)
        return cut.reshape(shape[:axis] + (half,) + shape[axis + 1 :])

    qkv_own = own_blocks(qkv_weight, 3, core)
    out_own = own_blocks(out_weight, 1, core)
    out_other = own_blocks(out_weight, 1, 1 - core)
    w_pairs = qkv_own.reshape(layers, 3, model, pairs, 128).transpose(0, 3, 2, 1, 4).reshape(layers, pairs, model, 384)
    pos = jnp.einsum("nbd,ncde->ncbe", rel_table, qkv_own[:, :2], preferred_element_type=F32).astype(BF)
    ext = jnp.einsum("ub,ncbe->ncue", table, pos, preferred_element_type=F32).astype(BF)
    pe_fwd = ext.reshape(layers, 2, WIDE, pairs, 128).transpose(0, 3, 1, 2, 4)
    ext_b = jnp.einsum("ub,nbe->nue", tables[1], pos[:, 1], preferred_element_type=F32).astype(BF)
    pe_bwd = jnp.stack([ext[:, 0], ext_b], axis=1).reshape(layers, 2, WIDE, pairs, 128).transpose(0, 3, 1, 2, 4)

    x, xb = start, start
    kept = []
    for n in range(layers):
        xb_other = wires.to_core(xb)
        o_own, saved, probs = attention(meta, xb, xb_other, w_pairs[n], pe_fwd[n], rev)
        o_other = wires.to_core(o_own)
        y, yb, mb, resid, pre, slope = token_step(
            meta, n, o_own, o_other, x, out_own[n], out_other[n], norm_params[n], wire_args[n]
        )
        rows_all = lax.all_gather(mb, "col", axis=0, tiled=True)
        kept.append((xb, xb_other, o_own, o_other, saved, probs, resid, pre, slope, rows_all))
        x, xb = y, yb
    output = wires.turn(x)
    ups = [d_final]
    main, rel, norms, hidden = [None] * layers, [None] * layers, [None] * layers, [None] * layers
    chunks = wires.seqs * wires.rows
    for n in reversed(range(layers)):
        xb, xb_other, o_own, o_other, saved, probs, resid, pre, slope, rows_all = kept[n]
        df, dr, drb, dn = token_grad(meta, n, ups, pre, resid, slope, norm_params[n], wire_args[n])
        drb_other = wires.to_core(drb)
        df_all = lax.all_gather(df, "col", axis=0, tiled=True)
        dqkv, dpe, dx_mine, dx_theirs = attention_grad(
            meta, drb, drb_other, out_own[n], saved, probs, pe_bwd[n], rev, w_pairs[n]
        )
        dx_got = wires.to_core(dx_theirs)
        ups = [dr, dx_mine, dx_got]
        packed, extra = projection_grad(
            meta, xb, xb_other, dqkv, o_own, o_other, drb, drb_other, dpe, tables, rel_table[n], w_pairs[n], dn, 8
        )
        main[n], rel[n], norms[n] = reduce_projection(packed, wires.to_core(extra), wires, 2)
        grads = hidden_grad(n, rows_all, df_all, ffn_in, ffn_out)
        grads = grads.reshape(2, chunks, model // chunks, grads.shape[2])
        hidden[n] = reduce_rows(grads, 1, wires).astype(F32)
    d_input = wires.turn(sum(item.astype(F32) for item in ups))
    parts = [unpack(main[n], rel[n], wires) for n in range(layers)]
    grad_qkv = jnp.stack([jnp.stack(part[0][:3]) for part in parts])
    grad_out = jnp.stack([part[0][3] for part in parts])
    grad_rel = jnp.stack([part[1] for part in parts])
    grad_norms = jnp.stack(norms).astype(F32)[:, None]
    grad_in = jnp.stack([item[0] for item in hidden])
    grad_down = jnp.stack([item[1] for item in hidden])
    return (output[None], d_input[None], grad_qkv, grad_out, grad_rel, grad_in, grad_down, grad_norms)


def solution(mesh):
    placed = (
        P(("rows", "col"), "seq", None),
        P(("rows", "col"), None),
        P(),
        P(),
        P(),
        P(None, None, "col"),
        P(None, None, "col"),
        P(),
        P(("rows", "col"), "seq", None),
    )
    return jax.shard_map(
        per_device,
        mesh=mesh,
        in_specs=placed,
        out_specs=(
            P(("rows", "col"), "seq", None),
            P(("rows", "col"), "seq", None),
            P(None, None, ("seq", "rows"), "col"),
            P(None, ("seq", "rows"), "col"),
            P(None, ("seq", "rows"), "col"),
            P(None, ("seq", "rows"), "col"),
            P(None, ("seq", "rows"), "col"),
            P(None, "col", ("seq", "rows")),
        ),
        check_vma=False,
    )
```

```python
import functools

import jax
import jax.numpy as jnp
import numpy as np
from jax import lax
from jax.experimental import pallas as pl
from jax.experimental.pallas import tpu as pltpu
from jax.sharding import PartitionSpec as P

HEAD_DIM = 64
SPAN = 256
MAX_REL = 512
WIDE = 640
HALF = 320
EPSILON = 1e-07
SCALE = (3.0 * HEAD_DIM) ** (-0.5)
LOG2E = 1.4426950408889634
BF = jnp.bfloat16
F32 = jnp.float32
NT = (((1,), (1,)), ((), ()))
NN = (((1,), (0,)), ((), ()))
TN = (((0,), (0,)), ((), ()))
VMEM_LIMIT = 56 << 20


def dot(a, b, dims=NN):
    return lax.dot_general(a, b, dims, preferred_element_type=F32)


def bucket_table():
    relative = HALF - np.arange(WIDE)
    middle = SPAN // 2
    absolute = np.where((relative < middle) & (relative > -middle), middle - 1, np.abs(relative))
    log_position = np.ceil(np.log(absolute / middle) / np.log((MAX_REL - 1) / middle) * (middle - 1)) + middle
    bucket = np.where(absolute <= middle, relative, log_position * np.sign(relative))
    bucket = np.clip(bucket + SPAN, 0, 2 * SPAN - 1).astype(np.int32)
    return (bucket[:, None] == np.arange(2 * SPAN)[None, :]).astype(np.float32)


def assemble(target, own, other, core, count):
    target[pl.ds(pl.multiple_of(core * count, count), count), :] = own[...]
    target[pl.ds(pl.multiple_of((1 - core) * count, count), count), :] = other[...]


def half_of(head):
    lane = lax.broadcasted_iota(jnp.int32, (1, 128), 1)
    return (lane < HEAD_DIM) if head == 0 else (lane >= HEAD_DIM)


def doc_number(position, meta_ref):
    total = jnp.zeros(position.shape, jnp.int32)
    for k in range(3):
        total = total + (position >= meta_ref[k]).astype(jnp.int32)
    return total


def skew(values, base):
    return pltpu.roll(values, base % WIDE, 1, stride=1, stride_axis=0)


def rolled(values):
    return pltpu.roll(values.astype(F32), HEAD_DIM, 1).astype(values.dtype)


def cost(microseconds):
    return pl.CostEstimate(flops=int(microseconds * 1e8), bytes_accessed=1 << 20, transcendentals=0)


def whole_block(*shape):
    return pl.BlockSpec(shape, lambda g, m: (0,) * len(shape))


def prepare_kernel(meta_ref, first_ref, second_ref, rel_ref, table_ref, w_ref, pe_ref):
    first = meta_ref[0] == 0
    low = half_of(0)

    @pl.when(pl.program_id(0) != 1)
    def _():
        for c in range(3):
            w_ref[0, 0, :, 128 * c : 128 * (c + 1)] = first_ref[0, c]

    @pl.when(pl.program_id(0) == 1)
    def _():
        for c in range(3):
            a, b = first_ref[0, c], second_ref[0, c]
            zero = jnp.where(low, a, rolled(b))
            one = jnp.where(low, rolled(a), b)
            w_ref[0, 0, :, 128 * c : 128 * (c + 1)] = jnp.where(first, zero, one)

    pos = dot(rel_ref[0], w_ref[0, 0, :, :256]).astype(BF)
    ext = dot(table_ref[0], pos).astype(BF)
    pe_ref[0, 0, 0] = ext[:, :128]
    pe_ref[0, 0, 1] = ext[:, 128:]
    pe_ref[0, 0, 2] = dot(table_ref[1], pos[:, 128:]).astype(BF)


def prepare(core, layer, qkv_weight, rel_table, tables):
    kinds, model = qkv_weight.shape[1:3]
    pairs, buckets = 3, rel_table.shape[1]
    return pl.pallas_call(
        prepare_kernel,
        out_shape=(
            jax.ShapeDtypeStruct((1, pairs, model, 384), BF),
            jax.ShapeDtypeStruct((1, pairs, 3, WIDE, 128), BF),
        ),
        grid_spec=pltpu.PrefetchScalarGridSpec(
            num_scalar_prefetch=1,
            grid=(pairs,),
            in_specs=[
                pl.BlockSpec(
                    (1, kinds, model, 128),
                    lambda g, m: (layer, 0, 0, jnp.where(g == 1, 1, jnp.where(g == 0, 0, 3) + 2 * m[0])),
                ),
                pl.BlockSpec((1, kinds, model, 128), lambda g, m: (layer, 0, 0, 4)),
                pl.BlockSpec((1, buckets, model), lambda g, m: (layer, 0, 0)),
                whole_block(2, WIDE, buckets),
            ],
            out_specs=(
                pl.BlockSpec((1, 1, model, 384), lambda g, m: (0, g, 0, 0)),
                pl.BlockSpec((1, 1, 3, WIDE, 128), lambda g, m: (0, g, 0, 0, 0)),
            ),
        ),
        compiler_params=pltpu.CompilerParams(vmem_limit_bytes=VMEM_LIMIT),
        cost_estimate=cost(5),
        name="prepare",
    )(core[None], qkv_weight, qkv_weight, rel_table, tables)


def attention_kernel(meta_ref, own_ref, other_ref, w_ref, pe_ref, rev_ref, o_ref, sv_ref, p_ref, x_ref, bt_ref, sb_ref, *, length, blk):
    core = meta_ref[3]

    @pl.when(pl.program_id(0) == 0)
    def _():
        assemble(x_ref, own_ref, other_ref, core, length // 2)

    qkv = dot(x_ref[...], w_ref[0, 0]).astype(BF)
    sv_ref[0, :, :128] = qkv[:, :128]
    sb_ref[...] = qkv
    sv_ref[0, :, 128:] = dot(rev_ref[...], qkv[:, 128:]).astype(BF)
    zero = jnp.zeros((), BF)
    ids_j = doc_number(lax.broadcasted_iota(jnp.int32, (1, length), 1), meta_ref)
    for h in range(2):
        own = half_of(h)
        for b in range(length // blk):
            sl = slice(b * blk, (b + 1) * blk)
            kb = jnp.where(own, sb_ref[sl, 128:256], zero)
            t2 = skew(dot(kb, pe_ref[0, 0, 0], NT), b * blk + HALF)
            bt_ref[:, sl] = t2[:, :length].T
        for b in range(length // blk):
            sl = slice(b * blk, (b + 1) * blk)
            qb = jnp.where(own, sb_ref[sl, :128], zero)
            t1 = skew(dot(qb, pe_ref[0, 0, 1], NT), b * blk + HALF)
            s = dot(qb, sb_ref[:, 128:256], NT) + t1[:, :length] + bt_ref[sl, :]
            ids_i = doc_number(lax.broadcasted_iota(jnp.int32, (blk, 1), 0) + b * blk, meta_ref)
            s = jnp.where(ids_i == ids_j, s, -1e30)
            e = jnp.exp2((s - jnp.max(s, axis=1, keepdims=True)) * (SCALE * LOG2E))
            p = (e * (1.0 / jnp.sum(e, axis=1, keepdims=True))).astype(BF)
            o = dot(p, sb_ref[:, 256:]).astype(BF)
            if h == 0:
                o_ref[sl, :] = o
            else:
                o_ref[sl, :] = jnp.where(own, o, o_ref[sl, :])
            p_ref[h, sl, :] = dot(p, rev_ref[...]).astype(BF)


def attention(meta, layer, group, own, other, w, pe, rev):
    base, pairs = group
    count, model = own.shape
    length = 2 * count
    return pl.pallas_call(
        functools.partial(attention_kernel, length=length, blk=256),
        out_shape=(
            jax.ShapeDtypeStruct((length, pairs * 128), BF),
            jax.ShapeDtypeStruct((pairs, length, 384), BF),
            jax.ShapeDtypeStruct((2 * pairs, length, length), BF),
        ),
        grid_spec=pltpu.PrefetchScalarGridSpec(
            num_scalar_prefetch=1,
            grid=(pairs,),
            in_specs=[
                whole_block(count, model),
                whole_block(count, model),
                pl.BlockSpec((1, 1, model, 384), lambda g, m: (0, base + g, 0, 0)),
                pl.BlockSpec((1, 1, 2, WIDE, 128), lambda g, m: (0, base + g, 0, 0, 0)),
                whole_block(length, length),
            ],
            out_specs=(
                pl.BlockSpec((length, 128), lambda g, m: (0, g)),
                pl.BlockSpec((1, length, 384), lambda g, m: (g, 0, 0)),
                pl.BlockSpec((2, length, length), lambda g, m: (g, 0, 0)),
            ),
            scratch_shapes=[
                pltpu.VMEM((length, model), BF),
                pltpu.VMEM((length, length), F32),
                pltpu.VMEM((length, 384), BF),
            ],
        ),
        compiler_params=pltpu.CompilerParams(vmem_limit_bytes=VMEM_LIMIT),
        cost_estimate=cost(7 * pairs),
        name="attention",
    )(meta, own, other, w, pe, rev)


def attention_grad_kernel(
    meta_ref, own_ref, other_ref, wo_low_ref, wo_high_ref, sv_ref, p_ref, pe_ref, rev_ref, w_ref, table_ref, *rest,
    length, blk, first, last,
):
    if not first:
        before_ref, *rest = rest
    dqkv_ref, dpos_ref, *rest = rest
    if last:
        mine_ref, theirs_ref, *rest = rest
    else:
        sum_ref, *rest = rest
    drb_ref, dt_ref, u_ref, acc_ref, dx_ref = rest
    g = pl.program_id(0)
    core = meta_ref[3]
    count = length // 2

    @pl.when(g == 0)
    def _():
        assemble(drb_ref, own_ref, other_ref, core, count)

    zero = jnp.zeros((), BF)
    pad = jnp.zeros((blk, WIDE - length), F32)
    d_o = dot(drb_ref[...], jnp.concatenate([wo_low_ref[0], wo_high_ref[0]], axis=0), NT).astype(BF)
    q = sv_ref[0, :, :128]
    q_t, kr_t = q.T, sv_ref[0, :, 128:256].T
    for h in range(2):
        own = half_of(h)
        hs = slice(HEAD_DIM * h, HEAD_DIM * (h + 1))
        krh = jnp.where(own, sv_ref[0, :, 128:256], zero)
        pkh = jnp.where(own, pe_ref[0, 0, 2], zero)
        d_oh = jnp.where(own, d_o, zero)
        for b in range(length // blk):
            sl = slice(b * blk, (b + 1) * blk)
            da = dot(d_oh[sl], sv_ref[0, :, 256:], NT)
            p = p_ref[h, sl, :].astype(F32)
            ds = (p * (da - jnp.sum(p * da, axis=1, keepdims=True))).astype(BF)
            wide = ds.astype(F32)
            dt_ref[:, sl] = wide.T
            u = skew(jnp.concatenate([wide, pad], axis=1), b * blk + WIDE - 192).astype(BF)
            u_ref[sl, :] = u
            r = dot(ds, krh) + dot(u, pkh)
            acc_ref[sl, :128] = r if h == 0 else acc_ref[sl, :128] + r
        d_ext = (dot(q_t[hs], u_ref[...]) * SCALE).astype(BF)
        dpos_ref[0, 1, hs, :] = dot(d_ext, table_ref[1]).astype(BF)
        r = dot(p_ref[h], d_oh, TN)
        acc_ref[:, 256:] = r if h == 0 else acc_ref[:, 256:] + r
        qh = jnp.where(own, q, zero)
        pqh = jnp.where(own, pe_ref[0, 0, 0], zero)
        for b in range(length // blk):
            sl = slice(b * blk, (b + 1) * blk)
            z = dt_ref[sl, :]
            u = skew(jnp.concatenate([z, pad], axis=1), b * blk + WIDE - 191).astype(BF)
            u_ref[sl, :] = u
            r = dot(z.astype(BF), qh) + dot(u, pqh)
            acc_ref[sl, 128:256] = r if h == 0 else acc_ref[sl, 128:256] + r
        d_ext = (dot(kr_t[hs], u_ref[...]) * SCALE).astype(BF)
        dpos_ref[0, 0, hs, :] = dot(d_ext, table_ref[0]).astype(BF)
    dq = (acc_ref[:, :128] * SCALE).astype(BF)
    dk = (acc_ref[:, 128:256] * SCALE).astype(BF)
    dv = acc_ref[:, 256:].astype(BF)
    dkv = dot(rev_ref[...], jnp.concatenate([dk, dv], axis=1)).astype(BF)
    dqkv = jnp.concatenate([dq, dkv], axis=1)
    dqkv_ref[0] = dqkv
    part = dot(dqkv, w_ref[0, 0], NT)

    @pl.when(g == 0)
    def _():
        dx_ref[...] = part if first else part + before_ref[...]

    @pl.when(g > 0)
    def _():
        dx_ref[...] = dx_ref[...] + part

    @pl.when(g == pl.num_programs(0) - 1)
    def _():
        if last:
            mine_ref[...] = dx_ref[pl.ds(pl.multiple_of(core * count, count), count), :]
            theirs_ref[...] = dx_ref[pl.ds(pl.multiple_of((1 - core) * count, count), count), :].astype(BF)
        else:
            sum_ref[...] = dx_ref[...]


def attention_grad(meta, layer, group, own, other, wo, saved, probs, pe, rev, w, tables, before, last):
    base, pairs = group
    buckets = tables.shape[2]
    count, model = own.shape
    length = 2 * count
    low = lambda g, m: (layer, jnp.where(base + g == 1, 2 + m[3], 3 * (base + g) + 4 * m[3]), 0)
    high = lambda g, m: (layer, jnp.where(base + g == 1, 8 + m[3], 3 * (base + g) + 4 * m[3] + 1), 0)
    if last:
        sums = [jax.ShapeDtypeStruct((count, model), F32), jax.ShapeDtypeStruct((count, model), BF)]
    else:
        sums = [jax.ShapeDtypeStruct((length, model), F32)]
    extra = [] if before is None else [before]
    return pl.pallas_call(
        functools.partial(attention_grad_kernel, length=length, blk=256, first=before is None, last=last),
        out_shape=[
            jax.ShapeDtypeStruct((pairs, length, 384), BF),
            jax.ShapeDtypeStruct((pairs, 2, 128, buckets), BF),
        ] + sums,
        grid_spec=pltpu.PrefetchScalarGridSpec(
            num_scalar_prefetch=1,
            grid=(pairs,),
            in_specs=[
                whole_block(count, model),
                whole_block(count, model),
                pl.BlockSpec((1, 64, model), low),
                pl.BlockSpec((1, 64, model), high),
                pl.BlockSpec((1, length, 384), lambda g, m: (g, 0, 0)),
                pl.BlockSpec((2, length, length), lambda g, m: (g, 0, 0)),
                pl.BlockSpec((1, 1, 3, WIDE, 128), lambda g, m: (0, base + g, 0, 0, 0)),
                whole_block(length, length),
                pl.BlockSpec((1, 1, model, 384), lambda g, m: (0, base + g, 0, 0)),
                whole_block(2, WIDE, buckets),
            ] + [whole_block(length, model)] * len(extra),
            out_specs=[
                pl.BlockSpec((1, length, 384), lambda g, m: (g, 0, 0)),
                pl.BlockSpec((1, 2, 128, buckets), lambda g, m: (g, 0, 0, 0)),
            ] + [whole_block(*item.shape) for item in sums],
            scratch_shapes=[
                pltpu.VMEM((length, model), BF),
                pltpu.VMEM((length, length), F32),
                pltpu.VMEM((length, WIDE), BF),
                pltpu.VMEM((length, 384), F32),
                pltpu.VMEM((length, model), F32),
            ],
        ),
        compiler_params=pltpu.CompilerParams(vmem_limit_bytes=VMEM_LIMIT),
        cost_estimate=cost(8 * pairs),
        name="attention_grad",
    )(meta, own, other, wo, wo, saved, probs, pe, rev, w, tables, *extra)


def pieces_kernel(meta_ref, in_ref, down_ref, in_piece, down_piece):
    in_piece[...] = in_ref[0]
    down_piece[...] = down_ref[0]


def weight_pieces(seq, layer, ffn_in, ffn_out):
    model, hidden = ffn_in.shape[1:]
    rows = model // 2
    steps = 4
    return pl.pallas_call(
        pieces_kernel,
        out_shape=[jax.ShapeDtypeStruct((rows, hidden), BF)] * 2,
        grid_spec=pltpu.PrefetchScalarGridSpec(
            num_scalar_prefetch=1,
            grid=(steps,),
            in_specs=[pl.BlockSpec((1, rows // steps, hidden), lambda g, m: (layer, steps * m[0] + g, 0))] * 2,
            out_specs=[pl.BlockSpec((rows // steps, hidden), lambda g, m: (g, 0))] * 2,
        ),
        cost_estimate=cost(1),
        name="weight_pieces",
    )(seq[None], ffn_in, ffn_out)


def weight_copies(layer, refs, scratch, sems, meta_ref):
    shards = []
    for s in range(4):
        group = []
        for m in range(2):
            own, core_own, near, far, core_near, core_far = refs[m]
            place = scratch.at[m, s]
            if s < 2:
                group.append(((own if s == 0 else core_own).at[layer], place))
            else:
                first, second = (near, far) if s == 2 else (core_near, core_far)
                rows = first.shape[0]
                one = pl.multiple_of(meta_ref[4] * rows, rows)
                two = pl.multiple_of((1 - meta_ref[4]) * rows, rows)
                group.append((first, place.at[pl.ds(one, rows)]))
                group.append((second, place.at[pl.ds(two, rows)]))
        shards.append(group)
    copies, k = [], 0
    for group in shards:
        made = []
        for source, target in group:
            made.append(pltpu.make_async_copy(source, target, sems.at[k]))
            k += 1
        copies.append(made)
    return copies


COPIES = 12


def row_norm(state, gain, bias):
    centered = state - jnp.mean(state, axis=1, keepdims=True)
    inverse = lax.rsqrt(jnp.mean(centered * centered, axis=1, keepdims=True) + EPSILON)
    return centered * inverse * gain + bias


def row_norm_grad(state, gain, d_result):
    centered = state - jnp.mean(state, axis=1, keepdims=True)
    inverse = lax.rsqrt(jnp.mean(centered * centered, axis=1, keepdims=True) + EPSILON)
    unit = centered * inverse
    d_unit = d_result * gain
    d_state = inverse * (
        d_unit
        - jnp.mean(d_unit, axis=1, keepdims=True)
        - unit * jnp.mean(d_unit * unit, axis=1, keepdims=True)
    )
    return d_state, jnp.sum(d_result * unit, axis=0, keepdims=True), jnp.sum(d_result, axis=0, keepdims=True)


def head_rows(core):
    return ((256 * core, 128), (128 + 64 * core, 64), (512 + 64 * core, 64), (384 + 256 * core, 128))


def tokens_kernel(meta_ref, *rest, layer, chunk, groups):
    o_refs, rest = rest[: 2 * groups], rest[2 * groups :]
    x_ref, wo_ref, norm_ref, *rest = rest
    wires, rest = rest[:12], rest[12:]
    y_ref, yb_ref, mb_ref, resid_ref, pre_ref, slope_ref, scratch, sems, heads = rest
    copies = weight_copies(layer, (wires[:6], wires[6:]), scratch, sems, meta_ref)
    for group in copies:
        for item in group:
            item.start()
    at = 0
    for core in (meta_ref[3], 1 - meta_ref[3]):
        for first, size in head_rows(core):
            heads[at : at + size] = wo_ref[0, pl.ds(pl.multiple_of(first, 64), size), :]
            at += size
    resid = x_ref[...].astype(F32) + dot(jnp.concatenate([o[...] for o in o_refs], axis=1), heads[...])
    resid_ref[...] = resid
    middle = row_norm(resid, norm_ref[0:1, :], norm_ref[1:2, :])
    mb = middle.astype(BF)
    mb_ref[...] = mb
    pre_ref[...] = middle
    hidden = scratch.shape[3]
    per = hidden // chunk
    total = 4 * per

    def up(k):
        s, c = k // per, k % per
        if c == 0:
            for item in copies[s]:
                item.wait()
        return dot(mb, scratch[0, s, :, c * chunk : (c + 1) * chunk])

    ahead = up(0)
    for k in range(total):
        s, c = k // per, k % per
        h = ahead
        if k + 1 < total:
            ahead = up(k + 1)
        cumulative = 0.5 * (1.0 + lax.erf(h * 0.7071067811865476))
        density = jnp.exp(-0.5 * h * h) * 0.3989422804014327
        slope_ref[:, k * chunk : (k + 1) * chunk] = (cumulative + h * density).astype(BF)
        act = (h * cumulative).astype(BF)
        pre_ref[...] = pre_ref[...] + dot(act, scratch[1, s, :, c * chunk : (c + 1) * chunk], NT)
    y = row_norm(pre_ref[...], norm_ref[2:3, :], norm_ref[3:4, :])
    y_ref[...] = y
    yb_ref[...] = y.astype(BF)


def token_step(meta, layer, o_own, o_other, x, wo, norms, wires):
    count, model = x.shape
    hidden = wires[0].shape[2]
    mine = [pl.BlockSpec((count, o.shape[1]), lambda g, m: (m[3], 0)) for o in o_own + o_other]
    hbm = pl.BlockSpec(memory_space=pl.ANY)
    return pl.pallas_call(
        functools.partial(tokens_kernel, layer=layer, chunk=768, groups=len(o_own)),
        out_shape=(
            jax.ShapeDtypeStruct((count, model), F32),
            jax.ShapeDtypeStruct((count, model), BF),
            jax.ShapeDtypeStruct((count, model), BF),
            jax.ShapeDtypeStruct((count, model), F32),
            jax.ShapeDtypeStruct((count, model), F32),
            jax.ShapeDtypeStruct((count, 4 * hidden), BF),
        ),
        grid_spec=pltpu.PrefetchScalarGridSpec(
            num_scalar_prefetch=1,
            grid=(1,),
            in_specs=mine + [
                whole_block(count, model),
                pl.BlockSpec((1, model, model), lambda g, m: (layer, 0, 0)),
                whole_block(4, model),
            ] + [hbm] * 12,
            out_specs=(
                whole_block(count, model), whole_block(count, model), whole_block(count, model), whole_block(count, model), whole_block(count, model),
                whole_block(count, 4 * hidden),
            ),
            scratch_shapes=[
                pltpu.VMEM((2, 4, model, hidden), BF),
                pltpu.SemaphoreType.DMA((COPIES,)),
                pltpu.VMEM((model, model), BF),
            ],
        ),
        compiler_params=pltpu.CompilerParams(vmem_limit_bytes=VMEM_LIMIT),
        cost_estimate=cost(10),
        name="token_step",
    )(meta, *o_own, *o_other, x, wo, norms, *wires)


def tokens_grad_kernel(meta_ref, *rest, layer, chunk, parts):
    ups, rest = rest[:parts], rest[parts:]
    pre_ref, resid_ref, slope_ref, norm_ref, *rest = rest
    wires, rest = rest[:12], rest[12:]
    df_ref, dr_ref, drb_ref, dn_ref, scratch, sems, dm_ref = rest
    copies = weight_copies(layer, (wires[:6], wires[6:]), scratch, sems, meta_ref)
    for group in copies:
        for item in group:
            item.start()
    dy = ups[0][...].astype(F32)
    for item in ups[1:]:
        dy = dy + item[...].astype(F32)
    dz, dg2, db2 = row_norm_grad(pre_ref[...], norm_ref[2:3, :], dy)
    df = dz.astype(BF)
    df_ref[...] = df
    dm_ref[...] = dz
    hidden = scratch.shape[3]
    per = hidden // chunk
    total = 4 * per

    def down(k):
        s, c = k // per, k % per
        if c == 0:
            for item in copies[s]:
                item.wait()
        return dot(df, scratch[1, s, :, c * chunk : (c + 1) * chunk])

    ahead = down(0)
    for k in range(total):
        s, c = k // per, k % per
        dg = ahead
        if k + 1 < total:
            ahead = down(k + 1)
        dh = (dg * slope_ref[:, k * chunk : (k + 1) * chunk].astype(F32)).astype(BF)
        dm_ref[...] = dm_ref[...] + dot(dh, scratch[0, s, :, c * chunk : (c + 1) * chunk], NT)
    dr, dg1, db1 = row_norm_grad(resid_ref[...], norm_ref[0:1, :], dm_ref[...])
    dr_ref[...] = dr
    drb_ref[...] = dr.astype(BF)
    dn_ref[0:1, :] = dg1
    dn_ref[1:2, :] = db1
    dn_ref[2:3, :] = dg2
    dn_ref[3:4, :] = db2


def token_grad(meta, layer, ups, pre, resid, slope, norms, wires):
    count, model = pre.shape
    hidden = wires[0].shape[2]
    hbm = pl.BlockSpec(memory_space=pl.ANY)
    return pl.pallas_call(
        functools.partial(tokens_grad_kernel, layer=layer, chunk=768, parts=len(ups)),
        out_shape=(
            jax.ShapeDtypeStruct((count, model), BF),
            jax.ShapeDtypeStruct((count, model), F32),
            jax.ShapeDtypeStruct((count, model), BF),
            jax.ShapeDtypeStruct((4, model), F32),
        ),
        grid_spec=pltpu.PrefetchScalarGridSpec(
            num_scalar_prefetch=1,
            grid=(1,),
            in_specs=[whole_block(count, model)] * len(ups)
            + [whole_block(count, model), whole_block(count, model), whole_block(count, 4 * hidden), whole_block(4, model)]
            + [hbm] * 12,
            out_specs=(whole_block(count, model), whole_block(count, model), whole_block(count, model), whole_block(4, model)),
            scratch_shapes=[
                pltpu.VMEM((2, 4, model, hidden), BF),
                pltpu.SemaphoreType.DMA((COPIES,)),
                pltpu.VMEM((count, model), F32),
            ],
        ),
        compiler_params=pltpu.CompilerParams(vmem_limit_bytes=VMEM_LIMIT),
        cost_estimate=cost(10),
        name="token_grad",
    )(meta, *ups, pre, resid, slope, norms, *wires)


def hidden_grad_kernel(meta_ref, *refs):
    m_refs, d_refs = refs[:4], refs[4:8]
    wi_ref, wd_ref, keep_ref, give_ref, m_ref, d_ref, mt_ref, dt_ref = refs[8:]

    @pl.when(pl.program_id(0) == 0)
    def _():
        for sources, target, transposed in ((m_refs, m_ref, mt_ref), (d_refs, d_ref, dt_ref)):
            for k, source in enumerate(sources):
                count = source.shape[0]
                target[k * count : (k + 1) * count, :] = source[...]
                transposed[:, k * count : (k + 1) * count] = source[...].T

    h = dot(m_ref[...], wi_ref[0])
    cumulative = 0.5 * (1.0 + lax.erf(h * 0.7071067811865476))
    density = jnp.exp(-0.5 * h * h) * 0.3989422804014327
    act = (h * cumulative).astype(BF)
    dh = (dot(d_ref[...], wd_ref[0]) * (cumulative + h * density)).astype(BF)
    rows = mt_ref.shape[0] // 2
    for target, part in ((keep_ref, meta_ref[4]), (give_ref, 1 - meta_ref[4])):
        place = pl.ds(pl.multiple_of(part * rows, rows), rows)
        target[0] = dot(mt_ref[place, :], dh).astype(BF)
        target[1] = dot(dt_ref[place, :], act).astype(BF)


def hidden_grad(meta, layer, rows, d_rows, w_in, w_down):
    count, model = rows[0].shape
    hidden = w_in.shape[2]
    chunk = 256
    return pl.pallas_call(
        hidden_grad_kernel,
        out_shape=[jax.ShapeDtypeStruct((2, model // 2, hidden), BF)] * 2,
        grid_spec=pltpu.PrefetchScalarGridSpec(
            num_scalar_prefetch=1,
            grid=(hidden // chunk,),
            in_specs=[whole_block(count, model)] * 8 + [
                pl.BlockSpec((1, model, chunk), lambda g, m: (layer, 0, g)),
                pl.BlockSpec((1, model, chunk), lambda g, m: (layer, 0, g)),
            ],
            out_specs=[pl.BlockSpec((2, model // 2, chunk), lambda g, m: (0, 0, g))] * 2,
            scratch_shapes=[pltpu.VMEM((4 * count, model), BF)] * 2 + [pltpu.VMEM((model, 4 * count), BF)] * 2,
        ),
        compiler_params=pltpu.CompilerParams(vmem_limit_bytes=VMEM_LIMIT),
        cost_estimate=cost(10),
        name="hidden_grad",
    )(meta, *rows, *d_rows, w_in, w_down)


def projection_grad_kernel(
    meta_ref, x_own_ref, x_other_ref, d_own_ref, d_other_ref, *rest, length, chunks, pairs, groups, grads,
):
    lists = []
    for size in (groups, groups, grads[0], grads[1], grads[1]):
        lists.append(rest[:size])
        rest = rest[size:]
    o_own = [o.at[:, 128 * k : 128 * (k + 1)] for o in lists[0] for k in range(o.shape[1] // 128)]
    o_other = [o.at[:, 128 * k : 128 * (k + 1)] for o in lists[1] for k in range(o.shape[1] // 128)]
    dqkv, dpos, dpos_other = ([r.at[k] for r in part for k in range(r.shape[0])] for part in lists[2:])
    rel_ref, wq_ref, wk_ref, a_keep, a_give, b_keep, b_give, *rest = rest
    x_ref, d_ref, left_ref, out_ref, right_ref, pos_ref, w_ref = rest
    core = meta_ref[3]
    seq = meta_ref[4]
    y_own = meta_ref[5]
    count = length // 2
    model = x_ref.shape[1]
    buckets = rel_ref.shape[1]
    low = half_of(0)
    zero = jnp.zeros((), BF)
    assemble(x_ref, x_own_ref, x_other_ref, core, count)
    assemble(d_ref, d_own_ref, d_other_ref, core, count)
    left_ref[:, :length] = x_ref[...].T
    left_ref[:, length:] = rel_ref[0].T
    for place, o, dp in ((core, o_own, dpos), (1 - core, o_other, dpos_other)):
        at = 0
        for first, size in head_rows(place):
            rows = pl.ds(pl.multiple_of(first, 64), size)
            p, inner = at // 128, at % 128
            if inner == 0:
                o_t = o[p][...].T
            out_ref[rows, :] = o_t[inner : inner + size]
            for c in range(2):
                pos_ref[c, rows, :] = dp[p][c, inner : inner + size, :]
            at += size
    per = model // chunks
    first_core = core == 0
    half_chunks = chunks // 2
    tile = lambda c, p: dqkv[p][:, 128 * c : 128 * (c + 1)]
    own_pos = [[dpos[p][c].astype(F32).T.astype(BF) for p in range(pairs)] for c in range(2)]
    at = 0
    for first, size in head_rows(core):
        rows = pl.ds(pl.multiple_of(first, 64), size)
        w_ref[0, at : at + size, :] = wq_ref[0, 0, rows, :]
        w_ref[1, at : at + size, :] = wk_ref[0, 0, rows, :]
        at += size
    back = (dot(w_ref[0], pos_ref[0]) + dot(w_ref[1], pos_ref[1])).T
    share = buckets // chunks
    for y in range(2):
        full = 0 if y == 0 else 2
        if y == 0:
            mixed = lambda q, k: jnp.where(low, q, rolled(k))
            v_mix = jnp.where(low, tile(2, 1), zero)
        else:
            mixed = lambda q, k: jnp.where(low, rolled(q), k)
            v_mix = jnp.where(low, rolled(tile(2, 1)), zero)
        right_ref[:length, 0:128] = tile(0, full)
        right_ref[:length, 128:256] = tile(1, full)
        right_ref[:length, 256:384] = mixed(tile(0, 1), tile(1, 1))
        right_ref[length:, 0:128] = own_pos[0][full]
        right_ref[length:, 128:256] = own_pos[1][full]
        right_ref[length:, 256:384] = mixed(own_pos[0][1], own_pos[1][1])
        base = 384 * y
        t0, t1, t2 = (d_ref[:, base + 128 * k : base + 128 * (k + 1)] for k in range(3))
        of = jnp.where(first_core, t0, t2)
        om = jnp.where(low, zero, jnp.where(first_core, rolled(t1), t1))
        one = dot(left_ref[...], right_ref[...])
        two = dot(left_ref[:, :length], jnp.concatenate([tile(2, full), v_mix], axis=1))
        three = dot(out_ref[...], jnp.concatenate([om, of], axis=1))
        rel_full = back[:, 128 * full : 128 * (full + 1)]
        rel_rest = back[:, 128:256] if y == 0 else pltpu.roll(back[:, 128:256], HEAD_DIM, 1)

        def store_a(ref, n, keep):
            rows = slice(n * per, (n + 1) * per)
            ref[keep, :per, :] = one[rows].astype(BF)
            for k in range(3):
                part = slice(n * share + 16 * k, n * share + 16 * (k + 1))
                ref[keep, per:, 128 * k : 128 * (k + 1)] = rel_full[part].astype(BF)

        def store_b(ref, n, keep):
            rows = slice(n * per, (n + 1) * per)
            ref[keep, :per, 0:128] = two[rows, :128].astype(BF)
            ref[keep, :per, 128:256] = (two[rows, 128:] + three[rows, :128]).astype(BF)
            ref[keep, :per, 256:384] = three[rows, 128:].astype(BF)
            ref[keep, per:, 0:128] = rel_full[n * share + 48 : (n + 1) * share].astype(BF)
            for k in range(2):
                a = rel_rest[n * share + 32 * k : n * share + 32 * k + 16]
                b = rel_rest[n * share + 32 * k + 16 : n * share + 32 * k + 32]
                ref[keep, per:, 128 * (k + 1) : 128 * (k + 2)] = jnp.where(low, a, pltpu.roll(b, HEAD_DIM, 1)).astype(BF)

        @pl.when(y_own == y)
        def _():
            for n in range(chunks):
                store_a(a_keep, n, n)

        @pl.when(y_own != y)
        def _():
            for n in range(chunks):
                store_a(a_give, n, n)

        for s in range(2):
            @pl.when(seq == s)
            def _():
                for n in range(chunks):
                    kept = n // half_chunks == s
                    store_b((b_keep if kept else b_give).at[y], n, n % half_chunks)


def projection_grad(meta, layer, x_own, x_other, dqkv, o_own, o_other, d_own, d_other, dpos, dpos_other, rel, qkv_weight):
    count, model = x_own.shape
    length = 2 * count
    buckets = rel.shape[1]
    chunks = 8
    rows = model // chunks + 16
    args = (x_own, x_other, d_own, d_other, *o_own, *o_other, *dqkv, *dpos, *dpos_other)
    return pl.pallas_call(
        functools.partial(
            projection_grad_kernel, length=length, chunks=chunks, pairs=3, groups=len(o_own), grads=(len(dqkv), len(dpos))
        ),
        out_shape=[jax.ShapeDtypeStruct((chunks, rows, model // 2), BF)] * 2
        + [jax.ShapeDtypeStruct((2, chunks // 2, rows, model // 2), BF)] * 2,
        grid_spec=pltpu.PrefetchScalarGridSpec(
            num_scalar_prefetch=1,
            grid=(1,),
            in_specs=[whole_block(*a.shape) for a in args]
            + [
                pl.BlockSpec((1, buckets, model), lambda g, m: (layer, 0, 0)),
                pl.BlockSpec((1, 1, model, model), lambda g, m: (layer, 0, 0, 0)),
                pl.BlockSpec((1, 1, model, model), lambda g, m: (layer, 1, 0, 0)),
            ],
            out_specs=[whole_block(chunks, rows, model // 2)] * 2 + [whole_block(2, chunks // 2, rows, model // 2)] * 2,
            scratch_shapes=[
                pltpu.VMEM((length, model), BF),
                pltpu.VMEM((length, model), BF),
                pltpu.VMEM((model, length + buckets), BF),
                pltpu.VMEM((model, length), BF),
                pltpu.VMEM((length + buckets, 384), BF),
                pltpu.VMEM((2, model, buckets), BF),
                pltpu.VMEM((2, 384, model), BF),
            ],
        ),
        compiler_params=pltpu.CompilerParams(vmem_limit_bytes=VMEM_LIMIT),
        cost_estimate=cost(10),
        name="projection_grad",
    )(meta, *args, rel, qkv_weight, qkv_weight)


class Wires:
    def __init__(self):
        self.seqs, self.rows, self.cols = (lax.axis_size(name) for name in ("seq", "rows", "col"))
        self.seq, self.row, self.col = (lax.axis_index(name) for name in ("seq", "rows", "col"))
        self.core, self.y = self.col % 2, self.col // 2

    def send(self, array, target):
        pairs = []
        for s in range(self.seqs):
            for r in range(self.rows):
                for c in range(self.cols):
                    t = target(s, r, c)
                    pairs.append(((s * self.rows + r) * self.cols + c, (t[0] * self.rows + t[1]) * self.cols + t[2]))
        return lax.ppermute(array, ("seq", "rows", "col"), pairs)

    def turn(self, array):
        return self.send(array, lambda s, r, c: (c % 2, r, c - c % 2 + s))

    def to_core(self, array):
        return self.send(array, lambda s, r, c: (s, r, c ^ 1))

    def to_y(self, array):
        return self.send(array, lambda s, r, c: (s, r, c ^ 2))

    def to_seq(self, array):
        return self.send(array, lambda s, r, c: (1 - s, r, c))

    def to_row(self, array, bit):
        return self.send(array, lambda s, r, c: (s, r ^ (1 << bit), c))


def cut(array, axis, mine):
    shape = array.shape
    pairs = array.reshape(shape[:axis] + (shape[axis] // 2, 2) + shape[axis + 1 :])
    return pick(pairs, axis + 1, mine), pick(pairs, axis + 1, 1 - mine)


def bits_of(count):
    return count.bit_length() - 1


def add(a, b):
    return (a.astype(F32) + b.astype(F32)).astype(a.dtype)


def pick(array, axis, index):
    return lax.dynamic_index_in_dim(array, index, axis, keepdims=False)


def unpack(main, rel, wires):
    t = [main[:, 128 * k : 128 * (k + 1)] for k in range(6)]
    full = [t[0], t[1], t[3], t[5], rel[:, :128]]
    rest = [t[2][:, :64], t[2][:, 64:], t[4][:, :64], t[4][:, 64:], rel[:, 128:]]
    out = []
    for f, r in zip(full, rest):
        out.append(jnp.where(wires.core == 0, jnp.concatenate([f, r], 1), jnp.concatenate([r, f], 1)).astype(F32))
    return out


def norm_flow(norms, wires):
    layers, kinds, model = norms.shape
    norms = norms.reshape(layers, 2, 2, model)
    got = yield [(wires.to_core, pick(norms, 2, 1 - wires.core))]
    norms = pick(norms, 2, wires.core) + got[0]
    got = yield [(wires.to_y, pick(norms, 1, 1 - wires.y))]
    norms = pick(norms, 1, wires.y) + got[0]
    parts = wires.seqs * wires.rows
    norms = norms.reshape(layers, wires.seqs, wires.rows, model // parts)
    for bit in range(bits_of(wires.rows)):
        keep, give = cut(norms, 2, (wires.row >> bit) & 1)
        got = yield [(functools.partial(wires.to_row, bit=bit), give)]
        norms = keep + got[0]
    norms = norms[:, :, 0]
    got = yield [(wires.to_seq, pick(norms, 1, 1 - wires.seq))]
    return pick(norms, 1, wires.seq) + got[0]


def after(arrays, *earlier):
    return lax.optimization_barrier((arrays, earlier))[0]


def hidden_flow(keep, give, wires):
    got = yield [(wires.to_seq, give)]
    total = add(keep, got[0])
    total = total.reshape(2, wires.rows, total.shape[1] // wires.rows, total.shape[2])
    for bit in range(bits_of(wires.rows)):
        keep, give = cut(total, 1, (wires.row >> bit) & 1)
        got = yield [(functools.partial(wires.to_row, bit=bit), give)]
        total = add(keep, got[0])
    return total[:, 0].astype(F32)


def projection_flow(a_keep, a_give, b_keep, b_give, wires):
    got = yield [(wires.to_y, a_give), (wires.to_seq, b_give)]
    a = add(a_keep, got[0]).reshape((2, 4) + a_keep.shape[1:])
    b = add(b_keep, got[1])
    got = yield [(wires.to_seq, pick(a, 0, 1 - wires.seq)), (wires.to_y, pick(b, 0, 1 - wires.y))]
    both = jnp.stack([add(pick(a, 0, wires.seq), got[0]), add(pick(b, 0, wires.y), got[1])])
    low = bits_of(wires.rows) - 2
    for bit in (low, low + 1):
        keep, give = cut(both, 1, (wires.row >> bit) & 1)
        got = yield [(functools.partial(wires.to_row, bit=bit), give)]
        both = add(keep, got[0])
    both = both[:, 0]
    main = jnp.concatenate([both[0, :-16], both[1, :-16]], axis=1)
    tail = jnp.concatenate([both[0, -16:], both[1, -16:]], axis=1)
    full = jnp.concatenate([tail[:, 128 * k : 128 * (k + 1)] for k in range(4)], axis=0)
    rest = jnp.concatenate([tail[:, 512 + 64 * k : 576 + 64 * k] for k in range(4)], axis=0)
    rel = jnp.concatenate([full, rest], axis=1)
    for bit in reversed(range(low)):
        mine = (wires.row >> bit) & 1
        sums = []
        for v in (main, rel):
            v = v.reshape((2, v.shape[0] // 2) + v.shape[1:])
            sums.append(add(pick(v, 0, mine), wires.to_row(pick(v, 0, 1 - mine), bit)))
        main, rel = sums
    return unpack(main, rel, wires)


class Flow:
    def __init__(self, steps):
        self.steps, self.value = steps, None
        self.take(next(steps))

    def take(self, sends):
        self.ready = [array for _, array in sends]
        self.under_way = [send(array) for send, array in sends]

    def step(self, *earlier):
        if self.under_way is None:
            return
        arrived = after(self.under_way, earlier) if earlier else self.under_way
        try:
            self.take(self.steps.send(arrived))
        except StopIteration as stop:
            self.ready, self.under_way, self.value = stop.value, None, stop.value

    def finish(self, *earlier):
        while self.under_way is not None:
            self.step(*earlier)
        return self.value


def gather_start(rows, wires):
    return rows, wires.to_core(rows), wires.to_y(rows)


def gather_end(gathered, wires, *earlier):
    rows, other, far = gathered
    return rows, other, far, wires.to_core(after(far, earlier))


def per_device(tokens, lengths, qkv_weight, out_weight, rel_table, ffn_in, ffn_out, norm_params, cotangent):
    wires = Wires()
    core = wires.core
    count, model = tokens.shape[1:]
    length = 2 * count
    layers = qkv_weight.shape[0]
    table_np = bucket_table()
    tables = jnp.asarray(np.stack([table_np, table_np[::-1]]), BF)
    rev = jnp.asarray(np.eye(length)[::-1], BF)
    split = [(0, 1), (1, 1), (2, 1)]
    joined = [(0, 3)]

    weights = (ffn_in, ffn_out)
    pieces = [weight_pieces(wires.seq, 0, ffn_in, ffn_out), None]
    start = wires.turn(tokens[0])
    near = [[wires.to_y(piece) for piece in pieces[0]], [None, None]]
    far, core_near, core_far = ([[None, None], [None, None]] for _ in range(3))
    lengths = jnp.where(core == wires.seq, lengths, wires.to_core(lengths))
    ends = jnp.cumsum(lengths[0]).astype(jnp.int32)
    meta = jnp.concatenate([ends[:3], jnp.stack([core, wires.seq, wires.y])]).astype(jnp.int32)
    prepared = [prepare(after(core, pieces[0], meta), 0, qkv_weight, rel_table, tables)]
    pieces[1] = weight_pieces(after(wires.seq, prepared[0]), 1, ffn_in, ffn_out)

    xb = start
    xb_other = wires.to_core(start)
    core_own = [wires.to_core(after(ffn_in, prepared[0])), None]
    near[1][0] = wires.to_y(pieces[1][0])
    w_pairs, pe = prepared[0]
    outs = []

    def attend(group, *arrived):
        outs.append(attention(meta, 0, group, after(xb, arrived), xb_other, w_pairs, pe, rev))

    attend(split[0], near[0][0], pieces[1], core_own[0])
    far[0][0] = wires.to_seq(after(near[0][0], outs[0]))
    core_near[0][0] = wires.to_core(after(near[0][0], outs[0]))
    core_own[1] = wires.to_core(after(ffn_out, outs[0]))
    attend(split[1], outs[0], near[0][1])
    far[0][1] = wires.to_seq(after(near[0][1], outs[1]))
    core_near[0][1] = wires.to_core(after(near[0][1], outs[1]))
    core_far[0][0] = wires.to_core(after(far[0][0], outs[1]))
    near[1][1] = wires.to_y(after(pieces[1][1], outs[1]))
    attend(split[2], outs[1], far[0][0], core_near[0][0], core_own[1])
    o_own = [jnp.concatenate([item[0] for item in outs], axis=1)]
    o_other = [wires.to_core(item) for item in o_own]
    prepared.append(
        prepare(after(core, o_own, core_near[0][1], core_far[0][0], near[1][0]), 1, qkv_weight, rel_table, tables)
    )
    far[1][0] = wires.to_seq(after(near[1][0], prepared[1]))
    core_far[0][1] = wires.to_core(after(far[0][1], prepared[1]))
    core_near[1][0] = wires.to_core(after(near[1][0], prepared[1]))

    def wire_args(n):
        return [
            item for m in range(2)
            for item in (weights[m], core_own[m], near[n][m], far[n][m], core_near[n][m], core_far[n][m])
        ]

    x = after(start, prepared[1])
    y, yb, mb, resid, pre, slope = token_step(meta, 0, o_own, o_other, x, out_weight, norm_params[0], wire_args(0))
    kept = [(xb, xb_other, outs, o_own, o_other, resid, pre, slope, mb)]

    xb, xb_other = yb, wires.to_core(yb)
    far[1][1] = wires.to_seq(after(near[1][1], yb))
    core_near[1][1] = wires.to_core(after(near[1][1], yb))
    core_far[1][0] = wires.to_core(after(far[1][0], yb))
    w_pairs, pe = prepared[1]
    outs = [attention(meta, 1, (0, 3), after(xb, near[1][1], core_near[1][0]), xb_other, w_pairs, pe, rev)]
    o_own = [outs[0][0]]
    o_other = [wires.to_core(item) for item in o_own]
    core_far[1][1] = wires.to_core(after(far[1][1], o_own))
    d_final = wires.turn(after(cotangent[0], o_own))
    y, yb, mb, resid, pre, slope = token_step(meta, 1, o_own, o_other, y, out_weight, norm_params[1], wire_args(1))
    kept.append((xb, xb_other, outs, o_own, o_other, resid, pre, slope, mb))
    m_rows = [gather_start(after(kept[0][-1], y), wires), gather_start(mb, wires)]

    norms = [None] * layers
    xb, xb_other, outs, o_own, o_other, resid, pre, slope, mb = kept[1]
    w_pairs, pe = prepared[1]
    df, dr, drb, norms[1] = token_grad(meta, 1, [after(d_final, m_rows[1][0])], pre, resid, slope, norm_params[1], wire_args(1))
    drb_other = wires.to_core(drb)
    output = wires.turn(after(y, drb))
    d_rows = [None, gather_start(df, wires)]
    m_rows[1] = gather_end(m_rows[1], wires, drb)
    saved, probs = outs[0][1:]
    dqkv, dpos, dx_mine, dx_theirs = attention_grad(
        meta, 1, (0, 3), after(drb, m_rows[1][1]), drb_other, out_weight, saved, probs, pe, rev, w_pairs, tables, None, True
    )
    m_rows[0] = gather_end(m_rows[0], wires, dx_mine)
    d_rows[1] = gather_end(d_rows[1], wires, dx_mine)
    dx_got = wires.to_core(dx_theirs)
    dpos_other = wires.to_core(dpos)
    h_keep, h_give = hidden_grad(after(meta, dx_mine, output), 1, m_rows[1], d_rows[1], ffn_in, ffn_out)
    hidden = [None, Flow(hidden_flow(h_keep, h_give, wires))]
    projection = [None, None]
    projection_args = (xb, xb_other, [dqkv], o_own, o_other, drb, drb_other, [dpos], [dpos_other], rel_table, qkv_weight)

    xb, xb_other, outs, o_own, o_other, resid, pre, slope, mb = kept[0]
    w_pairs, pe = prepared[0]
    ups = [after(dr, h_keep, dpos_other, m_rows[0]), dx_mine, dx_got]
    df, dr, drb, norms[0] = token_grad(meta, 0, ups, pre, resid, slope, norm_params[0], wire_args(0))
    d_rows[0] = gather_start(df, wires)
    norm_sum = Flow(norm_flow(jnp.stack(norms), wires))
    packed = projection_grad(after(meta, df), 1, *projection_args)
    projection[1] = Flow(projection_flow(*packed, wires))
    d_rows[0] = gather_end(d_rows[0], wires, packed)
    norm_sum.step(packed)
    drb_other = wires.to_core(after(drb, packed))
    h_keep, h_give = hidden_grad(after(meta, packed, norm_sum.ready), 0, m_rows[0], d_rows[0], ffn_in, ffn_out)
    norm_sum.step(h_keep)
    hidden[0] = Flow(hidden_flow(h_keep, h_give, wires))
    hidden[1].step(h_keep)
    grads, before = [], None
    for k, group in enumerate(split):
        if k == 0:
            drb_now = after(drb, h_keep, hidden[1].ready, norm_sum.ready)
        elif k == 1:
            norm_sum.step(before)
            projection[1].step(before)
            drb_now = after(drb, before, projection[1].ready, norm_sum.ready)
        else:
            norm_sum.step(before)
            hidden[1].step(before)
            projection[1].step(before)
            drb_now = after(drb, before, hidden[1].ready, projection[1].ready, norm_sum.ready)
        saved, probs = outs[k][1:]
        grads.append(
            attention_grad(
                meta, 0, group, drb_now, drb_other, out_weight, saved, probs, pe, rev, w_pairs, tables, before, k == 2
            )
        )
        before = grads[-1][2]
    dx_mine, dx_theirs = grads[-1][2:]
    dx_got = wires.to_core(dx_theirs)
    dqkv, dpos = [g[0] for g in grads], [g[1] for g in grads]
    dpos = [jnp.concatenate(dpos, axis=0)]
    dpos_other = [wires.to_core(d) for d in dpos]
    hidden[0].step(before)
    projection[1].step(before)
    now = after(meta, dx_mine, hidden[0].ready, projection[1].ready)
    packed = projection_grad(now, 0, xb, xb_other, dqkv, o_own, o_other, drb, drb_other, dpos, dpos_other, rel_table, qkv_weight)
    projection[0] = Flow(projection_flow(*packed, wires))
    d_input = wires.turn((dr + dx_mine + after(dx_got, packed).astype(F32)).astype(BF)).astype(F32)
    grad_norms = norm_sum.finish(packed)[:, None]
    parts = [flow.finish(packed) for flow in projection]
    hidden = [flow.finish(packed) for flow in hidden]
    grad_qkv = jnp.stack([jnp.stack(part[:3]) for part in parts])
    grad_out = jnp.stack([part[3] for part in parts])
    grad_rel = jnp.stack([part[4] for part in parts])
    grad_in = jnp.stack([item[0] for item in hidden])
    grad_down = jnp.stack([item[1] for item in hidden])
    return (output[None], d_input[None], grad_qkv, grad_out, grad_rel, grad_in, grad_down, grad_norms)


def solution(mesh):
    placed = (
        P(("rows", "col"), "seq", None),
        P(("rows", "col"), None),
        P(),
        P(),
        P(),
        P(None, None, "col"),
        P(None, None, "col"),
        P(),
        P(("rows", "col"), "seq", None),
    )
    return jax.shard_map(
        per_device,
        mesh=mesh,
        in_specs=placed,
        out_specs=(
            P(("rows", "col"), "seq", None),
            P(("rows", "col"), "seq", None),
            P(None, None, ("seq", "rows"), "col"),
            P(None, ("seq", "rows"), "col"),
            P(None, ("seq", "rows"), "col"),
            P(None, ("seq", "rows"), "col"),
            P(None, ("seq", "rows"), "col"),
            P(None, "col", ("seq", "rows")),
        ),
        check_vma=False,
    )
```

```python
import functools

import jax
import jax.numpy as jnp
import numpy as np
from jax import lax
from jax.experimental import pallas as pl
from jax.experimental.pallas import tpu as pltpu
from jax.sharding import PartitionSpec as P

HEAD_DIM = 64
SPAN = 256
MAX_REL = 512
WIDE = 640
HALF = 320
EPSILON = 1e-07
SCALE = (3.0 * HEAD_DIM) ** (-0.5)
LOG2E = 1.4426950408889634
BF = jnp.bfloat16
F32 = jnp.float32
NT = (((1,), (1,)), ((), ()))
NN = (((1,), (0,)), ((), ()))
TN = (((0,), (0,)), ((), ()))
VMEM_LIMIT = 56 << 20
NORM_ROWS = 16


def dot(a, b, dims=NN):
    return lax.dot_general(a, b, dims, preferred_element_type=F32)


def bucket_table():
    relative = HALF - np.arange(WIDE)
    middle = SPAN // 2
    absolute = np.where((relative < middle) & (relative > -middle), middle - 1, np.abs(relative))
    log_position = np.ceil(np.log(absolute / middle) / np.log((MAX_REL - 1) / middle) * (middle - 1)) + middle
    bucket = np.where(absolute <= middle, relative, log_position * np.sign(relative))
    bucket = np.clip(bucket + SPAN, 0, 2 * SPAN - 1).astype(np.int32)
    return (bucket[:, None] == np.arange(2 * SPAN)[None, :]).astype(np.float32)


def assemble(target, own, other, core, count):
    target[pl.ds(pl.multiple_of(core * count, count), count), :] = own[...]
    target[pl.ds(pl.multiple_of((1 - core) * count, count), count), :] = other[...]


def half_of(head):
    lane = lax.broadcasted_iota(jnp.int32, (1, 128), 1)
    return (lane < HEAD_DIM) if head == 0 else (lane >= HEAD_DIM)


def doc_number(position, meta_ref):
    total = jnp.zeros(position.shape, jnp.int32)
    for k in range(3):
        total = total + (position >= meta_ref[k]).astype(jnp.int32)
    return total


def skew(values, base):
    return pltpu.roll(values, base % WIDE, 1, stride=1, stride_axis=0)


def rolled(values):
    return pltpu.roll(values.astype(F32), HEAD_DIM, 1).astype(values.dtype)


def cost(microseconds):
    return pl.CostEstimate(flops=int(microseconds * 1e8), bytes_accessed=1 << 20, transcendentals=0)


def whole_block(*shape):
    return pl.BlockSpec(shape, lambda g, m: (0,) * len(shape))


def prepare_kernel(meta_ref, first_ref, second_ref, rel_ref, table_ref, w_ref, pe_ref):
    first = meta_ref[0] == 0
    low = half_of(0)

    @pl.when(pl.program_id(0) != 1)
    def _():
        for c in range(3):
            w_ref[0, 0, :, 128 * c : 128 * (c + 1)] = first_ref[0, c]

    @pl.when(pl.program_id(0) == 1)
    def _():
        for c in range(3):
            a, b = first_ref[0, c], second_ref[0, c]
            zero = jnp.where(low, a, rolled(b))
            one = jnp.where(low, rolled(a), b)
            w_ref[0, 0, :, 128 * c : 128 * (c + 1)] = jnp.where(first, zero, one)

    pos = dot(rel_ref[0], w_ref[0, 0, :, :256]).astype(BF)
    ext = dot(table_ref[0], pos).astype(BF)
    pe_ref[0, 0, 0] = ext[:, :128]
    pe_ref[0, 0, 1] = ext[:, 128:]
    pe_ref[0, 0, 2] = dot(table_ref[1], pos[:, 128:]).astype(BF)


def prepare(core, layer, qkv_weight, rel_table, tables):
    kinds, model = qkv_weight.shape[1:3]
    pairs, buckets = 3, rel_table.shape[1]
    return pl.pallas_call(
        prepare_kernel,
        out_shape=(
            jax.ShapeDtypeStruct((1, pairs, model, 384), BF),
            jax.ShapeDtypeStruct((1, pairs, 3, WIDE, 128), BF),
        ),
        grid_spec=pltpu.PrefetchScalarGridSpec(
            num_scalar_prefetch=1,
            grid=(pairs,),
            in_specs=[
                pl.BlockSpec(
                    (1, kinds, model, 128),
                    lambda g, m: (layer, 0, 0, jnp.where(g == 1, 1, jnp.where(g == 0, 0, 3) + 2 * m[0])),
                ),
                pl.BlockSpec((1, kinds, model, 128), lambda g, m: (layer, 0, 0, 4)),
                pl.BlockSpec((1, buckets, model), lambda g, m: (layer, 0, 0)),
                whole_block(2, WIDE, buckets),
            ],
            out_specs=(
                pl.BlockSpec((1, 1, model, 384), lambda g, m: (0, g, 0, 0)),
                pl.BlockSpec((1, 1, 3, WIDE, 128), lambda g, m: (0, g, 0, 0, 0)),
            ),
        ),
        compiler_params=pltpu.CompilerParams(vmem_limit_bytes=VMEM_LIMIT),
        cost_estimate=cost(5),
        name="prepare",
    )(core[None], qkv_weight, qkv_weight, rel_table, tables)


def attention_kernel(
    meta_ref, own_ref, other_ref, w_ref, pe_ref, rev_ref, o_ref, sv_ref, p_hbm,
    x_ref, s_ref, t1_ref, t2_ref, bt_ref, sb_ref, pp_ref, pj_ref, sems, *, length, blk, pairs,
):
    assemble(x_ref, own_ref, other_ref, meta_ref[3], length // 2)
    zero = jnp.zeros((), BF)
    ids_j = doc_number(lax.broadcasted_iota(jnp.int32, (1, length), 1), meta_ref)
    blocks = [slice(b, b + blk) for b in range(0, length, blk)]
    copies = []

    def project(p):
        for sl in blocks:
            qkv = dot(x_ref[sl, :], w_ref[0, p]).astype(BF)
            sb_ref[p, sl, :] = qkv
            sv_ref[p, sl, :128] = qkv[:, :128]

    def reverse(p):
        for sl in blocks:
            sv_ref[p, sl, 128:] = dot(rev_ref[sl, :], sb_ref[p, :, 128:]).astype(BF)

    def key_positions(h):
        for sl in blocks:
            kb = jnp.where(half_of(h % 2), sb_ref[h // 2, sl, 128:256], zero)
            t2_ref[h % 2, sl, :] = dot(kb, pe_ref[0, h // 2, 0], NT)

    def key_skew(h):
        for sl in blocks:
            t2 = skew(t2_ref[h % 2, sl, :], sl.start + HALF)[:, :length].astype(BF)
            bt_ref[h % 2, :, sl] = t2.T

    def products(h):
        for sl in blocks:
            qb = jnp.where(half_of(h % 2), sb_ref[h // 2, sl, :128], zero)
            t1_ref[h % 2, sl, :] = dot(qb, pe_ref[0, h // 2, 1], NT)
            s_ref[h % 2, sl, :] = dot(qb, sb_ref[h // 2, :, 128:256], NT)

    def softmax(h):
        for sl in blocks:
            t1 = skew(t1_ref[h % 2, sl, :], sl.start + HALF)[:, :length]
            total = s_ref[h % 2, sl, :] + t1 + bt_ref[h % 2, sl, :].astype(F32)
            ids_i = doc_number(lax.broadcasted_iota(jnp.int32, (blk, 1), 0) + sl.start, meta_ref)
            total = jnp.where(ids_i == ids_j, total, -1e30)
            e = jnp.exp2((total - jnp.max(total, axis=1, keepdims=True)) * (SCALE * LOG2E))
            pp_ref[h % 2, sl, :] = (e * (1.0 / jnp.sum(e, axis=1, keepdims=True))).astype(BF)

    def outputs(h):
        lanes = slice(128 * (h // 2), 128 * (h // 2 + 1))
        for sl in blocks:
            o = dot(pp_ref[h % 2, sl, :], sb_ref[h // 2, :, 256:]).astype(BF)
            o_ref[sl, lanes] = o if h % 2 == 0 else jnp.where(half_of(1), o, o_ref[sl, lanes])
        if h >= 2:
            copies[h - 2].wait()
        for sl in blocks:
            pj_ref[h % 2, sl, :] = dot(pp_ref[h % 2, sl, :], rev_ref[...]).astype(BF)
        copies.append(pltpu.make_async_copy(pj_ref.at[h % 2], p_hbm.at[h], sems.at[h % 2]))
        copies[h].start()

    project(0)
    key_positions(0)
    for h in range(2 * pairs):
        products(h)
        if h > 0:
            outputs(h - 1)
        else:
            reverse(0)
        key_skew(h)
        if h + 1 < 2 * pairs:
            if h % 2 == 1:
                project((h + 1) // 2)
            key_positions(h + 1)
            if h % 2 == 1:
                reverse((h + 1) // 2)
        softmax(h)
    outputs(2 * pairs - 1)
    copies[-2].wait()
    copies[-1].wait()


def attention(meta, layer, group, own, other, w, pe, rev):
    base, pairs = group
    base //= pairs
    count, model = own.shape
    length = 2 * count
    return pl.pallas_call(
        functools.partial(attention_kernel, length=length, blk=256, pairs=pairs),
        out_shape=(
            jax.ShapeDtypeStruct((length, pairs * 128), BF),
            jax.ShapeDtypeStruct((pairs, length, 384), BF),
            jax.ShapeDtypeStruct((2 * pairs, length, length), BF),
        ),
        grid_spec=pltpu.PrefetchScalarGridSpec(
            num_scalar_prefetch=1,
            grid=(1,),
            in_specs=[
                whole_block(count, model),
                whole_block(count, model),
                pl.BlockSpec((1, pairs, model, 384), lambda g, m: (0, base, 0, 0)),
                pl.BlockSpec((1, pairs, 2, WIDE, 128), lambda g, m: (0, base, 0, 0, 0)),
                whole_block(length, length),
            ],
            out_specs=(
                whole_block(length, pairs * 128),
                whole_block(pairs, length, 384),
                pl.BlockSpec(memory_space=pl.ANY),
            ),
            scratch_shapes=[
                pltpu.VMEM((length, model), BF),
                pltpu.VMEM((2, length, length), F32),
                pltpu.VMEM((2, length, WIDE), F32),
                pltpu.VMEM((2, length, WIDE), F32),
                pltpu.VMEM((2, length, length), BF),
                pltpu.VMEM((pairs, length, 384), BF),
                pltpu.VMEM((2, length, length), BF),
                pltpu.VMEM((2, length, length), BF),
                pltpu.SemaphoreType.DMA((2,)),
            ],
        ),
        compiler_params=pltpu.CompilerParams(vmem_limit_bytes=VMEM_LIMIT),
        cost_estimate=cost(5 * pairs),
        name="attention",
    )(meta, own, other, w, pe, rev)


def head_rows(core):
    return ((256 * core, 128), (128 + 64 * core, 64), (512 + 64 * core, 64), (384 + 256 * core, 128))


def attention_grad_kernel(
    meta_ref, own_ref, other_ref, wo_ref, pe_ref, rev_ref, w_ref, table_ref, *rest,
    length, blk, base, sizes, first, last,
):
    pairs = sum(sizes)
    sv = [ref.at[k] for ref, size in zip(rest, sizes) for k in range(size)]
    p_hbm = [ref.at[k] for ref, size in zip(rest[len(sizes) :], sizes) for k in range(2 * size)]
    rest = rest[2 * len(sizes) :]
    if not first:
        before_ref, *rest = rest
    dqkv_ref, dpos_ref, *rest = rest
    if last:
        mine_ref, theirs_ref, *rest = rest
    else:
        sum_ref, *rest = rest
    drb_ref, do_ref, p_ref, da_ref, ds_ref, dt_ref, u_ref, v_ref, acc_ref, dx_ref, heads_ref, sems = rest
    copies = [pltpu.make_async_copy(p_hbm[h], p_ref.at[h], sems.at[h]) for h in range(2 * pairs)]
    for item in copies:
        item.start()
    core = meta_ref[3]
    count = length // 2
    assemble(drb_ref, own_ref, other_ref, core, count)
    at = 0
    for start, size in head_rows(core):
        heads_ref[at : at + size] = wo_ref[0, pl.ds(pl.multiple_of(start, 64), size), :]
        at += size
    zero = jnp.zeros((), BF)
    pad = jnp.zeros((blk, WIDE - length), F32)
    blocks = [slice(b, b + blk) for b in range(0, length, blk)]
    half = lambda h: slice(HEAD_DIM * (h % 2), HEAD_DIM * (h % 2 + 1))

    def attended(p):
        rows = slice(128 * (base + p), 128 * (base + p + 1))
        for sl in blocks:
            do_ref[p, sl, :] = dot(drb_ref[sl, :], heads_ref[rows, :], NT).astype(BF)

    def probabilities(h):
        for sl in blocks:
            d_o = jnp.where(half_of(h % 2), do_ref[h // 2, sl, :], zero)
            da_ref[h % 2, sl, :] = dot(d_o, sv[h // 2][:, 256:], NT)

    def scores(h):
        copies[h].wait()
        for sl in blocks:
            da = da_ref[h % 2, sl, :]
            p = p_ref[h, sl, :].astype(F32)
            ds = (p * (da - jnp.sum(p * da, axis=1, keepdims=True))).astype(BF)
            ds_ref[h % 2, sl, :] = ds
            dt_ref[h % 2, :, sl] = ds.T

    def query_skew(h):
        for sl in blocks:
            wide = jnp.concatenate([ds_ref[h % 2, sl, :].astype(F32), pad], axis=1)
            u_ref[h % 2, sl, :] = skew(wide, sl.start + WIDE - 192).astype(BF)

    def key_skew(h):
        for sl in blocks:
            wide = jnp.concatenate([dt_ref[h % 2, sl, :].astype(F32), pad], axis=1)
            v_ref[h % 2, sl, :] = skew(wide, sl.start + WIDE - 191).astype(BF)

    def add_to(p, sl, lanes, h, value):
        acc_ref[p % 2, sl, lanes] = value if h % 2 == 0 else acc_ref[p % 2, sl, lanes] + value

    def values(h):
        p = h // 2
        d_o = jnp.where(half_of(h % 2), do_ref[p], zero)
        add_to(p, slice(0, length), slice(256, 384), h, dot(p_ref[h], d_o, TN))

    def queries(h):
        p, own = h // 2, half_of(h % 2)
        kr = jnp.where(own, sv[p][:, 128:256], zero)
        pk = jnp.where(own, pe_ref[0, p, 2], zero)
        for sl in blocks:
            add_to(p, sl, slice(0, 128), h, dot(ds_ref[h % 2, sl, :], kr) + dot(u_ref[h % 2, sl, :], pk))
        d_ext = (dot(sv[p][:, :128].T[half(h)], u_ref[h % 2]) * SCALE).astype(BF)
        dpos_ref[p, 1, half(h), :] = dot(d_ext, table_ref[1]).astype(BF)

    def keys(h):
        p, own = h // 2, half_of(h % 2)
        q = jnp.where(own, sv[p][:, :128], zero)
        pq = jnp.where(own, pe_ref[0, p, 0], zero)
        for sl in blocks:
            add_to(p, sl, slice(128, 256), h, dot(dt_ref[h % 2, sl, :], q) + dot(v_ref[h % 2, sl, :], pq))
        d_ext = (dot(sv[p][:, 128:256].T[half(h)], v_ref[h % 2]) * SCALE).astype(BF)
        dpos_ref[p, 0, half(h), :] = dot(d_ext, table_ref[0]).astype(BF)

    def inputs(p):
        acc = acc_ref[p % 2]
        dqkv_ref[p, :, :128] = (acc[:, :128] * SCALE).astype(BF)
        dkv = jnp.concatenate([(acc[:, 128:256] * SCALE).astype(BF), acc[:, 256:].astype(BF)], axis=1)
        for sl in blocks:
            dqkv_ref[p, sl, 128:] = dot(rev_ref[sl, :], dkv).astype(BF)
        for sl in blocks:
            part = dot(dqkv_ref[p, sl, :], w_ref[0, p], NT)
            if p > 0:
                part = part + dx_ref[sl, :]
            elif not first:
                part = part + before_ref[sl, :]
            dx_ref[sl, :] = part

    total = 2 * pairs
    attended(0)
    probabilities(0)
    for h in range(total):
        scores(h)
        if h + 1 < total:
            if h % 2 == 1:
                attended((h + 1) // 2)
            probabilities(h + 1)
        values(h)
        query_skew(h)
        if h > 0:
            keys(h - 1)
            if h % 2 == 0:
                inputs(h // 2 - 1)
        key_skew(h)
        queries(h)
    keys(total - 1)
    inputs(pairs - 1)
    if last:
        mine_ref[...] = dx_ref[pl.ds(pl.multiple_of(core * count, count), count), :]
        theirs_ref[...] = dx_ref[pl.ds(pl.multiple_of((1 - core) * count, count), count), :].astype(BF)
    else:
        sum_ref[...] = dx_ref[...]


def attention_grad(meta, layer, group, own, other, wo, saved, probs, pe, rev, w, tables, before, last):
    base, pairs = group
    at = base // pairs
    buckets = tables.shape[2]
    count, model = own.shape
    length = 2 * count
    if last:
        sums = [jax.ShapeDtypeStruct((count, model), F32), jax.ShapeDtypeStruct((count, model), BF)]
    else:
        sums = [jax.ShapeDtypeStruct((length, model), F32)]
    sizes = tuple(item.shape[0] for item in saved)
    extra = [] if before is None else [before]
    return pl.pallas_call(
        functools.partial(
            attention_grad_kernel, length=length, blk=256, base=base, sizes=sizes, first=before is None, last=last
        ),
        out_shape=[
            jax.ShapeDtypeStruct((pairs, length, 384), BF),
            jax.ShapeDtypeStruct((pairs, 2, 128, buckets), BF),
        ] + sums,
        grid_spec=pltpu.PrefetchScalarGridSpec(
            num_scalar_prefetch=1,
            grid=(1,),
            in_specs=[
                whole_block(count, model),
                whole_block(count, model),
                pl.BlockSpec((1, model, model), lambda g, m: (layer, 0, 0)),
                pl.BlockSpec((1, pairs, 3, WIDE, 128), lambda g, m: (0, at, 0, 0, 0)),
                whole_block(length, length),
                pl.BlockSpec((1, pairs, model, 384), lambda g, m: (0, at, 0, 0)),
                whole_block(2, WIDE, buckets),
            ]
            + [whole_block(*item.shape) for item in saved]
            + [pl.BlockSpec(memory_space=pl.ANY)] * len(probs)
            + [whole_block(length, model)] * len(extra),
            out_specs=[whole_block(pairs, length, 384), whole_block(pairs, 2, 128, buckets)]
            + [whole_block(*item.shape) for item in sums],
            scratch_shapes=[
                pltpu.VMEM((length, model), BF),
                pltpu.VMEM((pairs, length, 128), BF),
                pltpu.VMEM((2 * pairs, length, length), BF),
                pltpu.VMEM((2, length, length), F32),
                pltpu.VMEM((2, length, length), BF),
                pltpu.VMEM((2, length, length), BF),
                pltpu.VMEM((2, length, WIDE), BF),
                pltpu.VMEM((2, length, WIDE), BF),
                pltpu.VMEM((2, length, 384), F32),
                pltpu.VMEM((length, model), F32),
                pltpu.VMEM((model // 2, model), BF),
                pltpu.SemaphoreType.DMA((2 * pairs,)),
            ],
        ),
        compiler_params=pltpu.CompilerParams(vmem_limit_bytes=VMEM_LIMIT),
        cost_estimate=cost(6 * pairs),
        name="attention_grad",
    )(meta, own, other, wo, pe, rev, w, tables, *saved, *probs, *extra)


def pieces_kernel(meta_ref, in_ref, down_ref, in_piece, down_piece):
    in_piece[...] = in_ref[0]
    down_piece[...] = down_ref[0]


def weight_pieces(seq, layer, ffn_in, ffn_out):
    model, hidden = ffn_in.shape[1:]
    rows = model // 2
    steps = 4
    return pl.pallas_call(
        pieces_kernel,
        out_shape=[jax.ShapeDtypeStruct((rows, hidden), BF)] * 2,
        grid_spec=pltpu.PrefetchScalarGridSpec(
            num_scalar_prefetch=1,
            grid=(steps,),
            in_specs=[pl.BlockSpec((1, rows // steps, hidden), lambda g, m: (layer, steps * m[0] + g, 0))] * 2,
            out_specs=[pl.BlockSpec((rows // steps, hidden), lambda g, m: (g, 0))] * 2,
        ),
        cost_estimate=cost(1),
        name="weight_pieces",
    )(seq[None], ffn_in, ffn_out)


def weight_copies(layer, refs, scratch, sems, meta_ref):
    shards = []
    for s in range(4):
        group = []
        for m in range(2):
            own, core_own, near, far, core_near, core_far = refs[m]
            place = scratch.at[m, s]
            if s < 2:
                group.append(((own if s == 0 else core_own).at[layer], place))
            else:
                first, second = (near, far) if s == 2 else (core_near, core_far)
                rows = first.shape[0]
                one = pl.multiple_of(meta_ref[4] * rows, rows)
                two = pl.multiple_of((1 - meta_ref[4]) * rows, rows)
                group.append((first, place.at[pl.ds(one, rows)]))
                group.append((second, place.at[pl.ds(two, rows)]))
        shards.append(group)
    copies, k = [], 0
    for group in shards:
        made = []
        for source, target in group:
            made.append(pltpu.make_async_copy(source, target, sems.at[k]))
            k += 1
        copies.append(made)
    return copies


COPIES = 12


def row_norm(state, gain, bias):
    centered = state - jnp.mean(state, axis=1, keepdims=True)
    inverse = lax.rsqrt(jnp.mean(centered * centered, axis=1, keepdims=True) + EPSILON)
    return centered * inverse * gain + bias


def row_norm_grad(state, gain, d_result):
    centered = state - jnp.mean(state, axis=1, keepdims=True)
    inverse = lax.rsqrt(jnp.mean(centered * centered, axis=1, keepdims=True) + EPSILON)
    unit = centered * inverse
    d_unit = d_result * gain
    d_state = inverse * (
        d_unit
        - jnp.mean(d_unit, axis=1, keepdims=True)
        - unit * jnp.mean(d_unit * unit, axis=1, keepdims=True)
    )
    return d_state, jnp.sum(d_result * unit, axis=0, keepdims=True), jnp.sum(d_result, axis=0, keepdims=True)


def tokens_kernel(meta_ref, *rest, layer, chunk, groups):
    o_refs, rest = rest[: 2 * groups], rest[2 * groups :]
    x_ref, wo_ref, norm_ref, *rest = rest
    wires, rest = rest[:12], rest[12:]
    y_ref, yb_ref, mb_ref, resid_ref, pre_ref, slope_ref, scratch, sems, heads = rest
    copies = weight_copies(layer, (wires[:6], wires[6:]), scratch, sems, meta_ref)
    for group in copies:
        for item in group:
            item.start()
    at = 0
    for core in (meta_ref[3], 1 - meta_ref[3]):
        for first, size in head_rows(core):
            heads[at : at + size] = wo_ref[0, pl.ds(pl.multiple_of(first, 64), size), :]
            at += size
    resid = x_ref[...].astype(F32) + dot(jnp.concatenate([o[...] for o in o_refs], axis=1), heads[...])
    resid_ref[...] = resid
    middle = row_norm(resid, norm_ref[0:1, :], norm_ref[1:2, :])
    mb = middle.astype(BF)
    mb_ref[...] = mb
    pre_ref[...] = middle
    hidden = scratch.shape[3]
    per = hidden // chunk
    total = 4 * per

    def up(k):
        s, c = k // per, k % per
        if c == 0:
            for item in copies[s]:
                item.wait()
        return dot(mb, scratch[0, s, :, c * chunk : (c + 1) * chunk])

    ahead = up(0)
    for k in range(total):
        s, c = k // per, k % per
        h = ahead
        if k + 1 < total:
            ahead = up(k + 1)
        cumulative = 0.5 * (1.0 + lax.erf(h * 0.7071067811865476))
        density = jnp.exp(-0.5 * h * h) * 0.3989422804014327
        slope_ref[:, k * chunk : (k + 1) * chunk] = (cumulative + h * density).astype(BF)
        act = (h * cumulative).astype(BF)
        pre_ref[...] = pre_ref[...] + dot(act, scratch[1, s, :, c * chunk : (c + 1) * chunk], NT)
    y = row_norm(pre_ref[...], norm_ref[2:3, :], norm_ref[3:4, :])
    y_ref[...] = y
    yb_ref[...] = y.astype(BF)


def token_step(meta, layer, o_own, o_other, x, wo, norms, wires):
    count, model = x.shape
    hidden = wires[0].shape[2]
    mine = [pl.BlockSpec((count, o.shape[1]), lambda g, m: (m[3], 0)) for o in o_own + o_other]
    hbm = pl.BlockSpec(memory_space=pl.ANY)
    return pl.pallas_call(
        functools.partial(tokens_kernel, layer=layer, chunk=768, groups=len(o_own)),
        out_shape=(
            jax.ShapeDtypeStruct((count, model), F32),
            jax.ShapeDtypeStruct((count, model), BF),
            jax.ShapeDtypeStruct((count, model), BF),
            jax.ShapeDtypeStruct((count, model), F32),
            jax.ShapeDtypeStruct((count, model), F32),
            jax.ShapeDtypeStruct((count, 4 * hidden), BF),
        ),
        grid_spec=pltpu.PrefetchScalarGridSpec(
            num_scalar_prefetch=1,
            grid=(1,),
            in_specs=mine + [
                whole_block(count, model),
                pl.BlockSpec((1, model, model), lambda g, m: (layer, 0, 0)),
                whole_block(4, model),
            ] + [hbm] * 12,
            out_specs=(
                whole_block(count, model), whole_block(count, model), whole_block(count, model), whole_block(count, model), whole_block(count, model),
                whole_block(count, 4 * hidden),
            ),
            scratch_shapes=[
                pltpu.VMEM((2, 4, model, hidden), BF),
                pltpu.SemaphoreType.DMA((COPIES,)),
                pltpu.VMEM((model, model), BF),
            ],
        ),
        compiler_params=pltpu.CompilerParams(vmem_limit_bytes=VMEM_LIMIT),
        cost_estimate=cost(10),
        name="token_step",
    )(meta, *o_own, *o_other, x, wo, norms, *wires)


def tokens_grad_kernel(meta_ref, *rest, layer, chunk, parts):
    ups, rest = rest[:parts], rest[parts:]
    pre_ref, resid_ref, slope_ref, norm_ref, *rest = rest
    wires, rest = rest[:12], rest[12:]
    df_ref, dr_ref, drb_ref, scratch, sems, dm_ref, dn_ref = rest
    count = dm_ref.shape[0]
    copies = weight_copies(layer, (wires[:6], wires[6:]), scratch, sems, meta_ref)
    for group in copies:
        for item in group:
            item.start()
    dy = ups[0][...].astype(F32)
    for item in ups[1:]:
        dy = dy + item[...].astype(F32)
    dz, dg2, db2 = row_norm_grad(pre_ref[...], norm_ref[2:3, :], dy)
    df = dz.astype(BF)
    df_ref[:count, :] = df
    dm_ref[...] = dz
    hidden = scratch.shape[3]
    per = hidden // chunk
    total = 4 * per

    def down(k):
        s, c = k // per, k % per
        if c == 0:
            for item in copies[s]:
                item.wait()
        return dot(df, scratch[1, s, :, c * chunk : (c + 1) * chunk])

    ahead = down(0)
    for k in range(total):
        s, c = k // per, k % per
        dg = ahead
        if k + 1 < total:
            ahead = down(k + 1)
        dh = (dg * slope_ref[:, k * chunk : (k + 1) * chunk].astype(F32)).astype(BF)
        dm_ref[...] = dm_ref[...] + dot(dh, scratch[0, s, :, c * chunk : (c + 1) * chunk], NT)
    dr, dg1, db1 = row_norm_grad(resid_ref[...], norm_ref[0:1, :], dm_ref[...])
    dr_ref[...] = dr
    drb_ref[...] = dr.astype(BF)
    dn_ref[...] = jnp.zeros_like(dn_ref)
    for k, row in enumerate((dg1, db1, dg2, db2)):
        high = row.astype(BF)
        dn_ref[k : k + 1, :] = high.astype(F32)
        dn_ref[4 + k : 5 + k, :] = row - high.astype(F32)
    df_ref[count:, :] = dn_ref[...].astype(BF)


def token_grad(meta, layer, ups, pre, resid, slope, norms, wires):
    count, model = pre.shape
    hidden = wires[0].shape[2]
    hbm = pl.BlockSpec(memory_space=pl.ANY)
    return pl.pallas_call(
        functools.partial(tokens_grad_kernel, layer=layer, chunk=768, parts=len(ups)),
        out_shape=(
            jax.ShapeDtypeStruct((count + NORM_ROWS, model), BF),
            jax.ShapeDtypeStruct((count, model), F32),
            jax.ShapeDtypeStruct((count, model), BF),
        ),
        grid_spec=pltpu.PrefetchScalarGridSpec(
            num_scalar_prefetch=1,
            grid=(1,),
            in_specs=[whole_block(count, model)] * len(ups)
            + [whole_block(count, model), whole_block(count, model), whole_block(count, 4 * hidden), whole_block(4, model)]
            + [hbm] * 12,
            out_specs=(whole_block(count + NORM_ROWS, model), whole_block(count, model), whole_block(count, model)),
            scratch_shapes=[
                pltpu.VMEM((2, 4, model, hidden), BF),
                pltpu.SemaphoreType.DMA((COPIES,)),
                pltpu.VMEM((count, model), F32),
                pltpu.VMEM((NORM_ROWS, model), F32),
            ],
        ),
        compiler_params=pltpu.CompilerParams(vmem_limit_bytes=VMEM_LIMIT),
        cost_estimate=cost(10),
        name="token_grad",
    )(meta, *ups, pre, resid, slope, norms, *wires)


def hidden_grad_kernel(meta_ref, *refs):
    m_refs, d_refs = refs[:4], refs[4:8]
    wi_ref, wd_ref, keep_ref, give_ref, down_ref, m_ref, d_ref, mt_ref, dt_ref = refs[8:]
    per = keep_ref.shape[1]
    chunk = wi_ref.shape[2]

    @pl.when(pl.program_id(0) == 0)
    def _():
        for sources, target, transposed in ((m_refs, m_ref, mt_ref), (d_refs, d_ref, dt_ref)):
            for k, source in enumerate(sources):
                count = m_refs[0].shape[0]
                target[k * count : (k + 1) * count, :] = source[:count, :]
                transposed[:, k * count : (k + 1) * count] = source[:count, :].T

    kind = 2 * meta_ref[5] + meta_ref[3]
    count = m_refs[0].shape[0]
    rows = jnp.zeros((NORM_ROWS, d_refs[0].shape[1]), F32)
    for source in d_refs:
        rows = rows + source[count:, :].astype(F32)
    number = lax.broadcasted_iota(jnp.int32, rows.shape, 0)
    norm = jnp.sum(jnp.where((number == kind) | (number == kind + 4), rows, 0.0), axis=0, keepdims=True)
    high = norm.astype(BF).astype(F32)
    norm = jnp.where(lax.broadcasted_iota(jnp.int32, rows.shape, 0) == 0, high, norm - high).astype(BF)

    h = dot(m_ref[...], wi_ref[0])
    cumulative = 0.5 * (1.0 + lax.erf(h * 0.7071067811865476))
    density = jnp.exp(-0.5 * h * h) * 0.3989422804014327
    act = (h * cumulative).astype(BF)
    dh = (dot(d_ref[...], wd_ref[0]) * (cumulative + h * density)).astype(BF)
    half = mt_ref.shape[0] // 2
    for s in range(2):
        here = meta_ref[4] == s
        part = slice(s * half, (s + 1) * half)
        gi = dot(mt_ref[part, :], dh).astype(BF)
        gd = dot(dt_ref[part, :], act).astype(BF)
        for n in range(half // per):
            rows = slice(n * per, (n + 1) * per)
            down_ref[s, n, :per, :] = gd[rows]
            at = s * half + n * per
            piece = jnp.concatenate([norm[:, at : at + per], jnp.zeros((NORM_ROWS, 128 - per), BF)], axis=1)
            down_ref[s, n, per:, :] = jnp.concatenate([piece] * (chunk // 128), axis=1)

        @pl.when(here)
        def _():
            for n in range(half // per):
                keep_ref[n] = gi[n * per : (n + 1) * per]

        @pl.when(jnp.logical_not(here))
        def _():
            for n in range(half // per):
                give_ref[n] = gi[n * per : (n + 1) * per]


def hidden_grad(meta, layer, rows, d_rows, w_in, w_down):
    count, model = rows[0].shape
    hidden = w_in.shape[2]
    chunk = 256
    shape = (4, model // 8, hidden)
    down = (2, 4, model // 8 + NORM_ROWS, hidden)
    return pl.pallas_call(
        hidden_grad_kernel,
        out_shape=[jax.ShapeDtypeStruct(shape, BF)] * 2 + [jax.ShapeDtypeStruct(down, BF)],
        grid_spec=pltpu.PrefetchScalarGridSpec(
            num_scalar_prefetch=1,
            grid=(hidden // chunk,),
            in_specs=[whole_block(*a.shape) for a in (*rows, *d_rows)] + [
                pl.BlockSpec((1, model, chunk), lambda g, m: (layer, 0, g)),
                pl.BlockSpec((1, model, chunk), lambda g, m: (layer, 0, g)),
            ],
            out_specs=[pl.BlockSpec(shape[:2] + (chunk,), lambda g, m: (0, 0, g))] * 2
            + [pl.BlockSpec(down[:3] + (chunk,), lambda g, m: (0, 0, 0, g))],
            scratch_shapes=[pltpu.VMEM((4 * count, model), BF)] * 2 + [pltpu.VMEM((model, 4 * count), BF)] * 2,
        ),
        compiler_params=pltpu.CompilerParams(vmem_limit_bytes=VMEM_LIMIT),
        cost_estimate=cost(10),
        name="hidden_grad",
    )(meta, *rows, *d_rows, w_in, w_down)


def projection_grad_kernel(
    meta_ref, x_own_ref, x_other_ref, d_own_ref, d_other_ref, *rest, length, chunks, pairs, groups, grads,
):
    lists = []
    for size in (groups, groups, grads[0], grads[1], grads[1]):
        lists.append(rest[:size])
        rest = rest[size:]
    o_own = [o.at[:, 128 * k : 128 * (k + 1)] for o in lists[0] for k in range(o.shape[1] // 128)]
    o_other = [o.at[:, 128 * k : 128 * (k + 1)] for o in lists[1] for k in range(o.shape[1] // 128)]
    dqkv, dpos, dpos_other = ([r.at[k] for r in part for k in range(r.shape[0])] for part in lists[2:])
    rel_ref, wq_ref, wk_ref, a_keep, a_give, b_keep, b_give, *rest = rest
    x_ref, d_ref, left_ref, out_ref, right_ref, pos_ref, w_ref = rest
    core = meta_ref[3]
    seq = meta_ref[4]
    y_own = meta_ref[5]
    count = length // 2
    model = x_ref.shape[1]
    buckets = rel_ref.shape[1]
    low = half_of(0)
    zero = jnp.zeros((), BF)
    assemble(x_ref, x_own_ref, x_other_ref, core, count)
    assemble(d_ref, d_own_ref, d_other_ref, core, count)
    left_ref[:, :length] = x_ref[...].T
    left_ref[:, length:] = rel_ref[0].T
    for place, o, dp in ((core, o_own, dpos), (1 - core, o_other, dpos_other)):
        at = 0
        for first, size in head_rows(place):
            rows = pl.ds(pl.multiple_of(first, 64), size)
            p, inner = at // 128, at % 128
            if inner == 0:
                o_t = o[p][...].T
            out_ref[rows, :] = o_t[inner : inner + size]
            for c in range(2):
                pos_ref[c, rows, :] = dp[p][c, inner : inner + size, :]
            at += size
    per = model // chunks
    first_core = core == 0
    half_chunks = chunks // 2
    tile = lambda c, p: dqkv[p][:, 128 * c : 128 * (c + 1)]
    own_pos = [[dpos[p][c].astype(F32).T.astype(BF) for p in range(pairs)] for c in range(2)]
    at = 0
    for first, size in head_rows(core):
        rows = pl.ds(pl.multiple_of(first, 64), size)
        w_ref[0, at : at + size, :] = wq_ref[0, 0, rows, :]
        w_ref[1, at : at + size, :] = wk_ref[0, 0, rows, :]
        at += size
    back = (dot(w_ref[0], pos_ref[0]) + dot(w_ref[1], pos_ref[1])).T
    share = buckets // chunks
    for y in range(2):
        full = 0 if y == 0 else 2
        if y == 0:
            mixed = lambda q, k: jnp.where(low, q, rolled(k))
            v_mix = jnp.where(low, tile(2, 1), zero)
        else:
            mixed = lambda q, k: jnp.where(low, rolled(q), k)
            v_mix = jnp.where(low, rolled(tile(2, 1)), zero)
        right_ref[:length, 0:128] = tile(0, full)
        right_ref[:length, 128:256] = tile(1, full)
        right_ref[:length, 256:384] = mixed(tile(0, 1), tile(1, 1))
        right_ref[length:, 0:128] = own_pos[0][full]
        right_ref[length:, 128:256] = own_pos[1][full]
        right_ref[length:, 256:384] = mixed(own_pos[0][1], own_pos[1][1])
        base = 384 * y
        t0, t1, t2 = (d_ref[:, base + 128 * k : base + 128 * (k + 1)] for k in range(3))
        of = jnp.where(first_core, t0, t2)
        om = jnp.where(low, zero, jnp.where(first_core, rolled(t1), t1))
        one = dot(left_ref[...], right_ref[...])
        two = dot(left_ref[:, :length], jnp.concatenate([tile(2, full), v_mix], axis=1))
        three = dot(out_ref[...], jnp.concatenate([om, of], axis=1))
        rel_full = back[:, 128 * full : 128 * (full + 1)]
        rel_rest = back[:, 128:256] if y == 0 else pltpu.roll(back[:, 128:256], HEAD_DIM, 1)

        def store_a(ref, n, keep):
            rows = slice(n * per, (n + 1) * per)
            ref[keep, :per, :] = one[rows].astype(BF)
            for k in range(3):
                part = slice(n * share + 16 * k, n * share + 16 * (k + 1))
                ref[keep, per:, 128 * k : 128 * (k + 1)] = rel_full[part].astype(BF)

        def store_b(ref, n, keep):
            rows = slice(n * per, (n + 1) * per)
            ref[keep, :per, 0:128] = two[rows, :128].astype(BF)
            ref[keep, :per, 128:256] = (two[rows, 128:] + three[rows, :128]).astype(BF)
            ref[keep, :per, 256:384] = three[rows, 128:].astype(BF)
            ref[keep, per:, 0:128] = rel_full[n * share + 48 : (n + 1) * share].astype(BF)
            for k in range(2):
                a = rel_rest[n * share + 32 * k : n * share + 32 * k + 16]
                b = rel_rest[n * share + 32 * k + 16 : n * share + 32 * k + 32]
                ref[keep, per:, 128 * (k + 1) : 128 * (k + 2)] = jnp.where(low, a, pltpu.roll(b, HEAD_DIM, 1)).astype(BF)

        @pl.when(y_own == y)
        def _():
            for n in range(chunks):
                store_a(a_keep, n, n)

        @pl.when(y_own != y)
        def _():
            for n in range(chunks):
                store_a(a_give, n, n)

        for s in range(2):
            @pl.when(seq == s)
            def _():
                for n in range(chunks):
                    kept = n // half_chunks == s
                    store_b((b_keep if kept else b_give).at[y], n, n % half_chunks)


def projection_grad(meta, layer, x_own, x_other, dqkv, o_own, o_other, d_own, d_other, dpos, dpos_other, rel, qkv_weight):
    count, model = x_own.shape
    length = 2 * count
    buckets = rel.shape[1]
    chunks = 8
    rows = model // chunks + 16
    args = (x_own, x_other, d_own, d_other, *o_own, *o_other, *dqkv, *dpos, *dpos_other)
    return pl.pallas_call(
        functools.partial(
            projection_grad_kernel, length=length, chunks=chunks, pairs=3, groups=len(o_own), grads=(len(dqkv), len(dpos))
        ),
        out_shape=[jax.ShapeDtypeStruct((chunks, rows, model // 2), BF)] * 2
        + [jax.ShapeDtypeStruct((2, chunks // 2, rows, model // 2), BF)] * 2,
        grid_spec=pltpu.PrefetchScalarGridSpec(
            num_scalar_prefetch=1,
            grid=(1,),
            in_specs=[whole_block(*a.shape) for a in args]
            + [
                pl.BlockSpec((1, buckets, model), lambda g, m: (layer, 0, 0)),
                pl.BlockSpec((1, 1, model, model), lambda g, m: (layer, 0, 0, 0)),
                pl.BlockSpec((1, 1, model, model), lambda g, m: (layer, 1, 0, 0)),
            ],
            out_specs=[whole_block(chunks, rows, model // 2)] * 2 + [whole_block(2, chunks // 2, rows, model // 2)] * 2,
            scratch_shapes=[
                pltpu.VMEM((length, model), BF),
                pltpu.VMEM((length, model), BF),
                pltpu.VMEM((model, length + buckets), BF),
                pltpu.VMEM((model, length), BF),
                pltpu.VMEM((length + buckets, 384), BF),
                pltpu.VMEM((2, model, buckets), BF),
                pltpu.VMEM((2, 384, model), BF),
            ],
        ),
        compiler_params=pltpu.CompilerParams(vmem_limit_bytes=VMEM_LIMIT),
        cost_estimate=cost(10),
        name="projection_grad",
    )(meta, *args, rel, qkv_weight, qkv_weight)


class Wires:
    def __init__(self):
        self.seqs, self.rows, self.cols = (lax.axis_size(name) for name in ("seq", "rows", "col"))
        self.seq, self.row, self.col = (lax.axis_index(name) for name in ("seq", "rows", "col"))
        self.core, self.y = self.col % 2, self.col // 2

    def send(self, array, target):
        pairs = []
        for s in range(self.seqs):
            for r in range(self.rows):
                for c in range(self.cols):
                    t = target(s, r, c)
                    pairs.append(((s * self.rows + r) * self.cols + c, (t[0] * self.rows + t[1]) * self.cols + t[2]))
        return lax.ppermute(array, ("seq", "rows", "col"), pairs)

    def turn(self, array):
        return self.send(array, lambda s, r, c: (c % 2, r, c - c % 2 + s))

    def to_core(self, array):
        return self.send(array, lambda s, r, c: (s, r, c ^ 1))

    def to_y(self, array):
        return self.send(array, lambda s, r, c: (s, r, c ^ 2))

    def to_seq(self, array):
        return self.send(array, lambda s, r, c: (1 - s, r, c))

    def to_row(self, array, bit):
        return self.send(array, lambda s, r, c: (s, r ^ (1 << bit), c))


def cut(array, axis, mine):
    shape = array.shape
    pairs = array.reshape(shape[:axis] + (shape[axis] // 2, 2) + shape[axis + 1 :])
    return pick(pairs, axis + 1, mine), pick(pairs, axis + 1, 1 - mine)


def bits_of(count):
    return count.bit_length() - 1


def add(a, b):
    return (a.astype(F32) + b.astype(F32)).astype(a.dtype)


def pick(array, axis, index):
    return lax.dynamic_index_in_dim(array, index, axis, keepdims=False)


def unpack(main, rel, wires):
    t = [main[:, 128 * k : 128 * (k + 1)] for k in range(6)]
    full = [t[0], t[1], t[3], t[5], rel[:, :128]]
    rest = [t[2][:, :64], t[2][:, 64:], t[4][:, :64], t[4][:, 64:], rel[:, 128:]]
    out = []
    for f, r in zip(full, rest):
        out.append(jnp.where(wires.core == 0, jnp.concatenate([f, r], 1), jnp.concatenate([r, f], 1)).astype(F32))
    return out


def after(arrays, *earlier):
    return lax.optimization_barrier((arrays, earlier))[0]


def finer(parts, wires):
    for bit in reversed(range(bits_of(wires.rows) - 2)):
        mine = (wires.row >> bit) & 1
        sums = []
        for v in parts:
            v = v.reshape((2, v.shape[0] // 2) + v.shape[1:])
            sums.append(add(pick(v, 0, mine), wires.to_row(pick(v, 0, 1 - mine), bit)))
        parts = sums
    return parts


def first_flow(keep, give, wires):
    got = yield [(wires.to_seq, give)]
    total = add(keep, got[0])
    low = bits_of(wires.rows) - 2
    for bit in (low, low + 1):
        keep, give = cut(total, 0, (wires.row >> bit) & 1)
        got = yield [(functools.partial(wires.to_row, bit=bit), give)]
        total = add(keep, got[0])
    return finer([total[0]], wires)[0].astype(F32)


def second_flow(total, wires):
    low = bits_of(wires.rows) - 2
    for bit in (low, low + 1):
        keep, give = cut(total, 1, (wires.row >> bit) & 1)
        got = yield [(functools.partial(wires.to_row, bit=bit), give)]
        total = add(keep, got[0])
    total = total[:, 0]
    got = yield [(wires.to_seq, pick(total, 0, 1 - wires.seq))]
    total = add(pick(total, 0, wires.seq), got[0])
    per = total.shape[0] - NORM_ROWS
    down, norm = finer([total[:per], total[per : per + 2, :per].T], wires)
    norm = norm.astype(F32)
    return down.astype(F32), norm[:, 0] + norm[:, 1]


def projection_flow(a_keep, a_give, b_keep, b_give, wires):
    got = yield [(wires.to_y, a_give), (wires.to_seq, b_give)]
    a = add(a_keep, got[0]).reshape((2, 4) + a_keep.shape[1:])
    b = add(b_keep, got[1])
    got = yield [(wires.to_seq, pick(a, 0, 1 - wires.seq)), (wires.to_y, pick(b, 0, 1 - wires.y))]
    both = jnp.stack([add(pick(a, 0, wires.seq), got[0]), add(pick(b, 0, wires.y), got[1])])
    low = bits_of(wires.rows) - 2
    for bit in (low, low + 1):
        keep, give = cut(both, 1, (wires.row >> bit) & 1)
        got = yield [(functools.partial(wires.to_row, bit=bit), give)]
        both = add(keep, got[0])
    both = both[:, 0]
    main = jnp.concatenate([both[0, :-16], both[1, :-16]], axis=1)
    tail = jnp.concatenate([both[0, -16:], both[1, -16:]], axis=1)
    full = jnp.concatenate([tail[:, 128 * k : 128 * (k + 1)] for k in range(4)], axis=0)
    rest = jnp.concatenate([tail[:, 512 + 64 * k : 576 + 64 * k] for k in range(4)], axis=0)
    rel = jnp.concatenate([full, rest], axis=1)
    main, rel = finer([main, rel], wires)
    return unpack(main, rel, wires)


class Flow:
    def __init__(self, steps):
        self.steps, self.value = steps, None
        self.take(next(steps))

    def take(self, sends):
        self.ready = [array for _, array in sends]
        self.under_way = [send(array) for send, array in sends]

    def step(self, *earlier):
        if self.under_way is None:
            return
        arrived = after(self.under_way, earlier) if earlier else self.under_way
        try:
            self.take(self.steps.send(arrived))
        except StopIteration as stop:
            self.ready, self.under_way, self.value = stop.value, None, stop.value

    def finish(self, *earlier):
        while self.under_way is not None:
            self.step(*earlier)
        return self.value


def gather_start(rows, wires):
    return rows, wires.to_core(rows), wires.to_y(rows)


def gather_end(gathered, wires, *earlier):
    rows, other, far = gathered
    return rows, other, far, wires.to_core(after(far, earlier))


def per_device(tokens, lengths, qkv_weight, out_weight, rel_table, ffn_in, ffn_out, norm_params, cotangent):
    wires = Wires()
    core = wires.core
    count, model = tokens.shape[1:]
    length = 2 * count
    layers = qkv_weight.shape[0]
    table_np = bucket_table()
    tables = jnp.asarray(np.stack([table_np, table_np[::-1]]), BF)
    rev = jnp.asarray(np.eye(length)[::-1], BF)
    split = [(0, 2), (2, 1)]

    weights = (ffn_in, ffn_out)
    near, far, core_near, core_far = ([[None, None], [None, None]] for _ in range(4))
    core_own = [None, None]
    start = wires.turn(tokens[0])
    other_lengths = wires.to_core(lengths)
    pieces = [weight_pieces(wires.seq, 0, ffn_in, ffn_out), None]
    done = (pieces[0], start, other_lengths)
    lengths = jnp.where(core == wires.seq, lengths, after(other_lengths, done))
    ends = jnp.cumsum(lengths[0]).astype(jnp.int32)
    meta = jnp.concatenate([ends[:3], jnp.stack([core, wires.seq, wires.y])]).astype(jnp.int32)
    xb = start
    near[0] = [wires.to_y(after(piece, done)) for piece in pieces[0]]
    xb_other = wires.to_core(after(start, done))
    core_own[0] = wires.to_core(after(ffn_in, done))

    prepared = [prepare(after(core, done, meta), 0, qkv_weight, rel_table, tables), None]
    pieces[1] = weight_pieces(after(wires.seq, prepared[0]), 1, ffn_in, ffn_out)
    done = (pieces[1], near[0][0], xb_other, core_own[0])
    far[0][0] = wires.to_seq(after(near[0][0], done))
    core_near[0][0] = wires.to_core(after(near[0][0], done))
    core_own[1] = wires.to_core(after(ffn_out, done))
    near[1][0] = wires.to_y(after(pieces[1][0], done))

    w_pairs, pe = prepared[0]
    outs = []

    def attend(group, *arrived):
        outs.append(attention(meta, 0, group, after(xb, arrived), xb_other, w_pairs, pe, rev))

    attend(split[0], done)
    done = (outs[0], far[0][0], core_near[0][0], core_own[1], near[0][1])
    far[0][1] = wires.to_seq(after(near[0][1], done))
    core_near[0][1] = wires.to_core(after(near[0][1], done))
    core_far[0][0] = wires.to_core(after(far[0][0], done))
    near[1][1] = wires.to_y(after(pieces[1][1], done))
    attend(split[1], done)
    o_own = [jnp.concatenate([item[0] for item in outs], axis=1)]
    done = (o_own, core_near[0][1], core_far[0][0], near[1][0])
    o_other = [wires.to_core(after(item, done)) for item in o_own]
    core_near[1][0] = wires.to_core(after(near[1][0], done))
    far[1][0] = wires.to_seq(after(near[1][0], done))
    prepared[1] = prepare(after(core, done), 1, qkv_weight, rel_table, tables)
    done = (prepared[1], far[0][1], o_other, core_near[1][0])
    core_far[0][1] = wires.to_core(after(far[0][1], done))

    def wire_args(n):
        return [
            item for m in range(2)
            for item in (weights[m], core_own[m], near[n][m], far[n][m], core_near[n][m], core_far[n][m])
        ]

    x = after(start, done)
    y, yb, mb, resid, pre, slope = token_step(meta, 0, o_own, o_other, x, out_weight, norm_params[0], wire_args(0))
    kept = [(xb, xb_other, outs, o_own, o_other, resid, pre, slope, mb)]

    done = (yb, far[1][0], near[1][1])
    xb, xb_other = yb, wires.to_core(after(yb, done))
    core_far[1][0] = wires.to_core(after(far[1][0], done))
    far[1][1] = wires.to_seq(after(near[1][1], done))
    core_near[1][1] = wires.to_core(after(near[1][1], done))
    w_pairs, pe = prepared[1]
    outs = [attention(meta, 1, (0, 3), after(xb, done, xb_other), xb_other, w_pairs, pe, rev)]
    o_own = [outs[0][0]]
    done = (o_own, far[1][1], core_far[1][0], core_near[1][1])
    o_other = [wires.to_core(after(item, done)) for item in o_own]
    core_far[1][1] = wires.to_core(after(far[1][1], done))
    d_final = wires.turn(after(cotangent[0], done))
    x = after(y, done, o_other, core_far[1][1])
    y, yb, mb, resid, pre, slope = token_step(meta, 1, o_own, o_other, x, out_weight, norm_params[1], wire_args(1))
    kept.append((xb, xb_other, outs, o_own, o_other, resid, pre, slope, mb))
    done = (y, d_final)
    output = wires.turn(after(y, done))
    m_rows = [gather_start(after(kept[0][-1], done), wires), gather_start(after(mb, done), wires)]

    xb, xb_other, outs, o_own, o_other, resid, pre, slope, mb = kept[1]
    w_pairs, pe = prepared[1]
    df, dr, drb = token_grad(meta, 1, [after(d_final, m_rows[1][0])], pre, resid, slope, norm_params[1], wire_args(1))
    done = (df, m_rows[1][2], m_rows[1][1])
    drb_other = wires.to_core(after(drb, done))
    d_rows = [None, gather_start(after(df, done), wires)]
    m_rows[1] = gather_end(m_rows[1], wires, done)
    done = (done, drb_other, output)
    saved, probs = ([item[k] for item in outs] for k in (1, 2))
    dqkv, dpos, dx_mine, dx_theirs = attention_grad(
        meta, 1, (0, 3), after(drb, done), drb_other, out_weight, saved, probs, pe, rev, w_pairs, tables, None, True
    )
    done = (dx_mine, d_rows[1][2], d_rows[1][1], m_rows[1][3], m_rows[0][2], m_rows[0][1])
    d_rows[1] = gather_end(d_rows[1], wires, done)
    dx_got = wires.to_core(after(dx_theirs, done))
    dpos_other = wires.to_core(after(dpos, done))
    m_rows[0] = gather_end(m_rows[0], wires, done)
    keep, give, down = hidden_grad(after(meta, done), 1, m_rows[1], d_rows[1], ffn_in, ffn_out)
    done = (down, m_rows[0][3], dpos_other, dx_got)
    first = [None, Flow(first_flow(keep, after(give, done), wires))]
    second = [None, Flow(second_flow(after(down, done), wires))]
    projection = [None, None]
    projection_args = (xb, xb_other, [dqkv], o_own, o_other, drb, drb_other, [dpos], [dpos_other], rel_table, qkv_weight)

    xb, xb_other, outs, o_own, o_other, resid, pre, slope, mb = kept[0]
    w_pairs, pe = prepared[0]
    ups = [after(dr, done, second[1].ready), dx_mine, dx_got]
    df, dr, drb = token_grad(meta, 0, ups, pre, resid, slope, norm_params[0], wire_args(0))
    done = (df,)
    d_rows[0] = gather_start(after(df, done), wires)
    drb_other = wires.to_core(after(drb, done))
    packed = projection_grad(after(meta, done), 1, *projection_args)
    done = (packed, d_rows[0][2], d_rows[0][1], drb_other, first[1].under_way, second[1].under_way)
    d_rows[0] = gather_end(d_rows[0], wires, done)
    projection[1] = Flow(projection_flow(*after(packed, done), wires))
    first[1].step(done)
    second[1].step(done, first[1].ready)
    keep, give, down = hidden_grad(after(meta, done, second[1].ready), 0, m_rows[0], d_rows[0], ffn_in, ffn_out)
    done = (down, projection[1].under_way, first[1].under_way)
    projection[1].step(done)
    first[0] = Flow(first_flow(keep, after(give, done, projection[1].ready), wires))
    second[0] = Flow(second_flow(after(down, done), wires))
    done = (done, projection[1].ready, second[0].ready)
    saved, probs = ([item[k] for item in outs] for k in (1, 2))
    dqkv, dpos, dx_mine, dx_theirs = attention_grad(
        meta, 0, (0, 3), after(drb, done), drb_other, out_weight, saved, probs, pe, rev, w_pairs, tables, None, True
    )
    done = (dx_mine, projection[1].under_way, first[0].under_way, second[0].under_way, second[1].under_way)
    dpos_other = wires.to_core(after(dpos, done))
    projection[1].step(done)
    first[1].step(done)
    first[0].step(done, projection[1].ready)
    second[1].step(done)
    now = after(meta, done, projection[1].ready, first[0].ready, first[1].ready, second[1].ready)
    packed = projection_grad(
        now, 0, xb, xb_other, [dqkv], o_own, o_other, drb, drb_other, [dpos], [dpos_other], rel_table, qkv_weight
    )
    done = (packed, projection[1].under_way, first[0].under_way, first[1].under_way, second[1].under_way)
    projection[0] = Flow(projection_flow(*after(packed, done), wires))
    projection[1].step(done, projection[0].ready)
    first[0].step(done, projection[1].ready)
    second[0].step(done, first[0].ready)
    first[1].finish(second[0].ready)
    second[1].finish(second[0].ready)
    done = (projection[0].under_way, second[0].ready)
    projection[0].step(done)
    dx_got = wires.to_core(after(dx_theirs, projection[0].ready))
    d_input = wires.turn((dr + dx_mine + dx_got.astype(F32)).astype(BF)).astype(F32)
    done = (projection[0].under_way, projection[1].under_way, first[0].under_way)
    projection[0].step(done)
    projection[1].finish(projection[0].ready)
    first[0].finish(projection[0].ready)
    done = (projection[0].under_way, second[0].under_way)
    projection[0].step(done)
    second[0].step(projection[0].ready)
    parts = [flow.finish() for flow in projection]
    first, second = ([flow.finish() for flow in flows] for flows in (first, second))
    grad_qkv = jnp.stack([jnp.stack(part[:3]) for part in parts])
    grad_out = jnp.stack([part[3] for part in parts])
    grad_rel = jnp.stack([part[4] for part in parts])
    grad_in = jnp.stack(first)
    grad_down, grad_norms = (jnp.stack([item[k] for item in second]) for k in range(2))
    return (output[None], d_input[None], grad_qkv, grad_out, grad_rel, grad_in, grad_down, grad_norms[:, None])


def solution(mesh):
    placed = (
        P(("rows", "col"), "seq", None),
        P(("rows", "col"), None),
        P(),
        P(),
        P(),
        P(None, None, "col"),
        P(None, None, "col"),
        P(),
        P(("rows", "col"), "seq", None),
    )
    return jax.shard_map(
        per_device,
        mesh=mesh,
        in_specs=placed,
        out_specs=(
            P(("rows", "col"), "seq", None),
            P(("rows", "col"), "seq", None),
            P(None, None, ("seq", "rows"), "col"),
            P(None, ("seq", "rows"), "col"),
            P(None, ("seq", "rows"), "col"),
            P(None, ("seq", "rows"), "col"),
            P(None, ("seq", "rows"), "col"),
            P(None, "col", ("seq", "rows")),
        ),
        check_vma=False,
    )
```

```python
import functools

import jax
import jax.numpy as jnp
import numpy as np
from jax import lax
from jax.experimental import pallas as pl
from jax.experimental.pallas import tpu as pltpu
from jax.sharding import PartitionSpec as P

HEAD_DIM = 64
SPAN = 256
MAX_REL = 512
WIDE = 640
HALF = 320
EPSILON = 1e-07
SCALE = (3.0 * HEAD_DIM) ** (-0.5)
LOG2E = 1.4426950408889634
BF = jnp.bfloat16
F32 = jnp.float32
NT = (((1,), (1,)), ((), ()))
NN = (((1,), (0,)), ((), ()))
TN = (((0,), (0,)), ((), ()))
VMEM_LIMIT = 56 << 20
NORM_ROWS = 16


def dot(a, b, dims=NN):
    return lax.dot_general(a, b, dims, preferred_element_type=F32)


def bucket_table():
    relative = HALF - np.arange(WIDE)
    middle = SPAN // 2
    absolute = np.where((relative < middle) & (relative > -middle), middle - 1, np.abs(relative))
    log_position = np.ceil(np.log(absolute / middle) / np.log((MAX_REL - 1) / middle) * (middle - 1)) + middle
    bucket = np.where(absolute <= middle, relative, log_position * np.sign(relative))
    bucket = np.clip(bucket + SPAN, 0, 2 * SPAN - 1).astype(np.int32)
    return (bucket[:, None] == np.arange(2 * SPAN)[None, :]).astype(np.float32)


def assemble(target, own, other, core, count):
    target[pl.ds(pl.multiple_of(core * count, count), count), :] = own[...]
    target[pl.ds(pl.multiple_of((1 - core) * count, count), count), :] = other[...]


class Late:
    def __init__(self, source, target, sem):
        self.target, self.copy = target, pltpu.make_async_copy(source, target, sem)
        self.copy.start()

    def get(self):
        if self.copy is not None:
            self.copy.wait()
            self.copy = None
        return self.target


class Loads:
    def __init__(self, sems):
        self.sems, self.count = sems, 0

    def __call__(self, source, target):
        self.count += 1
        return Late(source, target, self.sems.at[self.count - 1])


def rows_at(number, count):
    return pl.ds(pl.multiple_of(number * count, count), count)


def half_of(head):
    lane = lax.broadcasted_iota(jnp.int32, (1, 128), 1)
    return (lane < HEAD_DIM) if head == 0 else (lane >= HEAD_DIM)


def doc_number(position, meta_ref):
    total = jnp.zeros(position.shape, jnp.int32)
    for k in range(3):
        total = total + (position >= meta_ref[k]).astype(jnp.int32)
    return total


def skew(values, base):
    return pltpu.roll(values, base % WIDE, 1, stride=1, stride_axis=0)


def rolled(values):
    return pltpu.roll(values.astype(F32), HEAD_DIM, 1).astype(values.dtype)


def cost(microseconds):
    return pl.CostEstimate(flops=int(microseconds * 1e8), bytes_accessed=1 << 20, transcendentals=0)


def whole_block(*shape):
    return pl.BlockSpec(shape, lambda g, m: (0,) * len(shape))


def prepare_kernel(meta_ref, first_ref, second_ref, rel_ref, table_ref, *rest):
    if len(rest) > 2:
        in_ref, down_ref, w_ref, pe_ref, in_piece, down_piece = rest
        in_piece[...] = in_ref[0]
        down_piece[...] = down_ref[0]
    else:
        w_ref, pe_ref = rest
    first = meta_ref[0] == 0
    low = half_of(0)

    @pl.when(pl.program_id(0) != 1)
    def _():
        for c in range(3):
            w_ref[0, 0, :, 128 * c : 128 * (c + 1)] = first_ref[0, c]

    @pl.when(pl.program_id(0) == 1)
    def _():
        for c in range(3):
            a, b = first_ref[0, c], second_ref[0, c]
            zero = jnp.where(low, a, rolled(b))
            one = jnp.where(low, rolled(a), b)
            w_ref[0, 0, :, 128 * c : 128 * (c + 1)] = jnp.where(first, zero, one)

    pos = dot(rel_ref[0], w_ref[0, 0, :, :256]).astype(BF)
    ext = dot(table_ref[0], pos).astype(BF)
    pe_ref[0, 0, 0] = ext[:, :128]
    pe_ref[0, 0, 1] = ext[:, 128:]
    pe_ref[0, 0, 2] = dot(table_ref[1], pos[:, 128:]).astype(BF)


def prepare(place, layer, qkv_weight, rel_table, tables, ffn=()):
    hidden = ffn[0].shape[2] if ffn else 0
    rows = qkv_weight.shape[2] // 2
    kinds, model = qkv_weight.shape[1:3]
    pairs, buckets = 3, rel_table.shape[1]
    return pl.pallas_call(
        prepare_kernel,
        out_shape=(
            jax.ShapeDtypeStruct((1, pairs, model, 384), BF),
            jax.ShapeDtypeStruct((1, pairs, 3, WIDE, 128), BF),
        ) + (jax.ShapeDtypeStruct((rows, hidden), BF),) * len(ffn),
        grid_spec=pltpu.PrefetchScalarGridSpec(
            num_scalar_prefetch=1,
            grid=(pairs,),
            in_specs=[
                pl.BlockSpec(
                    (1, kinds, model, 128),
                    lambda g, m: (layer, 0, 0, jnp.where(g == 1, 1, jnp.where(g == 0, 0, 3) + 2 * m[0])),
                ),
                pl.BlockSpec((1, kinds, model, 128), lambda g, m: (layer, 0, 0, 4)),
                pl.BlockSpec((1, buckets, model), lambda g, m: (layer, 0, 0)),
                whole_block(2, WIDE, buckets),
            ] + [pl.BlockSpec((1, rows // pairs, hidden), lambda g, m: (layer + 1, pairs * m[1] + g, 0))] * len(ffn),
            out_specs=(
                pl.BlockSpec((1, 1, model, 384), lambda g, m: (0, g, 0, 0)),
                pl.BlockSpec((1, 1, 3, WIDE, 128), lambda g, m: (0, g, 0, 0, 0)),
            ) + (pl.BlockSpec((rows // pairs, hidden), lambda g, m: (g, 0)),) * len(ffn),
        ),
        compiler_params=pltpu.CompilerParams(vmem_limit_bytes=VMEM_LIMIT),
        cost_estimate=cost(5),
        name="prepare",
    )(place, qkv_weight, qkv_weight, rel_table, tables, *ffn)


def attention_kernel(
    meta_ref, own_ref, other_ref, w_ref, pe_ref, rev_ref, o_ref, sv_ref, p_hbm,
    x_ref, s_ref, t1_ref, t2_ref, bt_ref, sb_ref, pp_ref, pj_ref, sems, *, length, blk, pairs,
):
    assemble(x_ref, own_ref, other_ref, meta_ref[3], length // 2)
    zero = jnp.zeros((), BF)
    ids_j = doc_number(lax.broadcasted_iota(jnp.int32, (1, length), 1), meta_ref)
    blocks = [slice(b, b + blk) for b in range(0, length, blk)]
    copies = []

    def project(p):
        for sl in blocks:
            qkv = dot(x_ref[sl, :], w_ref[0, p]).astype(BF)
            sb_ref[p, sl, :] = qkv
            sv_ref[p, sl, :128] = qkv[:, :128]

    def reverse(p):
        for sl in blocks:
            sv_ref[p, sl, 128:] = dot(rev_ref[sl, :], sb_ref[p, :, 128:]).astype(BF)

    def key_positions(h):
        for sl in blocks:
            kb = jnp.where(half_of(h % 2), sb_ref[h // 2, sl, 128:256], zero)
            t2_ref[h % 2, sl, :] = dot(kb, pe_ref[0, h // 2, 0], NT)

    def key_skew(h):
        for sl in blocks:
            t2 = skew(t2_ref[h % 2, sl, :], sl.start + HALF)[:, :length].astype(BF)
            bt_ref[h % 2, :, sl] = t2.T

    def products(h):
        for sl in blocks:
            qb = jnp.where(half_of(h % 2), sb_ref[h // 2, sl, :128], zero)
            t1_ref[h % 2, sl, :] = dot(qb, pe_ref[0, h // 2, 1], NT)
            s_ref[h % 2, sl, :] = dot(qb, sb_ref[h // 2, :, 128:256], NT)

    def softmax(h):
        for sl in blocks:
            t1 = skew(t1_ref[h % 2, sl, :], sl.start + HALF)[:, :length]
            total = s_ref[h % 2, sl, :] + t1 + bt_ref[h % 2, sl, :].astype(F32)
            ids_i = doc_number(lax.broadcasted_iota(jnp.int32, (blk, 1), 0) + sl.start, meta_ref)
            total = jnp.where(ids_i == ids_j, total, -1e30)
            e = jnp.exp2((total - jnp.max(total, axis=1, keepdims=True)) * (SCALE * LOG2E))
            pp_ref[h % 2, sl, :] = (e * (1.0 / jnp.sum(e, axis=1, keepdims=True))).astype(BF)

    def outputs(h):
        lanes = slice(128 * (h // 2), 128 * (h // 2 + 1))
        for sl in blocks:
            o = dot(pp_ref[h % 2, sl, :], sb_ref[h // 2, :, 256:]).astype(BF)
            o_ref[sl, lanes] = o if h % 2 == 0 else jnp.where(half_of(1), o, o_ref[sl, lanes])
        if h >= 2:
            copies[h - 2].wait()
        for sl in blocks:
            pj_ref[h % 2, sl, :] = dot(pp_ref[h % 2, sl, :], rev_ref[...]).astype(BF)
        copies.append(pltpu.make_async_copy(pj_ref.at[h % 2], p_hbm.at[h], sems.at[h % 2]))
        copies[h].start()

    project(0)
    key_positions(0)
    for h in range(2 * pairs):
        products(h)
        if h > 0:
            outputs(h - 1)
        else:
            reverse(0)
        key_skew(h)
        if h + 1 < 2 * pairs:
            if h % 2 == 1:
                project((h + 1) // 2)
            key_positions(h + 1)
            if h % 2 == 1:
                reverse((h + 1) // 2)
        softmax(h)
    outputs(2 * pairs - 1)
    copies[-2].wait()
    copies[-1].wait()


def attention(meta, layer, group, own, other, w, pe, rev):
    base, pairs = group
    base //= pairs
    count, model = own.shape
    length = 2 * count
    return pl.pallas_call(
        functools.partial(attention_kernel, length=length, blk=256, pairs=pairs),
        out_shape=(
            jax.ShapeDtypeStruct((length, pairs * 128), BF),
            jax.ShapeDtypeStruct((pairs, length, 384), BF),
            jax.ShapeDtypeStruct((2 * pairs, length, length), BF),
        ),
        grid_spec=pltpu.PrefetchScalarGridSpec(
            num_scalar_prefetch=1,
            grid=(1,),
            in_specs=[
                whole_block(count, model),
                whole_block(count, model),
                pl.BlockSpec((1, pairs, model, 384), lambda g, m: (0, base, 0, 0)),
                pl.BlockSpec((1, pairs, 2, WIDE, 128), lambda g, m: (0, base, 0, 0, 0)),
                whole_block(length, length),
            ],
            out_specs=(
                whole_block(length, pairs * 128),
                whole_block(pairs, length, 384),
                pl.BlockSpec(memory_space=pl.ANY),
            ),
            scratch_shapes=[
                pltpu.VMEM((length, model), BF),
                pltpu.VMEM((2, length, length), F32),
                pltpu.VMEM((2, length, WIDE), F32),
                pltpu.VMEM((2, length, WIDE), F32),
                pltpu.VMEM((2, length, length), BF),
                pltpu.VMEM((pairs, length, 384), BF),
                pltpu.VMEM((2, length, length), BF),
                pltpu.VMEM((2, length, length), BF),
                pltpu.SemaphoreType.DMA((2,)),
            ],
        ),
        compiler_params=pltpu.CompilerParams(vmem_limit_bytes=VMEM_LIMIT),
        cost_estimate=cost(5 * pairs),
        name="attention",
    )(meta, own, other, w, pe, rev)


def head_rows(core):
    return ((256 * core, 128), (128 + 64 * core, 64), (512 + 64 * core, 64), (384 + 256 * core, 128))


def attention_grad_kernel(
    meta_ref, own_hbm, other_hbm, wo_hbm, pe_hbm, rev_hbm, w_hbm, table_hbm, *rest, layer, length, blk, base, sizes,
):
    pairs = sum(sizes)
    sv_hbm = [ref.at[k] for ref, size in zip(rest, sizes) for k in range(size)]
    p_hbm = [ref.at[k] for ref, size in zip(rest[len(sizes) :], sizes) for k in range(2 * size)]
    dqkv_ref, dpos_ref, mine_ref, theirs_ref, *rest = rest[2 * len(sizes) :]
    drb_ref, do_ref, p_ref, da_ref, ds_ref, dt_ref, u_ref, v_ref, acc_ref, dx_ref, heads_ref, *rest = rest
    sv_ref, pe_ref, rev_ref, w_ref, table_ref, loads = rest
    core = meta_ref[3]
    count = length // 2
    load = Loads(loads)
    rows = [load(own_hbm, drb_ref.at[rows_at(core, count)]), load(other_hbm, drb_ref.at[rows_at(1 - core, count)])]
    at = 0
    for start, size in head_rows(core):
        place = pl.ds(pl.multiple_of(start, 64), size)
        rows.append(load(wo_hbm.at[layer, place], heads_ref.at[pl.ds(at, size)]))
        at += size
    saved, probs = [], []
    for p in range(pairs):
        saved.append(load(sv_hbm[p], sv_ref.at[p]))
        probs += [load(p_hbm[2 * p + k], p_ref.at[2 * p + k]) for k in range(2)]
        if p == 0:
            pe = load(pe_hbm.at[0, pl.ds(base, pairs)], pe_ref)
            tables = load(table_hbm, table_ref)
            rev = load(rev_hbm, rev_ref)
            w = load(w_hbm.at[0, pl.ds(base, pairs)], w_ref)
    for item in rows:
        item.get()
    sv = [sv_ref.at[p] for p in range(pairs)]
    zero = jnp.zeros((), BF)
    pad = jnp.zeros((blk, WIDE - length), F32)
    blocks = [slice(b, b + blk) for b in range(0, length, blk)]
    half = lambda h: slice(HEAD_DIM * (h % 2), HEAD_DIM * (h % 2 + 1))

    def attended(p):
        rows = slice(128 * (base + p), 128 * (base + p + 1))
        for sl in blocks:
            do_ref[p, sl, :] = dot(drb_ref[sl, :], heads_ref[rows, :], NT).astype(BF)

    def probabilities(h):
        saved[h // 2].get()
        for sl in blocks:
            d_o = jnp.where(half_of(h % 2), do_ref[h // 2, sl, :], zero)
            da_ref[h % 2, sl, :] = dot(d_o, sv[h // 2][:, 256:], NT)

    def scores(h):
        probs[h].get()
        for sl in blocks:
            da = da_ref[h % 2, sl, :]
            p = p_ref[h, sl, :].astype(F32)
            ds = (p * (da - jnp.sum(p * da, axis=1, keepdims=True))).astype(BF)
            ds_ref[h % 2, sl, :] = ds
            dt_ref[h % 2, :, sl] = ds.T

    def query_skew(h):
        for sl in blocks:
            wide = jnp.concatenate([ds_ref[h % 2, sl, :].astype(F32), pad], axis=1)
            u_ref[h % 2, sl, :] = skew(wide, sl.start + WIDE - 192).astype(BF)

    def key_skew(h):
        for sl in blocks:
            wide = jnp.concatenate([dt_ref[h % 2, sl, :].astype(F32), pad], axis=1)
            v_ref[h % 2, sl, :] = skew(wide, sl.start + WIDE - 191).astype(BF)

    def add_to(p, sl, lanes, h, value):
        acc_ref[p % 2, sl, lanes] = value if h % 2 == 0 else acc_ref[p % 2, sl, lanes] + value

    def values(h):
        p = h // 2
        d_o = jnp.where(half_of(h % 2), do_ref[p], zero)
        add_to(p, slice(0, length), slice(256, 384), h, dot(p_ref[h], d_o, TN))

    def queries(h):
        pe.get()
        tables.get()
        p, own = h // 2, half_of(h % 2)
        kr = jnp.where(own, sv[p][:, 128:256], zero)
        pk = jnp.where(own, pe_ref[p, 2], zero)
        for sl in blocks:
            add_to(p, sl, slice(0, 128), h, dot(ds_ref[h % 2, sl, :], kr) + dot(u_ref[h % 2, sl, :], pk))
        d_ext = (dot(sv[p][:, :128].T[half(h)], u_ref[h % 2]) * SCALE).astype(BF)
        dpos_ref[p, 1, half(h), :] = dot(d_ext, table_ref[1]).astype(BF)

    def keys(h):
        p, own = h // 2, half_of(h % 2)
        q = jnp.where(own, sv[p][:, :128], zero)
        pq = jnp.where(own, pe_ref[p, 0], zero)
        for sl in blocks:
            add_to(p, sl, slice(128, 256), h, dot(dt_ref[h % 2, sl, :], q) + dot(v_ref[h % 2, sl, :], pq))
        d_ext = (dot(sv[p][:, 128:256].T[half(h)], v_ref[h % 2]) * SCALE).astype(BF)
        dpos_ref[p, 0, half(h), :] = dot(d_ext, table_ref[0]).astype(BF)

    def inputs(p):
        rev.get()
        w.get()
        acc = acc_ref[p % 2]
        dqkv_ref[p, :, :128] = (acc[:, :128] * SCALE).astype(BF)
        dkv = jnp.concatenate([(acc[:, 128:256] * SCALE).astype(BF), acc[:, 256:].astype(BF)], axis=1)
        for sl in blocks:
            dqkv_ref[p, sl, 128:] = dot(rev_ref[sl, :], dkv).astype(BF)
        for sl in blocks:
            part = dot(dqkv_ref[p, sl, :], w_ref[p], NT)
            if p > 0:
                part = part + dx_ref[sl, :]
            dx_ref[sl, :] = part

    total = 2 * pairs
    attended(0)
    probabilities(0)
    for h in range(total):
        scores(h)
        if h + 1 < total:
            if h % 2 == 1:
                attended((h + 1) // 2)
            probabilities(h + 1)
        values(h)
        query_skew(h)
        if h > 0:
            keys(h - 1)
            if h % 2 == 0:
                inputs(h // 2 - 1)
        key_skew(h)
        queries(h)
    keys(total - 1)
    inputs(pairs - 1)
    mine_ref[...] = dx_ref[rows_at(core, count), :]
    theirs_ref[...] = dx_ref[rows_at(1 - core, count), :].astype(BF)


def attention_grad(meta, layer, own, other, wo, saved, probs, pe, rev, w, tables):
    buckets = tables.shape[2]
    count, model = own.shape
    length = 2 * count
    sizes = tuple(item.shape[0] for item in saved)
    pairs = sum(sizes)
    out_shape = [
        jax.ShapeDtypeStruct((pairs, length, 384), BF),
        jax.ShapeDtypeStruct((pairs, 2, 128, buckets), BF),
        jax.ShapeDtypeStruct((count, model), F32),
        jax.ShapeDtypeStruct((count, model), BF),
    ]
    return pl.pallas_call(
        functools.partial(attention_grad_kernel, layer=layer, length=length, blk=256, base=0, sizes=sizes),
        out_shape=out_shape,
        grid_spec=pltpu.PrefetchScalarGridSpec(
            num_scalar_prefetch=1,
            grid=(1,),
            in_specs=[pl.BlockSpec(memory_space=pl.ANY)] * (7 + 2 * len(sizes)),
            out_specs=[whole_block(*item.shape) for item in out_shape],
            scratch_shapes=[
                pltpu.VMEM((length, model), BF),
                pltpu.VMEM((pairs, length, 128), BF),
                pltpu.VMEM((2 * pairs, length, length), BF),
                pltpu.VMEM((2, length, length), F32),
                pltpu.VMEM((2, length, length), BF),
                pltpu.VMEM((2, length, length), BF),
                pltpu.VMEM((2, length, WIDE), BF),
                pltpu.VMEM((2, length, WIDE), BF),
                pltpu.VMEM((2, length, 384), F32),
                pltpu.VMEM((length, model), F32),
                pltpu.VMEM((model // 2, model), BF),
                pltpu.VMEM((pairs, length, 384), BF),
                pltpu.VMEM((pairs, 3, WIDE, 128), BF),
                pltpu.VMEM((length, length), BF),
                pltpu.VMEM((pairs, model, 384), BF),
                pltpu.VMEM((2, WIDE, buckets), BF),
                pltpu.SemaphoreType.DMA((10 + 3 * pairs,)),
            ],
        ),
        compiler_params=pltpu.CompilerParams(vmem_limit_bytes=VMEM_LIMIT),
        cost_estimate=cost(6 * pairs),
        name="attention_grad",
    )(meta, own, other, wo, pe, rev, w, tables, *saved, *probs)


def pieces_kernel(meta_ref, in_ref, down_ref, in_piece, down_piece):
    in_piece[...] = in_ref[0]
    down_piece[...] = down_ref[0]


def weight_pieces(seq, layer, ffn_in, ffn_out):
    model, hidden = ffn_in.shape[1:]
    rows = model // 2
    steps = 4
    return pl.pallas_call(
        pieces_kernel,
        out_shape=[jax.ShapeDtypeStruct((rows, hidden), BF)] * 2,
        grid_spec=pltpu.PrefetchScalarGridSpec(
            num_scalar_prefetch=1,
            grid=(steps,),
            in_specs=[pl.BlockSpec((1, rows // steps, hidden), lambda g, m: (layer, steps * m[0] + g, 0))] * 2,
            out_specs=[pl.BlockSpec((rows // steps, hidden), lambda g, m: (g, 0))] * 2,
        ),
        cost_estimate=cost(1),
        name="weight_pieces",
    )(seq[None], ffn_in, ffn_out)


def weight_copies(layer, refs, scratch, sems, meta_ref):
    shards = []
    for s in range(4):
        group = []
        for m in range(2):
            own, core_own, near, far, core_near, core_far = refs[m]
            place = scratch.at[m, s]
            if s < 2:
                group.append(((own if s == 0 else core_own).at[layer], place))
            else:
                first, second = (near, far) if s == 2 else (core_near, core_far)
                rows = first.shape[0]
                one = pl.multiple_of(meta_ref[4] * rows, rows)
                two = pl.multiple_of((1 - meta_ref[4]) * rows, rows)
                group.append((first, place.at[pl.ds(one, rows)]))
                group.append((second, place.at[pl.ds(two, rows)]))
        shards.append(group)
    copies, k = [], 0
    for group in shards:
        made = []
        for source, target in group:
            made.append(pltpu.make_async_copy(source, target, sems.at[k]))
            k += 1
        copies.append(made)
    return copies


COPIES = 12


def row_norm(state, gain, bias):
    centered = state - jnp.mean(state, axis=1, keepdims=True)
    inverse = lax.rsqrt(jnp.mean(centered * centered, axis=1, keepdims=True) + EPSILON)
    return centered * inverse * gain + bias


def row_norm_grad(state, gain, d_result):
    centered = state - jnp.mean(state, axis=1, keepdims=True)
    inverse = lax.rsqrt(jnp.mean(centered * centered, axis=1, keepdims=True) + EPSILON)
    unit = centered * inverse
    d_unit = d_result * gain
    d_state = inverse * (
        d_unit
        - jnp.mean(d_unit, axis=1, keepdims=True)
        - unit * jnp.mean(d_unit * unit, axis=1, keepdims=True)
    )
    return d_state, jnp.sum(d_result * unit, axis=0, keepdims=True), jnp.sum(d_result, axis=0, keepdims=True)


def tokens_kernel(meta_ref, *rest, layer, chunk, groups):
    o_refs, rest = rest[: 2 * groups], rest[2 * groups :]
    x_ref, wo_ref, norm_ref, *rest = rest
    wires, rest = rest[:12], rest[12:]
    y_ref, yb_ref, mb_ref, resid_ref, pre_ref, slope_ref, scratch, sems, heads = rest
    copies = weight_copies(layer, (wires[:6], wires[6:]), scratch, sems, meta_ref)
    for group in copies:
        for item in group:
            item.start()
    at = 0
    for core in (meta_ref[3], 1 - meta_ref[3]):
        for first, size in head_rows(core):
            heads[at : at + size] = wo_ref[0, pl.ds(pl.multiple_of(first, 64), size), :]
            at += size
    resid = x_ref[...].astype(F32) + dot(jnp.concatenate([o[...] for o in o_refs], axis=1), heads[...])
    resid_ref[...] = resid
    middle = row_norm(resid, norm_ref[0:1, :], norm_ref[1:2, :])
    mb = middle.astype(BF)
    mb_ref[...] = mb
    pre_ref[...] = middle
    hidden = scratch.shape[3]
    per = hidden // chunk
    total = 4 * per

    def up(k):
        s, c = k // per, k % per
        if c == 0:
            for item in copies[s]:
                item.wait()
        return dot(mb, scratch[0, s, :, c * chunk : (c + 1) * chunk])

    ahead = up(0)
    for k in range(total):
        s, c = k // per, k % per
        h = ahead
        if k + 1 < total:
            ahead = up(k + 1)
        cumulative = 0.5 * (1.0 + lax.erf(h * 0.7071067811865476))
        density = jnp.exp(-0.5 * h * h) * 0.3989422804014327
        slope_ref[:, k * chunk : (k + 1) * chunk] = (cumulative + h * density).astype(BF)
        act = (h * cumulative).astype(BF)
        pre_ref[...] = pre_ref[...] + dot(act, scratch[1, s, :, c * chunk : (c + 1) * chunk], NT)
    y = row_norm(pre_ref[...], norm_ref[2:3, :], norm_ref[3:4, :])
    y_ref[...] = y
    yb_ref[...] = y.astype(BF)


def token_step(meta, layer, o_own, o_other, x, wo, norms, wires):
    count, model = x.shape
    hidden = wires[0].shape[2]
    mine = [pl.BlockSpec((count, o.shape[1]), lambda g, m: (m[3], 0)) for o in o_own + o_other]
    hbm = pl.BlockSpec(memory_space=pl.ANY)
    return pl.pallas_call(
        functools.partial(tokens_kernel, layer=layer, chunk=768, groups=len(o_own)),
        out_shape=(
            jax.ShapeDtypeStruct((count, model), F32),
            jax.ShapeDtypeStruct((count, model), BF),
            jax.ShapeDtypeStruct((count, model), BF),
            jax.ShapeDtypeStruct((count, model), F32),
            jax.ShapeDtypeStruct((count, model), F32),
            jax.ShapeDtypeStruct((count, 4 * hidden), BF),
        ),
        grid_spec=pltpu.PrefetchScalarGridSpec(
            num_scalar_prefetch=1,
            grid=(1,),
            in_specs=mine + [
                whole_block(count, model),
                pl.BlockSpec((1, model, model), lambda g, m: (layer, 0, 0)),
                whole_block(4, model),
            ] + [hbm] * 12,
            out_specs=(
                whole_block(count, model), whole_block(count, model), whole_block(count, model), whole_block(count, model), whole_block(count, model),
                whole_block(count, 4 * hidden),
            ),
            scratch_shapes=[
                pltpu.VMEM((2, 4, model, hidden), BF),
                pltpu.SemaphoreType.DMA((COPIES,)),
                pltpu.VMEM((model, model), BF),
            ],
        ),
        compiler_params=pltpu.CompilerParams(vmem_limit_bytes=VMEM_LIMIT),
        cost_estimate=cost(10),
        name="token_step",
    )(meta, *o_own, *o_other, x, wo, norms, *wires)


def tokens_grad_kernel(meta_ref, *rest, layer, chunk, parts):
    ups, rest = rest[:parts], rest[parts:]
    pre_ref, resid_ref, slope_ref, norm_ref, *rest = rest
    wires, rest = rest[:12], rest[12:]
    df_ref, dr_ref, drb_ref, scratch, sems, dm_ref, dn_ref = rest
    count = dm_ref.shape[0]
    copies = weight_copies(layer, (wires[:6], wires[6:]), scratch, sems, meta_ref)
    for group in copies:
        for item in group:
            item.start()
    dy = ups[0][...].astype(F32)
    for item in ups[1:]:
        dy = dy + item[...].astype(F32)
    dz, dg2, db2 = row_norm_grad(pre_ref[...], norm_ref[2:3, :], dy)
    df = dz.astype(BF)
    df_ref[:count, :] = df
    dm_ref[...] = dz
    hidden = scratch.shape[3]
    per = hidden // chunk
    total = 4 * per

    def down(k):
        s, c = k // per, k % per
        if c == 0:
            for item in copies[s]:
                item.wait()
        return dot(df, scratch[1, s, :, c * chunk : (c + 1) * chunk])

    ahead = down(0)
    for k in range(total):
        s, c = k // per, k % per
        dg = ahead
        if k + 1 < total:
            ahead = down(k + 1)
        dh = (dg * slope_ref[:, k * chunk : (k + 1) * chunk].astype(F32)).astype(BF)
        dm_ref[...] = dm_ref[...] + dot(dh, scratch[0, s, :, c * chunk : (c + 1) * chunk], NT)
    dr, dg1, db1 = row_norm_grad(resid_ref[...], norm_ref[0:1, :], dm_ref[...])
    dr_ref[...] = dr
    drb_ref[...] = dr.astype(BF)
    dn_ref[...] = jnp.zeros_like(dn_ref)
    for k, row in enumerate((dg1, db1, dg2, db2)):
        high = row.astype(BF)
        dn_ref[k : k + 1, :] = high.astype(F32)
        dn_ref[4 + k : 5 + k, :] = row - high.astype(F32)
    df_ref[count:, :] = dn_ref[...].astype(BF)


def token_grad(meta, layer, ups, pre, resid, slope, norms, wires):
    count, model = pre.shape
    hidden = wires[0].shape[2]
    hbm = pl.BlockSpec(memory_space=pl.ANY)
    return pl.pallas_call(
        functools.partial(tokens_grad_kernel, layer=layer, chunk=768, parts=len(ups)),
        out_shape=(
            jax.ShapeDtypeStruct((count + NORM_ROWS, model), BF),
            jax.ShapeDtypeStruct((count, model), F32),
            jax.ShapeDtypeStruct((count, model), BF),
        ),
        grid_spec=pltpu.PrefetchScalarGridSpec(
            num_scalar_prefetch=1,
            grid=(1,),
            in_specs=[whole_block(count, model)] * len(ups)
            + [whole_block(count, model), whole_block(count, model), whole_block(count, 4 * hidden), whole_block(4, model)]
            + [hbm] * 12,
            out_specs=(whole_block(count + NORM_ROWS, model), whole_block(count, model), whole_block(count, model)),
            scratch_shapes=[
                pltpu.VMEM((2, 4, model, hidden), BF),
                pltpu.SemaphoreType.DMA((COPIES,)),
                pltpu.VMEM((count, model), F32),
                pltpu.VMEM((NORM_ROWS, model), F32),
            ],
        ),
        compiler_params=pltpu.CompilerParams(vmem_limit_bytes=VMEM_LIMIT),
        cost_estimate=cost(10),
        name="token_grad",
    )(meta, *ups, pre, resid, slope, norms, *wires)


def hidden_grad_kernel(meta_ref, *refs):
    m_refs, d_refs = refs[:4], refs[4:8]
    wi_ref, wd_ref, keep_ref, give_ref, down_keep, down_give, m_ref, d_ref, mt_ref, dt_ref = refs[8:]
    per = keep_ref.shape[1]
    chunk = wi_ref.shape[2]

    bit, seq = meta_ref[6], meta_ref[4]

    @pl.when(pl.program_id(0) == 0)
    def _():
        for sources, target, transposed, second in ((m_refs, m_ref, mt_ref, False), (d_refs, d_ref, dt_ref, True)):
            for k, source in enumerate(sources):
                count = m_refs[0].shape[0]
                target[k * count : (k + 1) * count, :] = source[:count, :]
                turned = source[:count, :].T
                for n in range(8):
                    s, low = n // 4, n % 2
                    number = 4 * jnp.abs(low - bit) + n // 2 if second else 4 * jnp.abs(s - seq) + n % 4
                    place = pl.ds(pl.multiple_of(number * per, per), per)
                    transposed[place, k * count : (k + 1) * count] = turned[n * per : (n + 1) * per]

    kind = 2 * meta_ref[5] + meta_ref[3]
    count = m_refs[0].shape[0]
    rows = jnp.zeros((NORM_ROWS, d_refs[0].shape[1]), F32)
    for source in d_refs:
        rows = rows + source[count:, :].astype(F32)
    number = lax.broadcasted_iota(jnp.int32, rows.shape, 0)
    norm = jnp.sum(jnp.where((number == kind) | (number == kind + 4), rows, 0.0), axis=0, keepdims=True)
    high = norm.astype(BF).astype(F32)
    norm = jnp.where(lax.broadcasted_iota(jnp.int32, rows.shape, 0) == 0, high, norm - high).astype(BF)

    h = dot(m_ref[...], wi_ref[0])
    cumulative = 0.5 * (1.0 + lax.erf(h * 0.7071067811865476))
    density = jnp.exp(-0.5 * h * h) * 0.3989422804014327
    act = (h * cumulative).astype(BF)
    dh = (dot(d_ref[...], wd_ref[0]) * (cumulative + h * density)).astype(BF)
    half = mt_ref.shape[0] // 2
    for which, (first_out, second_out) in enumerate(((keep_ref, down_keep), (give_ref, down_give))):
        gi = dot(mt_ref[which * half : (which + 1) * half, :], dh).astype(BF)
        gd = dot(dt_ref[which * half : (which + 1) * half, :], act).astype(BF)
        for n in range(4):
            rows = slice(n * per, (n + 1) * per)
            first_out[n] = gi[rows]
            second_out[n // 2, n % 2, :per, :] = gd[rows]
            at = 2 * n * per
            even, odd = norm[:, at : at + per], norm[:, at + per : at + 2 * per]
            piece = jnp.where(bit == which, even.astype(F32), odd.astype(F32)).astype(BF)
            piece = jnp.concatenate([piece, jnp.zeros((NORM_ROWS, 128 - per), BF)], axis=1)
            second_out[n // 2, n % 2, per:, :] = jnp.concatenate([piece] * (chunk // 128), axis=1)


def hidden_grad(meta, layer, rows, d_rows, w_in, w_down):
    count, model = rows[0].shape
    hidden = w_in.shape[2]
    chunk = 256
    shape = (4, model // 8, hidden)
    down = (2, 2, model // 8 + NORM_ROWS, hidden)
    return pl.pallas_call(
        hidden_grad_kernel,
        out_shape=[jax.ShapeDtypeStruct(shape, BF)] * 2 + [jax.ShapeDtypeStruct(down, BF)] * 2,
        grid_spec=pltpu.PrefetchScalarGridSpec(
            num_scalar_prefetch=1,
            grid=(hidden // chunk,),
            in_specs=[whole_block(*a.shape) for a in (*rows, *d_rows)] + [
                pl.BlockSpec((1, model, chunk), lambda g, m: (layer, 0, g)),
                pl.BlockSpec((1, model, chunk), lambda g, m: (layer, 0, g)),
            ],
            out_specs=[pl.BlockSpec(shape[:2] + (chunk,), lambda g, m: (0, 0, g))] * 2
            + [pl.BlockSpec(down[:3] + (chunk,), lambda g, m: (0, 0, 0, g))] * 2,
            scratch_shapes=[pltpu.VMEM((4 * count, model), BF)] * 2 + [pltpu.VMEM((model, 4 * count), BF)] * 2,
        ),
        compiler_params=pltpu.CompilerParams(vmem_limit_bytes=VMEM_LIMIT),
        cost_estimate=cost(10),
        name="hidden_grad",
    )(meta, *rows, *d_rows, w_in, w_down)


def projection_grad_kernel(
    meta_ref, x_own_ref, x_other_ref, d_own_ref, d_other_ref, *rest, length, chunks, pairs, groups, grads,
):
    lists = []
    for size in (groups, groups, grads[0], grads[1], grads[1]):
        lists.append(rest[:size])
        rest = rest[size:]
    o_own = [o.at[:, 128 * k : 128 * (k + 1)] for o in lists[0] for k in range(o.shape[1] // 128)]
    o_other = [o.at[:, 128 * k : 128 * (k + 1)] for o in lists[1] for k in range(o.shape[1] // 128)]
    dqkv, dpos, dpos_other = ([r.at[k] for r in part for k in range(r.shape[0])] for part in lists[2:])
    rel_ref, wq_ref, wk_ref, a_keep, a_give, b_keep, b_give, *rest = rest
    x_ref, d_ref, left_ref, out_ref, right_ref, pos_ref, w_ref = rest
    core = meta_ref[3]
    seq = meta_ref[4]
    y_own = meta_ref[5]
    count = length // 2
    model = x_ref.shape[1]
    buckets = rel_ref.shape[1]
    low = half_of(0)
    zero = jnp.zeros((), BF)
    assemble(x_ref, x_own_ref, x_other_ref, core, count)
    assemble(d_ref, d_own_ref, d_other_ref, core, count)
    left_ref[:, :length] = x_ref[...].T
    left_ref[:, length:] = rel_ref[0].T
    for place, o, dp in ((core, o_own, dpos), (1 - core, o_other, dpos_other)):
        at = 0
        for first, size in head_rows(place):
            rows = pl.ds(pl.multiple_of(first, 64), size)
            p, inner = at // 128, at % 128
            if inner == 0:
                o_t = o[p][...].T
            out_ref[rows, :] = o_t[inner : inner + size]
            for c in range(2):
                pos_ref[c, rows, :] = dp[p][c, inner : inner + size, :]
            at += size
    per = model // chunks
    first_core = core == 0
    half_chunks = chunks // 2
    tile = lambda c, p: dqkv[p][:, 128 * c : 128 * (c + 1)]
    own_pos = [[dpos[p][c].astype(F32).T.astype(BF) for p in range(pairs)] for c in range(2)]
    at = 0
    for first, size in head_rows(core):
        rows = pl.ds(pl.multiple_of(first, 64), size)
        w_ref[0, at : at + size, :] = wq_ref[0, 0, rows, :]
        w_ref[1, at : at + size, :] = wk_ref[0, 0, rows, :]
        at += size
    back = (dot(w_ref[0], pos_ref[0]) + dot(w_ref[1], pos_ref[1])).T
    share = buckets // chunks
    for y in range(2):
        full = 0 if y == 0 else 2
        if y == 0:
            mixed = lambda q, k: jnp.where(low, q, rolled(k))
            v_mix = jnp.where(low, tile(2, 1), zero)
        else:
            mixed = lambda q, k: jnp.where(low, rolled(q), k)
            v_mix = jnp.where(low, rolled(tile(2, 1)), zero)
        right_ref[:length, 0:128] = tile(0, full)
        right_ref[:length, 128:256] = tile(1, full)
        right_ref[:length, 256:384] = mixed(tile(0, 1), tile(1, 1))
        right_ref[length:, 0:128] = own_pos[0][full]
        right_ref[length:, 128:256] = own_pos[1][full]
        right_ref[length:, 256:384] = mixed(own_pos[0][1], own_pos[1][1])
        base = 384 * y
        t0, t1, t2 = (d_ref[:, base + 128 * k : base + 128 * (k + 1)] for k in range(3))
        of = jnp.where(first_core, t0, t2)
        om = jnp.where(low, zero, jnp.where(first_core, rolled(t1), t1))
        one = dot(left_ref[...], right_ref[...])
        two = dot(left_ref[:, :length], jnp.concatenate([tile(2, full), v_mix], axis=1))
        three = dot(out_ref[...], jnp.concatenate([om, of], axis=1))
        rel_full = back[:, 128 * full : 128 * (full + 1)]
        rel_rest = back[:, 128:256] if y == 0 else pltpu.roll(back[:, 128:256], HEAD_DIM, 1)

        def store_a(ref, n, keep):
            rows = slice(n * per, (n + 1) * per)
            ref[keep, :per, :] = one[rows].astype(BF)
            for k in range(3):
                part = slice(n * share + 16 * k, n * share + 16 * (k + 1))
                ref[keep, per:, 128 * k : 128 * (k + 1)] = rel_full[part].astype(BF)

        def store_b(ref, n, keep):
            rows = slice(n * per, (n + 1) * per)
            ref[keep, :per, 0:128] = two[rows, :128].astype(BF)
            ref[keep, :per, 128:256] = (two[rows, 128:] + three[rows, :128]).astype(BF)
            ref[keep, :per, 256:384] = three[rows, 128:].astype(BF)
            ref[keep, per:, 0:128] = rel_full[n * share + 48 : (n + 1) * share].astype(BF)
            for k in range(2):
                a = rel_rest[n * share + 32 * k : n * share + 32 * k + 16]
                b = rel_rest[n * share + 32 * k + 16 : n * share + 32 * k + 32]
                ref[keep, per:, 128 * (k + 1) : 128 * (k + 2)] = jnp.where(low, a, pltpu.roll(b, HEAD_DIM, 1)).astype(BF)

        @pl.when(y_own == y)
        def _():
            for n in range(chunks):
                store_a(a_keep, n, n)

        @pl.when(y_own != y)
        def _():
            for n in range(chunks):
                store_a(a_give, n, n)

        for s in range(2):
            @pl.when(seq == s)
            def _():
                for n in range(chunks):
                    kept = n // half_chunks == s
                    store_b((b_keep if kept else b_give).at[y], n, n % half_chunks)


def projection_grad(meta, layer, x_own, x_other, dqkv, o_own, o_other, d_own, d_other, dpos, dpos_other, rel, qkv_weight):
    count, model = x_own.shape
    length = 2 * count
    buckets = rel.shape[1]
    chunks = 8
    rows = model // chunks + 16
    args = (x_own, x_other, d_own, d_other, *o_own, *o_other, *dqkv, *dpos, *dpos_other)
    return pl.pallas_call(
        functools.partial(
            projection_grad_kernel, length=length, chunks=chunks, pairs=3, groups=len(o_own), grads=(len(dqkv), len(dpos))
        ),
        out_shape=[jax.ShapeDtypeStruct((chunks, rows, model // 2), BF)] * 2
        + [jax.ShapeDtypeStruct((2, chunks // 2, rows, model // 2), BF)] * 2,
        grid_spec=pltpu.PrefetchScalarGridSpec(
            num_scalar_prefetch=1,
            grid=(1,),
            in_specs=[whole_block(*a.shape) for a in args]
            + [
                pl.BlockSpec((1, buckets, model), lambda g, m: (layer, 0, 0)),
                pl.BlockSpec((1, 1, model, model), lambda g, m: (layer, 0, 0, 0)),
                pl.BlockSpec((1, 1, model, model), lambda g, m: (layer, 1, 0, 0)),
            ],
            out_specs=[whole_block(chunks, rows, model // 2)] * 2 + [whole_block(2, chunks // 2, rows, model // 2)] * 2,
            scratch_shapes=[
                pltpu.VMEM((length, model), BF),
                pltpu.VMEM((length, model), BF),
                pltpu.VMEM((model, length + buckets), BF),
                pltpu.VMEM((model, length), BF),
                pltpu.VMEM((length + buckets, 384), BF),
                pltpu.VMEM((2, model, buckets), BF),
                pltpu.VMEM((2, 384, model), BF),
            ],
        ),
        compiler_params=pltpu.CompilerParams(vmem_limit_bytes=VMEM_LIMIT),
        cost_estimate=cost(10),
        name="projection_grad",
    )(meta, *args, rel, qkv_weight, qkv_weight)


class Wires:
    def __init__(self):
        self.seqs, self.rows, self.cols = (lax.axis_size(name) for name in ("seq", "rows", "col"))
        self.seq, self.row, self.col = (lax.axis_index(name) for name in ("seq", "rows", "col"))
        self.core, self.y = self.col % 2, self.col // 2

    def send(self, array, target):
        pairs = []
        for s in range(self.seqs):
            for r in range(self.rows):
                for c in range(self.cols):
                    t = target(s, r, c)
                    pairs.append(((s * self.rows + r) * self.cols + c, (t[0] * self.rows + t[1]) * self.cols + t[2]))
        return lax.ppermute(array, ("seq", "rows", "col"), pairs)

    def turn(self, array):
        return self.send(array, lambda s, r, c: (c % 2, r, c - c % 2 + s))

    def to_core(self, array):
        return self.send(array, lambda s, r, c: (s, r, c ^ 1))

    def to_y(self, array):
        return self.send(array, lambda s, r, c: (s, r, c ^ 2))

    def to_seq(self, array):
        return self.send(array, lambda s, r, c: (1 - s, r, c))

    def to_row(self, array, bit):
        return self.send(array, lambda s, r, c: (s, r ^ (1 << bit), c))


def cut(array, axis, mine):
    shape = array.shape
    pairs = array.reshape(shape[:axis] + (shape[axis] // 2, 2) + shape[axis + 1 :])
    return pick(pairs, axis + 1, mine), pick(pairs, axis + 1, 1 - mine)


def bits_of(count):
    return count.bit_length() - 1


def add(a, b):
    return (a.astype(F32) + b.astype(F32)).astype(a.dtype)


def pick(array, axis, index):
    return lax.dynamic_index_in_dim(array, index, axis, keepdims=False)


def unpack(main, rel, wires):
    t = [main[:, 128 * k : 128 * (k + 1)] for k in range(6)]
    full = [t[0], t[1], t[3], t[5], rel[:, :128]]
    rest = [t[2][:, :64], t[2][:, 64:], t[4][:, :64], t[4][:, 64:], rel[:, 128:]]
    out = []
    for f, r in zip(full, rest):
        out.append(jnp.where(wires.core == 0, jnp.concatenate([f, r], 1), jnp.concatenate([r, f], 1)).astype(F32))
    return out


def after(arrays, *earlier):
    return lax.optimization_barrier((arrays, earlier))[0]


def finer(parts, wires):
    for bit in reversed(range(bits_of(wires.rows) - 2)):
        mine = (wires.row >> bit) & 1
        sums = []
        for v in parts:
            v = v.reshape((2, v.shape[0] // 2) + v.shape[1:])
            sums.append(add(pick(v, 0, mine), wires.to_row(pick(v, 0, 1 - mine), bit)))
        parts = sums
    return parts


def first_flow(keep, give, wires):
    got = yield [(wires.to_seq, give)]
    total = add(keep, got[0])
    low = bits_of(wires.rows) - 2
    for bit in (low, low + 1):
        keep, give = cut(total, 0, (wires.row >> bit) & 1)
        got = yield [(functools.partial(wires.to_row, bit=bit), give)]
        total = add(keep, got[0])
    return finer([total[0]], wires)[0].astype(F32)


def second_flow(keep, give, wires):
    low = bits_of(wires.rows) - 2
    got = yield [(functools.partial(wires.to_row, bit=low), give)]
    keep, give = cut(add(keep, got[0]), 1, (wires.row >> (low + 1)) & 1)
    got = yield [(functools.partial(wires.to_row, bit=low + 1), give)]
    total = add(keep, got[0])[:, 0]
    got = yield [(wires.to_seq, pick(total, 0, 1 - wires.seq))]
    total = add(pick(total, 0, wires.seq), got[0])
    per = total.shape[0] - NORM_ROWS
    down, norm = finer([total[:per], total[per : per + 2, :per].T], wires)
    norm = norm.astype(F32)
    return down.astype(F32), norm[:, 0] + norm[:, 1]


def projection_flow(a_keep, a_give, b_keep, b_give, wires):
    got = yield [(wires.to_y, a_give), (wires.to_seq, b_give)]
    a = add(a_keep, got[0]).reshape((2, 4) + a_keep.shape[1:])
    b = add(b_keep, got[1])
    got = yield [(wires.to_seq, pick(a, 0, 1 - wires.seq)), (wires.to_y, pick(b, 0, 1 - wires.y))]
    both = jnp.stack([add(pick(a, 0, wires.seq), got[0]), add(pick(b, 0, wires.y), got[1])])
    low = bits_of(wires.rows) - 2
    for bit in (low, low + 1):
        keep, give = cut(both, 1, (wires.row >> bit) & 1)
        got = yield [(functools.partial(wires.to_row, bit=bit), give)]
        both = add(keep, got[0])
    both = both[:, 0]
    main = jnp.concatenate([both[0, :-16], both[1, :-16]], axis=1)
    tail = jnp.concatenate([both[0, -16:], both[1, -16:]], axis=1)
    full = jnp.concatenate([tail[:, 128 * k : 128 * (k + 1)] for k in range(4)], axis=0)
    rest = jnp.concatenate([tail[:, 512 + 64 * k : 576 + 64 * k] for k in range(4)], axis=0)
    rel = jnp.concatenate([full, rest], axis=1)
    main, rel = finer([main, rel], wires)
    return unpack(main, rel, wires)


class Flow:
    def __init__(self, steps):
        self.steps, self.value = steps, None
        self.take(next(steps))

    def take(self, sends):
        self.ready = [array for _, array in sends]
        self.under_way = [send(array) for send, array in sends]

    def step(self, *earlier):
        if self.under_way is None:
            return
        arrived = after(self.under_way, earlier) if earlier else self.under_way
        try:
            self.take(self.steps.send(arrived))
        except StopIteration as stop:
            self.ready, self.under_way, self.value = stop.value, None, stop.value

    def finish(self, *earlier):
        while self.under_way is not None:
            self.step(*earlier)
        return self.value


def gather_start(rows, wires):
    return rows, wires.to_core(rows), wires.to_y(rows)


def gather_end(gathered, wires, *earlier):
    rows, other, far = gathered
    return rows, other, far, wires.to_core(after(far, earlier))


def per_device(tokens, lengths, qkv_weight, out_weight, rel_table, ffn_in, ffn_out, norm_params, cotangent):
    wires = Wires()
    core = wires.core
    count, model = tokens.shape[1:]
    length = 2 * count
    layers = qkv_weight.shape[0]
    table_np = bucket_table()
    tables = jnp.asarray(np.stack([table_np, table_np[::-1]]), BF)
    rev = jnp.asarray(np.eye(length)[::-1], BF)
    split = [(0, 2), (2, 1)]

    weights = (ffn_in, ffn_out)
    near, far, core_near, core_far = ([[None, None], [None, None]] for _ in range(4))
    core_own = [None, None]
    start = wires.turn(tokens[0])
    other_lengths = wires.to_core(lengths)
    pieces = [weight_pieces(wires.seq, 0, ffn_in, ffn_out), None]
    done = (pieces[0], start, other_lengths)
    lengths = jnp.where(core == wires.seq, lengths, after(other_lengths, done))
    ends = jnp.cumsum(lengths[0]).astype(jnp.int32)
    low_bit = (wires.row >> (bits_of(wires.rows) - 2)) & 1
    meta = jnp.concatenate([ends[:3], jnp.stack([core, wires.seq, wires.y, low_bit])]).astype(jnp.int32)
    xb = start
    near[0] = [wires.to_y(after(piece, done)) for piece in pieces[0]]
    xb_other = wires.to_core(after(start, done))
    core_own[0] = wires.to_core(after(ffn_in, done))

    place = jnp.stack([core, wires.seq]).astype(jnp.int32)
    prepared = [prepare(after(place, done, meta), 0, qkv_weight, rel_table, tables, weights), None]
    prepared[0], pieces[1] = prepared[0][:2], prepared[0][2:]
    done = (pieces[1], near[0][0], xb_other, core_own[0])
    far[0][0] = wires.to_seq(after(near[0][0], done))
    core_near[0][0] = wires.to_core(after(near[0][0], done))
    core_own[1] = wires.to_core(after(ffn_out, done))
    near[1][0] = wires.to_y(after(pieces[1][0], done))

    w_pairs, pe = prepared[0]
    outs = []

    def attend(group, *arrived):
        outs.append(attention(meta, 0, group, after(xb, arrived), xb_other, w_pairs, pe, rev))

    attend(split[0], done)
    done = (outs[0], far[0][0], core_near[0][0], core_own[1], near[0][1])
    far[0][1] = wires.to_seq(after(near[0][1], done))
    core_near[0][1] = wires.to_core(after(near[0][1], done))
    core_far[0][0] = wires.to_core(after(far[0][0], done))
    near[1][1] = wires.to_y(after(pieces[1][1], done))
    attend(split[1], done)
    o_own = [jnp.concatenate([item[0] for item in outs], axis=1)]
    done = (o_own, core_near[0][1], core_far[0][0], near[1][0])
    o_other = [wires.to_core(after(item, done)) for item in o_own]
    core_near[1][0] = wires.to_core(after(near[1][0], done))
    far[1][0] = wires.to_seq(after(near[1][0], done))
    prepared[1] = prepare(after(place, done), 1, qkv_weight, rel_table, tables)
    done = (prepared[1], far[0][1], o_other, core_near[1][0])
    core_far[0][1] = wires.to_core(after(far[0][1], done))

    def wire_args(n):
        return [
            item for m in range(2)
            for item in (weights[m], core_own[m], near[n][m], far[n][m], core_near[n][m], core_far[n][m])
        ]

    x = after(start, done)
    y, yb, mb, resid, pre, slope = token_step(meta, 0, o_own, o_other, x, out_weight, norm_params[0], wire_args(0))
    kept = [(xb, xb_other, outs, o_own, o_other, resid, pre, slope, mb)]

    done = (yb, far[1][0], near[1][1])
    xb, xb_other = yb, wires.to_core(after(yb, done))
    core_far[1][0] = wires.to_core(after(far[1][0], done))
    far[1][1] = wires.to_seq(after(near[1][1], done))
    core_near[1][1] = wires.to_core(after(near[1][1], done))
    w_pairs, pe = prepared[1]
    outs = [attention(meta, 1, (0, 3), after(xb, done, xb_other), xb_other, w_pairs, pe, rev)]
    o_own = [outs[0][0]]
    done = (o_own, far[1][1], core_far[1][0], core_near[1][1])
    o_other = [wires.to_core(after(item, done)) for item in o_own]
    core_far[1][1] = wires.to_core(after(far[1][1], done))
    d_final = wires.turn(after(cotangent[0], done))
    x = after(y, done, o_other, core_far[1][1])
    y, yb, mb, resid, pre, slope = token_step(meta, 1, o_own, o_other, x, out_weight, norm_params[1], wire_args(1))
    kept.append((xb, xb_other, outs, o_own, o_other, resid, pre, slope, mb))
    done = (y, d_final)
    output = wires.turn(after(y, done))
    m_rows = [gather_start(after(kept[0][-1], done), wires), gather_start(after(mb, done), wires)]

    xb, xb_other, outs, o_own, o_other, resid, pre, slope, mb = kept[1]
    w_pairs, pe = prepared[1]
    df, dr, drb = token_grad(meta, 1, [after(d_final, m_rows[1][0])], pre, resid, slope, norm_params[1], wire_args(1))
    done = (df, m_rows[1][2], m_rows[1][1])
    drb_other = wires.to_core(after(drb, done))
    d_rows = [None, gather_start(after(df, done), wires)]
    m_rows[1] = gather_end(m_rows[1], wires, done)
    done = (done, drb_other, output)
    saved, probs = ([item[k] for item in outs] for k in (1, 2))
    dqkv, dpos, dx_mine, dx_theirs = attention_grad(
        meta, 1, after(drb, done), drb_other, out_weight, saved, probs, pe, rev, w_pairs, tables
    )
    done = (dx_mine, d_rows[1][2], d_rows[1][1], m_rows[1][3], m_rows[0][2], m_rows[0][1])
    d_rows[1] = gather_end(d_rows[1], wires, done)
    dx_got = wires.to_core(after(dx_theirs, done))
    dpos_other = wires.to_core(after(dpos, done))
    m_rows[0] = gather_end(m_rows[0], wires, done)
    keep, give, *down = hidden_grad(after(meta, done), 1, m_rows[1], d_rows[1], ffn_in, ffn_out)
    done = (down, m_rows[0][3], dpos_other, dx_got)
    first = [None, Flow(first_flow(keep, after(give, done), wires))]
    second = [None, Flow(second_flow(*after(down, done), wires))]
    projection = [None, None]
    projection_args = (xb, xb_other, [dqkv], o_own, o_other, drb, drb_other, [dpos], [dpos_other], rel_table, qkv_weight)

    xb, xb_other, outs, o_own, o_other, resid, pre, slope, mb = kept[0]
    w_pairs, pe = prepared[0]
    ups = [after(dr, done, second[1].ready), dx_mine, dx_got]
    df, dr, drb = token_grad(meta, 0, ups, pre, resid, slope, norm_params[0], wire_args(0))
    done = (df,)
    d_rows[0] = gather_start(after(df, done), wires)
    drb_other = wires.to_core(after(drb, done))
    packed = projection_grad(after(meta, done), 1, *projection_args)
    done = (packed, d_rows[0][2], d_rows[0][1], drb_other, first[1].under_way, second[1].under_way)
    d_rows[0] = gather_end(d_rows[0], wires, done)
    projection[1] = Flow(projection_flow(*after(packed, done), wires))
    first[1].step(done)
    second[1].step(done, first[1].ready)
    keep, give, *down = hidden_grad(after(meta, done, second[1].ready), 0, m_rows[0], d_rows[0], ffn_in, ffn_out)
    done = (down, projection[1].under_way, first[1].under_way, second[1].under_way)
    projection[1].step(done)
    first[1].step(done)
    first[0] = Flow(first_flow(keep, after(give, done, projection[1].ready), wires))
    second[0] = Flow(second_flow(*after(down, done), wires))
    done = (done, projection[1].ready, first[1].ready)
    saved, probs = ([item[k] for item in outs] for k in (1, 2))
    dqkv, dpos, dx_mine, dx_theirs = attention_grad(
        meta, 0, after(drb, done), drb_other, out_weight, saved, probs, pe, rev, w_pairs, tables
    )
    done = (dx_mine, projection[1].under_way, first[0].under_way, second[0].under_way, first[1].under_way)
    dpos_other = wires.to_core(after(dpos, done))
    projection[1].step(done)
    first[0].step(done, projection[1].ready)
    second[1].step(done)
    now = after(meta, done, projection[1].ready, first[0].ready, second[1].ready)
    packed = projection_grad(
        now, 0, xb, xb_other, [dqkv], o_own, o_other, drb, drb_other, [dpos], [dpos_other], rel_table, qkv_weight
    )
    done = (packed, projection[1].under_way, first[0].under_way, second[1].under_way)
    projection[0] = Flow(projection_flow(*after(packed, done), wires))
    projection[1].step(done, projection[0].ready)
    first[0].step(done, projection[1].ready)
    second[0].step(done, first[0].ready)
    first[1].finish(second[0].ready)
    second[1].finish(second[0].ready)
    done = (projection[0].under_way, second[0].ready)
    projection[0].step(done)
    dx_got = wires.to_core(after(dx_theirs, projection[0].ready))
    d_input = wires.turn((dr + dx_mine + dx_got.astype(F32)).astype(BF)).astype(F32)
    done = (projection[0].under_way, projection[1].under_way, first[0].under_way)
    projection[0].step(done)
    projection[1].finish(projection[0].ready)
    first[0].finish(projection[0].ready)
    done = (projection[0].under_way, second[0].under_way)
    projection[0].step(done)
    second[0].step(projection[0].ready)
    parts = [flow.finish() for flow in projection]
    first, second = ([flow.finish() for flow in flows] for flows in (first, second))
    grad_qkv = jnp.stack([jnp.stack(part[:3]) for part in parts])
    grad_out = jnp.stack([part[3] for part in parts])
    grad_rel = jnp.stack([part[4] for part in parts])
    grad_in = jnp.stack(first)
    grad_down, grad_norms = (jnp.stack([item[k] for item in second]) for k in range(2))
    return (output[None], d_input[None], grad_qkv, grad_out, grad_rel, grad_in, grad_down, grad_norms[:, None])


def solution(mesh):
    placed = (
        P(("rows", "col"), "seq", None),
        P(("rows", "col"), None),
        P(),
        P(),
        P(),
        P(None, None, "col"),
        P(None, None, "col"),
        P(),
        P(("rows", "col"), "seq", None),
    )
    return jax.shard_map(
        per_device,
        mesh=mesh,
        in_specs=placed,
        out_specs=(
            P(("rows", "col"), "seq", None),
            P(("rows", "col"), "seq", None),
            P(None, None, ("seq", "rows"), "col"),
            P(None, ("seq", "rows"), "col"),
            P(None, ("seq", "rows"), "col"),
            P(None, ("seq", "rows"), "col"),
            P(None, ("seq", "rows"), "col"),
            P(None, "col", ("seq", "rows")),
        ),
        check_vma=False,
    )
```

```python
import functools

import jax
import jax.numpy as jnp
import numpy as np
from jax import lax
from jax.experimental import pallas as pl
from jax.experimental.pallas import tpu as pltpu
from jax.sharding import PartitionSpec as P

HEAD_DIM = 64
SPAN = 256
MAX_REL = 512
WIDE = 640
HALF = 320
EPSILON = 1e-07
SCALE = (3.0 * HEAD_DIM) ** (-0.5)
LOG2E = 1.4426950408889634
BF = jnp.bfloat16
F32 = jnp.float32
NT = (((1,), (1,)), ((), ()))
NN = (((1,), (0,)), ((), ()))
TN = (((0,), (0,)), ((), ()))
VMEM_LIMIT = 50 << 20
NORM_ROWS = 16


def dot(a, b, dims=NN):
    return lax.dot_general(a, b, dims, preferred_element_type=F32)


def bucket_table():
    relative = HALF - np.arange(WIDE)
    middle = SPAN // 2
    absolute = np.where((relative < middle) & (relative > -middle), middle - 1, np.abs(relative))
    log_position = np.ceil(np.log(absolute / middle) / np.log((MAX_REL - 1) / middle) * (middle - 1)) + middle
    bucket = np.where(absolute <= middle, relative, log_position * np.sign(relative))
    bucket = np.clip(bucket + SPAN, 0, 2 * SPAN - 1).astype(np.int32)
    return (bucket[:, None] == np.arange(2 * SPAN)[None, :]).astype(np.float32)


def assemble(target, own, other, core, count):
    target[pl.ds(pl.multiple_of(core * count, count), count), :] = own[...]
    target[pl.ds(pl.multiple_of((1 - core) * count, count), count), :] = other[...]


class Late:
    def __init__(self, source, target, sem):
        self.target, self.copy = target, pltpu.make_async_copy(source, target, sem)
        self.copy.start()

    def get(self):
        if self.copy is not None:
            self.copy.wait()
            self.copy = None
        return self.target


class Loads:
    def __init__(self, sems):
        self.sems, self.count = sems, 0

    def __call__(self, source, target):
        self.count += 1
        return Late(source, target, self.sems.at[self.count - 1])


def rows_at(number, count):
    return pl.ds(pl.multiple_of(number * count, count), count)


def half_of(head):
    lane = lax.broadcasted_iota(jnp.int32, (1, 128), 1)
    return (lane < HEAD_DIM) if head == 0 else (lane >= HEAD_DIM)


def doc_number(position, meta_ref):
    total = jnp.zeros(position.shape, jnp.int32)
    for k in range(3):
        total = total + (position >= meta_ref[k]).astype(jnp.int32)
    return total


def skew(values, base):
    return pltpu.roll(values, base % WIDE, 1, stride=1, stride_axis=0)


def rolled(values):
    return pltpu.roll(values.astype(F32), HEAD_DIM, 1).astype(values.dtype)


def cost(microseconds):
    return pl.CostEstimate(flops=int(microseconds * 1e8), bytes_accessed=1 << 20, transcendentals=0)


def whole_block(*shape):
    return pl.BlockSpec(shape, lambda g, m: (0,) * len(shape))


def prepare_kernel(meta_ref, first_ref, second_ref, rel_ref, table_ref, *rest):
    if len(rest) > 2:
        in_ref, down_ref, w_ref, pe_ref, in_piece, down_piece = rest
        in_piece[...] = in_ref[0]
        down_piece[...] = down_ref[0]
    else:
        w_ref, pe_ref = rest
    first = meta_ref[0] == 0
    low = half_of(0)

    @pl.when(pl.program_id(0) != 1)
    def _():
        for c in range(3):
            w_ref[0, 0, :, 128 * c : 128 * (c + 1)] = first_ref[0, c]

    @pl.when(pl.program_id(0) == 1)
    def _():
        for c in range(3):
            a, b = first_ref[0, c], second_ref[0, c]
            zero = jnp.where(low, a, rolled(b))
            one = jnp.where(low, rolled(a), b)
            w_ref[0, 0, :, 128 * c : 128 * (c + 1)] = jnp.where(first, zero, one)

    pos = dot(rel_ref[0], w_ref[0, 0, :, :256]).astype(BF)
    ext = dot(table_ref[0], pos).astype(BF)
    pe_ref[0, 0, 0] = ext[:, :128]
    pe_ref[0, 0, 1] = ext[:, 128:]
    pe_ref[0, 0, 2] = dot(table_ref[1], pos[:, 128:]).astype(BF)


def prepare(place, layer, qkv_weight, rel_table, tables, ffn=()):
    hidden = ffn[0].shape[2] if ffn else 0
    rows = qkv_weight.shape[2] // 2
    kinds, model = qkv_weight.shape[1:3]
    pairs, buckets = 3, rel_table.shape[1]
    return pl.pallas_call(
        prepare_kernel,
        out_shape=(
            jax.ShapeDtypeStruct((1, pairs, model, 384), BF),
            jax.ShapeDtypeStruct((1, pairs, 3, WIDE, 128), BF),
        ) + (jax.ShapeDtypeStruct((rows, hidden), BF),) * len(ffn),
        grid_spec=pltpu.PrefetchScalarGridSpec(
            num_scalar_prefetch=1,
            grid=(pairs,),
            in_specs=[
                pl.BlockSpec(
                    (1, kinds, model, 128),
                    lambda g, m: (layer, 0, 0, jnp.where(g == 1, 1, jnp.where(g == 0, 0, 3) + 2 * m[0])),
                ),
                pl.BlockSpec((1, kinds, model, 128), lambda g, m: (layer, 0, 0, 4)),
                pl.BlockSpec((1, buckets, model), lambda g, m: (layer, 0, 0)),
                whole_block(2, WIDE, buckets),
            ] + [pl.BlockSpec((1, rows // pairs, hidden), lambda g, m: (layer + 1, pairs * m[1] + g, 0))] * len(ffn),
            out_specs=(
                pl.BlockSpec((1, 1, model, 384), lambda g, m: (0, g, 0, 0)),
                pl.BlockSpec((1, 1, 3, WIDE, 128), lambda g, m: (0, g, 0, 0, 0)),
            ) + (pl.BlockSpec((rows // pairs, hidden), lambda g, m: (g, 0)),) * len(ffn),
        ),
        compiler_params=pltpu.CompilerParams(vmem_limit_bytes=VMEM_LIMIT),
        cost_estimate=cost(5),
        name="prepare",
    )(place, qkv_weight, qkv_weight, rel_table, tables, *ffn)


def attention_kernel(
    meta_ref, own_ref, other_ref, w_ref, pe_ref, rev_ref, o_ref, sv_ref, p_hbm,
    x_ref, s_ref, t1_ref, t2_ref, bt_ref, sb_ref, pp_ref, pj_ref, sems, *, length, blk, pairs,
):
    assemble(x_ref, own_ref, other_ref, meta_ref[3], length // 2)
    zero = jnp.zeros((), BF)
    ids_j = doc_number(lax.broadcasted_iota(jnp.int32, (1, length), 1), meta_ref)
    blocks = [slice(b, b + blk) for b in range(0, length, blk)]
    copies = []

    def project(p):
        for sl in blocks:
            qkv = dot(x_ref[sl, :], w_ref[0, p]).astype(BF)
            sb_ref[p, sl, :] = qkv
            sv_ref[p, sl, :128] = qkv[:, :128]

    def reverse(p):
        for sl in blocks:
            sv_ref[p, sl, 128:] = dot(rev_ref[sl, :], sb_ref[p, :, 128:]).astype(BF)

    def key_positions(h):
        for sl in blocks:
            kb = jnp.where(half_of(h % 2), sb_ref[h // 2, sl, 128:256], zero)
            t2_ref[h % 2, sl, :] = dot(kb, pe_ref[0, h // 2, 0], NT)

    def key_skew(h):
        for sl in blocks:
            t2 = skew(t2_ref[h % 2, sl, :], sl.start + HALF)[:, :length].astype(BF)
            bt_ref[h % 2, :, sl] = t2.T

    def products(h):
        for sl in blocks:
            qb = jnp.where(half_of(h % 2), sb_ref[h // 2, sl, :128], zero)
            t1_ref[h % 2, sl, :] = dot(qb, pe_ref[0, h // 2, 1], NT)
            s_ref[h % 2, sl, :] = dot(qb, sb_ref[h // 2, :, 128:256], NT)

    def softmax(h):
        for sl in blocks:
            t1 = skew(t1_ref[h % 2, sl, :], sl.start + HALF)[:, :length]
            total = s_ref[h % 2, sl, :] + t1 + bt_ref[h % 2, sl, :].astype(F32)
            ids_i = doc_number(lax.broadcasted_iota(jnp.int32, (blk, 1), 0) + sl.start, meta_ref)
            total = jnp.where(ids_i == ids_j, total, -1e30)
            e = jnp.exp2((total - jnp.max(total, axis=1, keepdims=True)) * (SCALE * LOG2E))
            pp_ref[h % 2, sl, :] = (e * (1.0 / jnp.sum(e, axis=1, keepdims=True))).astype(BF)

    def outputs(h):
        lanes = slice(128 * (h // 2), 128 * (h // 2 + 1))
        for sl in blocks:
            o = dot(pp_ref[h % 2, sl, :], sb_ref[h // 2, :, 256:]).astype(BF)
            o_ref[sl, lanes] = o if h % 2 == 0 else jnp.where(half_of(1), o, o_ref[sl, lanes])
        if h >= 2:
            copies[h - 2].wait()
        for sl in blocks:
            pj_ref[h % 2, sl, :] = dot(pp_ref[h % 2, sl, :], rev_ref[...]).astype(BF)
        copies.append(pltpu.make_async_copy(pj_ref.at[h % 2], p_hbm.at[h], sems.at[h % 2]))
        copies[h].start()

    project(0)
    key_positions(0)
    for h in range(2 * pairs):
        products(h)
        if h > 0:
            outputs(h - 1)
        else:
            reverse(0)
        key_skew(h)
        if h + 1 < 2 * pairs:
            if h % 2 == 1:
                project((h + 1) // 2)
            key_positions(h + 1)
            if h % 2 == 1:
                reverse((h + 1) // 2)
        softmax(h)
    outputs(2 * pairs - 1)
    copies[-2].wait()
    copies[-1].wait()


def attention(meta, layer, group, own, other, w, pe, rev):
    base, pairs = group
    base //= pairs
    count, model = own.shape
    length = 2 * count
    return pl.pallas_call(
        functools.partial(attention_kernel, length=length, blk=256, pairs=pairs),
        out_shape=(
            jax.ShapeDtypeStruct((length, pairs * 128), BF),
            jax.ShapeDtypeStruct((pairs, length, 384), BF),
            jax.ShapeDtypeStruct((2 * pairs, length, length), BF),
        ),
        grid_spec=pltpu.PrefetchScalarGridSpec(
            num_scalar_prefetch=1,
            grid=(1,),
            in_specs=[
                whole_block(count, model),
                whole_block(count, model),
                pl.BlockSpec((1, pairs, model, 384), lambda g, m: (0, base, 0, 0)),
                pl.BlockSpec((1, pairs, 2, WIDE, 128), lambda g, m: (0, base, 0, 0, 0)),
                whole_block(length, length),
            ],
            out_specs=(
                whole_block(length, pairs * 128),
                whole_block(pairs, length, 384),
                pl.BlockSpec(memory_space=pl.ANY),
            ),
            scratch_shapes=[
                pltpu.VMEM((length, model), BF),
                pltpu.VMEM((2, length, length), F32),
                pltpu.VMEM((2, length, WIDE), F32),
                pltpu.VMEM((2, length, WIDE), F32),
                pltpu.VMEM((2, length, length), BF),
                pltpu.VMEM((pairs, length, 384), BF),
                pltpu.VMEM((2, length, length), BF),
                pltpu.VMEM((2, length, length), BF),
                pltpu.SemaphoreType.DMA((2,)),
            ],
        ),
        compiler_params=pltpu.CompilerParams(vmem_limit_bytes=VMEM_LIMIT),
        cost_estimate=cost(5 * pairs),
        name="attention",
    )(meta, own, other, w, pe, rev)


def head_rows(core):
    return ((256 * core, 128), (128 + 64 * core, 64), (512 + 64 * core, 64), (384 + 256 * core, 128))


def attention_grad_kernel(
    meta_ref, own_hbm, other_hbm, wo_hbm, pe_hbm, rev_hbm, w_hbm, table_hbm, *rest, layer, length, blk, base, sizes,
):
    pairs = sum(sizes)
    sv_hbm = [ref.at[k] for ref, size in zip(rest, sizes) for k in range(size)]
    p_hbm = [ref.at[k] for ref, size in zip(rest[len(sizes) :], sizes) for k in range(2 * size)]
    dqkv_ref, dpos_ref, mine_ref, theirs_ref, *rest = rest[2 * len(sizes) :]
    drb_ref, do_ref, p_ref, da_ref, ds_ref, dt_ref, u_ref, v_ref, acc_ref, dx_ref, heads_ref, *rest = rest
    sv_ref, pe_ref, rev_ref, w_ref, table_ref, loads = rest
    core = meta_ref[3]
    count = length // 2
    load = Loads(loads)
    rows = [load(own_hbm, drb_ref.at[rows_at(core, count)]), load(other_hbm, drb_ref.at[rows_at(1 - core, count)])]
    at = 0
    for start, size in head_rows(core):
        place = pl.ds(pl.multiple_of(start, 64), size)
        rows.append(load(wo_hbm.at[layer, place], heads_ref.at[pl.ds(at, size)]))
        at += size
    saved, probs = [], []
    for p in range(pairs):
        saved.append(load(sv_hbm[p], sv_ref.at[p]))
        probs += [load(p_hbm[2 * p + k], p_ref.at[2 * p + k]) for k in range(2)]
        if p == 0:
            pe = load(pe_hbm.at[0, pl.ds(base, pairs)], pe_ref)
            tables = load(table_hbm, table_ref)
            rev = load(rev_hbm, rev_ref)
            w = load(w_hbm.at[0, pl.ds(base, pairs)], w_ref)
    for item in rows:
        item.get()
    sv = [sv_ref.at[p] for p in range(pairs)]
    zero = jnp.zeros((), BF)
    pad = jnp.zeros((blk, WIDE - length), F32)
    blocks = [slice(b, b + blk) for b in range(0, length, blk)]
    half = lambda h: slice(HEAD_DIM * (h % 2), HEAD_DIM * (h % 2 + 1))

    def attended(p):
        rows = slice(128 * (base + p), 128 * (base + p + 1))
        for sl in blocks:
            do_ref[p, sl, :] = dot(drb_ref[sl, :], heads_ref[rows, :], NT).astype(BF)

    def probabilities(h):
        saved[h // 2].get()
        for sl in blocks:
            d_o = jnp.where(half_of(h % 2), do_ref[h // 2, sl, :], zero)
            da_ref[h % 2, sl, :] = dot(d_o, sv[h // 2][:, 256:], NT)

    def scores(h):
        probs[h].get()
        for sl in blocks:
            da = da_ref[h % 2, sl, :]
            p = p_ref[h, sl, :].astype(F32)
            ds = (p * (da - jnp.sum(p * da, axis=1, keepdims=True))).astype(BF)
            ds_ref[h % 2, sl, :] = ds
            dt_ref[h % 2, :, sl] = ds.T

    def query_skew(h):
        for sl in blocks:
            wide = jnp.concatenate([ds_ref[h % 2, sl, :].astype(F32), pad], axis=1)
            u_ref[h % 2, sl, :] = skew(wide, sl.start + WIDE - 192).astype(BF)

    def key_skew(h):
        for sl in blocks:
            wide = jnp.concatenate([dt_ref[h % 2, sl, :].astype(F32), pad], axis=1)
            v_ref[h % 2, sl, :] = skew(wide, sl.start + WIDE - 191).astype(BF)

    def add_to(p, sl, lanes, h, value):
        acc_ref[p % 2, sl, lanes] = value if h % 2 == 0 else acc_ref[p % 2, sl, lanes] + value

    def values(h):
        p = h // 2
        d_o = jnp.where(half_of(h % 2), do_ref[p], zero)
        add_to(p, slice(0, length), slice(256, 384), h, dot(p_ref[h], d_o, TN))

    def queries(h):
        pe.get()
        tables.get()
        p, own = h // 2, half_of(h % 2)
        kr = jnp.where(own, sv[p][:, 128:256], zero)
        pk = jnp.where(own, pe_ref[p, 2], zero)
        for sl in blocks:
            add_to(p, sl, slice(0, 128), h, dot(ds_ref[h % 2, sl, :], kr) + dot(u_ref[h % 2, sl, :], pk))
        d_ext = (dot(sv[p][:, :128].T[half(h)], u_ref[h % 2]) * SCALE).astype(BF)
        dpos_ref[p, 1, half(h), :] = dot(d_ext, table_ref[1]).astype(BF)

    def keys(h):
        p, own = h // 2, half_of(h % 2)
        q = jnp.where(own, sv[p][:, :128], zero)
        pq = jnp.where(own, pe_ref[p, 0], zero)
        for sl in blocks:
            add_to(p, sl, slice(128, 256), h, dot(dt_ref[h % 2, sl, :], q) + dot(v_ref[h % 2, sl, :], pq))
        d_ext = (dot(sv[p][:, 128:256].T[half(h)], v_ref[h % 2]) * SCALE).astype(BF)
        dpos_ref[p, 0, half(h), :] = dot(d_ext, table_ref[0]).astype(BF)

    def inputs(p):
        rev.get()
        w.get()
        acc = acc_ref[p % 2]
        dqkv_ref[p, :, :128] = (acc[:, :128] * SCALE).astype(BF)
        dkv = jnp.concatenate([(acc[:, 128:256] * SCALE).astype(BF), acc[:, 256:].astype(BF)], axis=1)
        for sl in blocks:
            dqkv_ref[p, sl, 128:] = dot(rev_ref[sl, :], dkv).astype(BF)
        for sl in blocks:
            part = dot(dqkv_ref[p, sl, :], w_ref[p], NT)
            if p > 0:
                part = part + dx_ref[sl, :]
            dx_ref[sl, :] = part

    total = 2 * pairs
    attended(0)
    probabilities(0)
    for h in range(total):
        scores(h)
        if h + 1 < total:
            if h % 2 == 1:
                attended((h + 1) // 2)
            probabilities(h + 1)
        values(h)
        query_skew(h)
        if h > 0:
            keys(h - 1)
            if h % 2 == 0:
                inputs(h // 2 - 1)
        key_skew(h)
        queries(h)
    keys(total - 1)
    inputs(pairs - 1)
    mine_ref[...] = dx_ref[rows_at(core, count), :]
    theirs_ref[...] = dx_ref[rows_at(1 - core, count), :].astype(BF)


def attention_grad(meta, layer, own, other, wo, saved, probs, pe, rev, w, tables):
    buckets = tables.shape[2]
    count, model = own.shape
    length = 2 * count
    sizes = tuple(item.shape[0] for item in saved)
    pairs = sum(sizes)
    out_shape = [
        jax.ShapeDtypeStruct((pairs, length, 384), BF),
        jax.ShapeDtypeStruct((pairs, 2, 128, buckets), BF),
        jax.ShapeDtypeStruct((count, model), F32),
        jax.ShapeDtypeStruct((count, model), BF),
    ]
    return pl.pallas_call(
        functools.partial(attention_grad_kernel, layer=layer, length=length, blk=256, base=0, sizes=sizes),
        out_shape=out_shape,
        grid_spec=pltpu.PrefetchScalarGridSpec(
            num_scalar_prefetch=1,
            grid=(1,),
            in_specs=[pl.BlockSpec(memory_space=pl.ANY)] * (7 + 2 * len(sizes)),
            out_specs=[whole_block(*item.shape) for item in out_shape],
            scratch_shapes=[
                pltpu.VMEM((length, model), BF),
                pltpu.VMEM((pairs, length, 128), BF),
                pltpu.VMEM((2 * pairs, length, length), BF),
                pltpu.VMEM((2, length, length), F32),
                pltpu.VMEM((2, length, length), BF),
                pltpu.VMEM((2, length, length), BF),
                pltpu.VMEM((2, length, WIDE), BF),
                pltpu.VMEM((2, length, WIDE), BF),
                pltpu.VMEM((2, length, 384), F32),
                pltpu.VMEM((length, model), F32),
                pltpu.VMEM((model // 2, model), BF),
                pltpu.VMEM((pairs, length, 384), BF),
                pltpu.VMEM((pairs, 3, WIDE, 128), BF),
                pltpu.VMEM((length, length), BF),
                pltpu.VMEM((pairs, model, 384), BF),
                pltpu.VMEM((2, WIDE, buckets), BF),
                pltpu.SemaphoreType.DMA((10 + 3 * pairs,)),
            ],
        ),
        compiler_params=pltpu.CompilerParams(vmem_limit_bytes=VMEM_LIMIT),
        cost_estimate=cost(6 * pairs),
        name="attention_grad",
    )(meta, own, other, wo, pe, rev, w, tables, *saved, *probs)


def pieces_kernel(meta_ref, in_ref, down_ref, in_piece, down_piece):
    in_piece[...] = in_ref[0]
    down_piece[...] = down_ref[0]


def weight_pieces(seq, layer, ffn_in, ffn_out):
    model, hidden = ffn_in.shape[1:]
    rows = model // 2
    steps = 4
    return pl.pallas_call(
        pieces_kernel,
        out_shape=[jax.ShapeDtypeStruct((rows, hidden), BF)] * 2,
        grid_spec=pltpu.PrefetchScalarGridSpec(
            num_scalar_prefetch=1,
            grid=(steps,),
            in_specs=[pl.BlockSpec((1, rows // steps, hidden), lambda g, m: (layer, steps * m[0] + g, 0))] * 2,
            out_specs=[pl.BlockSpec((rows // steps, hidden), lambda g, m: (g, 0))] * 2,
        ),
        cost_estimate=cost(1),
        name="weight_pieces",
    )(seq[None], ffn_in, ffn_out)


def weight_copies(layer, refs, scratch, sems, meta_ref):
    shards = []
    for s in range(4):
        group = []
        for m in range(2):
            own, core_own, near, far, core_near, core_far = refs[m]
            place = scratch.at[m, s]
            if s < 2:
                group.append(((own if s == 0 else core_own).at[layer], place))
            else:
                first, second = (near, far) if s == 2 else (core_near, core_far)
                rows = first.shape[0]
                one = pl.multiple_of(meta_ref[4] * rows, rows)
                two = pl.multiple_of((1 - meta_ref[4]) * rows, rows)
                group.append((first, place.at[pl.ds(one, rows)]))
                group.append((second, place.at[pl.ds(two, rows)]))
        shards.append(group)
    copies, k = [], 0
    for group in shards:
        made = []
        for source, target in group:
            made.append(pltpu.make_async_copy(source, target, sems.at[k]))
            k += 1
        copies.append(made)
    return copies


COPIES = 12


def row_norm(state, gain, bias):
    centered = state - jnp.mean(state, axis=1, keepdims=True)
    inverse = lax.rsqrt(jnp.mean(centered * centered, axis=1, keepdims=True) + EPSILON)
    return centered * inverse * gain + bias


def row_norm_grad(state, gain, d_result):
    centered = state - jnp.mean(state, axis=1, keepdims=True)
    inverse = lax.rsqrt(jnp.mean(centered * centered, axis=1, keepdims=True) + EPSILON)
    unit = centered * inverse
    d_unit = d_result * gain
    d_state = inverse * (
        d_unit
        - jnp.mean(d_unit, axis=1, keepdims=True)
        - unit * jnp.mean(d_unit * unit, axis=1, keepdims=True)
    )
    return d_state, jnp.sum(d_result * unit, axis=0, keepdims=True), jnp.sum(d_result, axis=0, keepdims=True)


def tokens_kernel(meta_ref, *rest, layer, chunk, groups):
    o_refs, rest = rest[: 2 * groups], rest[2 * groups :]
    x_ref, wo_ref, norm_ref, *rest = rest
    wires, rest = rest[:12], rest[12:]
    y_ref, yb_ref, mb_ref, resid_ref, pre_ref, slope_ref, scratch, sems, heads = rest
    copies = weight_copies(layer, (wires[:6], wires[6:]), scratch, sems, meta_ref)
    for group in copies:
        for item in group:
            item.start()
    at = 0
    for core in (meta_ref[3], 1 - meta_ref[3]):
        for first, size in head_rows(core):
            heads[at : at + size] = wo_ref[0, pl.ds(pl.multiple_of(first, 64), size), :]
            at += size
    resid = x_ref[...].astype(F32) + dot(jnp.concatenate([o[...] for o in o_refs], axis=1), heads[...])
    resid_ref[...] = resid
    middle = row_norm(resid, norm_ref[0:1, :], norm_ref[1:2, :])
    mb = middle.astype(BF)
    mb_ref[...] = mb
    pre_ref[...] = middle
    hidden = scratch.shape[3]
    per = hidden // chunk
    total = 4 * per

    def up(k):
        s, c = k // per, k % per
        if c == 0:
            for item in copies[s]:
                item.wait()
        return dot(mb, scratch[0, s, :, c * chunk : (c + 1) * chunk])

    ahead = up(0)
    for k in range(total):
        s, c = k // per, k % per
        h = ahead
        if k + 1 < total:
            ahead = up(k + 1)
        cumulative = 0.5 * (1.0 + lax.erf(h * 0.7071067811865476))
        density = jnp.exp(-0.5 * h * h) * 0.3989422804014327
        slope_ref[:, k * chunk : (k + 1) * chunk] = (cumulative + h * density).astype(BF)
        act = (h * cumulative).astype(BF)
        pre_ref[...] = pre_ref[...] + dot(act, scratch[1, s, :, c * chunk : (c + 1) * chunk], NT)
    y = row_norm(pre_ref[...], norm_ref[2:3, :], norm_ref[3:4, :])
    y_ref[...] = y
    yb_ref[...] = y.astype(BF)


def token_step(meta, layer, o_own, o_other, x, wo, norms, wires):
    count, model = x.shape
    hidden = wires[0].shape[2]
    mine = [pl.BlockSpec((count, o.shape[1]), lambda g, m: (m[3], 0)) for o in o_own + o_other]
    hbm = pl.BlockSpec(memory_space=pl.ANY)
    return pl.pallas_call(
        functools.partial(tokens_kernel, layer=layer, chunk=768, groups=len(o_own)),
        out_shape=(
            jax.ShapeDtypeStruct((count, model), F32),
            jax.ShapeDtypeStruct((count, model), BF),
            jax.ShapeDtypeStruct((count, model), BF),
            jax.ShapeDtypeStruct((count, model), F32),
            jax.ShapeDtypeStruct((count, model), F32),
            jax.ShapeDtypeStruct((count, 4 * hidden), BF),
        ),
        grid_spec=pltpu.PrefetchScalarGridSpec(
            num_scalar_prefetch=1,
            grid=(1,),
            in_specs=mine + [
                whole_block(count, model),
                pl.BlockSpec((1, model, model), lambda g, m: (layer, 0, 0)),
                whole_block(4, model),
            ] + [hbm] * 12,
            out_specs=(
                whole_block(count, model), whole_block(count, model), whole_block(count, model), whole_block(count, model), whole_block(count, model),
                whole_block(count, 4 * hidden),
            ),
            scratch_shapes=[
                pltpu.VMEM((2, 4, model, hidden), BF),
                pltpu.SemaphoreType.DMA((COPIES,)),
                pltpu.VMEM((model, model), BF),
            ],
        ),
        compiler_params=pltpu.CompilerParams(vmem_limit_bytes=VMEM_LIMIT),
        cost_estimate=cost(10),
        name="token_step",
    )(meta, *o_own, *o_other, x, wo, norms, *wires)


def tokens_grad_kernel(meta_ref, *rest, layer, chunk, parts):
    ups, rest = rest[:parts], rest[parts:]
    pre_ref, resid_ref, slope_ref, norm_ref, *rest = rest
    wires, rest = rest[:12], rest[12:]
    df_ref, dr_ref, drb_ref, scratch, sems, dm_ref, dn_ref = rest
    count = dm_ref.shape[0]
    copies = weight_copies(layer, (wires[:6], wires[6:]), scratch, sems, meta_ref)
    for group in copies:
        for item in group:
            item.start()
    dy = ups[0][...].astype(F32)
    for item in ups[1:]:
        dy = dy + item[...].astype(F32)
    dz, dg2, db2 = row_norm_grad(pre_ref[...], norm_ref[2:3, :], dy)
    df = dz.astype(BF)
    df_ref[:count, :] = df
    dm_ref[...] = dz
    hidden = scratch.shape[3]
    per = hidden // chunk
    total = 4 * per

    def down(k):
        s, c = k // per, k % per
        if c == 0:
            for item in copies[s]:
                item.wait()
        return dot(df, scratch[1, s, :, c * chunk : (c + 1) * chunk])

    ahead = down(0)
    for k in range(total):
        s, c = k // per, k % per
        dg = ahead
        if k + 1 < total:
            ahead = down(k + 1)
        dh = (dg * slope_ref[:, k * chunk : (k + 1) * chunk].astype(F32)).astype(BF)
        dm_ref[...] = dm_ref[...] + dot(dh, scratch[0, s, :, c * chunk : (c + 1) * chunk], NT)
    dr, dg1, db1 = row_norm_grad(resid_ref[...], norm_ref[0:1, :], dm_ref[...])
    dr_ref[...] = dr
    drb_ref[...] = dr.astype(BF)
    norm_rows(dn_ref, df_ref, count, (dg1, db1, dg2, db2))


def token_grad(meta, layer, ups, pre, resid, slope, norms, wires):
    count, model = pre.shape
    hidden = wires[0].shape[2]
    hbm = pl.BlockSpec(memory_space=pl.ANY)
    return pl.pallas_call(
        functools.partial(tokens_grad_kernel, layer=layer, chunk=768, parts=len(ups)),
        out_shape=(
            jax.ShapeDtypeStruct((count + NORM_ROWS, model), BF),
            jax.ShapeDtypeStruct((count, model), F32),
            jax.ShapeDtypeStruct((count, model), BF),
        ),
        grid_spec=pltpu.PrefetchScalarGridSpec(
            num_scalar_prefetch=1,
            grid=(1,),
            in_specs=[whole_block(count, model)] * len(ups)
            + [whole_block(count, model), whole_block(count, model), whole_block(count, 4 * hidden), whole_block(4, model)]
            + [hbm] * 12,
            out_specs=(whole_block(count + NORM_ROWS, model), whole_block(count, model), whole_block(count, model)),
            scratch_shapes=[
                pltpu.VMEM((2, 4, model, hidden), BF),
                pltpu.SemaphoreType.DMA((COPIES,)),
                pltpu.VMEM((count, model), F32),
                pltpu.VMEM((NORM_ROWS, model), F32),
            ],
        ),
        compiler_params=pltpu.CompilerParams(vmem_limit_bytes=VMEM_LIMIT),
        cost_estimate=cost(10),
        name="token_grad",
    )(meta, *ups, pre, resid, slope, norms, *wires)


def tokens_both_kernel(meta_ref, *rest, layer, chunk, groups):
    o_refs, rest = rest[: 2 * groups], rest[2 * groups :]
    x_ref, wo_ref, norm_ref, up_ref, *rest = rest
    wires, rest = rest[:12], rest[12:]
    y_ref, mb_ref, df_ref, dr_ref, drb_ref, scratch, sems, heads, pre_ref, slope_ref, dn_ref = rest
    copies = weight_copies(layer, (wires[:6], wires[6:]), scratch, sems, meta_ref)
    for group in copies:
        for item in group:
            item.start()
    at = 0
    for core in (meta_ref[3], 1 - meta_ref[3]):
        for first, size in head_rows(core):
            heads[at : at + size] = wo_ref[0, pl.ds(pl.multiple_of(first, 64), size), :]
            at += size
    resid = x_ref[...].astype(F32) + dot(jnp.concatenate([o[...] for o in o_refs], axis=1), heads[...])
    dr_ref[...] = resid
    middle = row_norm(resid, norm_ref[0:1, :], norm_ref[1:2, :])
    mb = middle.astype(BF)
    mb_ref[...] = mb
    pre_ref[...] = middle
    count, hidden = resid.shape[0], scratch.shape[3]
    per = hidden // chunk
    total = 4 * per

    def up(k):
        s, c = k // per, k % per
        if c == 0:
            for item in copies[s]:
                item.wait()
        return dot(mb, scratch[0, s, :, c * chunk : (c + 1) * chunk])

    ahead = up(0)
    for k in range(total):
        s, c = k // per, k % per
        h = ahead
        if k + 1 < total:
            ahead = up(k + 1)
        cumulative = 0.5 * (1.0 + lax.erf(h * 0.7071067811865476))
        density = jnp.exp(-0.5 * h * h) * 0.3989422804014327
        slope_ref[:, k * chunk : (k + 1) * chunk] = (cumulative + h * density).astype(BF)
        act = (h * cumulative).astype(BF)
        pre_ref[...] = pre_ref[...] + dot(act, scratch[1, s, :, c * chunk : (c + 1) * chunk], NT)
    y_ref[...] = row_norm(pre_ref[...], norm_ref[2:3, :], norm_ref[3:4, :])
    dz, dg2, db2 = row_norm_grad(pre_ref[...], norm_ref[2:3, :], up_ref[...].astype(F32))
    df = dz.astype(BF)
    df_ref[:count, :] = df
    pre_ref[...] = dz

    def down(k):
        s, c = k // per, k % per
        return dot(df, scratch[1, s, :, c * chunk : (c + 1) * chunk])

    ahead = down(0)
    for k in range(total):
        s, c = k // per, k % per
        dg = ahead
        if k + 1 < total:
            ahead = down(k + 1)
        dh = (dg * slope_ref[:, k * chunk : (k + 1) * chunk].astype(F32)).astype(BF)
        pre_ref[...] = pre_ref[...] + dot(dh, scratch[0, s, :, c * chunk : (c + 1) * chunk], NT)
    dr, dg1, db1 = row_norm_grad(dr_ref[...], norm_ref[0:1, :], pre_ref[...])
    dr_ref[...] = dr
    drb_ref[...] = dr.astype(BF)
    norm_rows(dn_ref, df_ref, count, (dg1, db1, dg2, db2))


def norm_rows(dn_ref, df_ref, count, sums):
    dn_ref[...] = jnp.zeros_like(dn_ref)
    for k, row in enumerate(sums):
        high = row.astype(BF)
        dn_ref[k : k + 1, :] = high.astype(F32)
        dn_ref[4 + k : 5 + k, :] = row - high.astype(F32)
    df_ref[count:, :] = dn_ref[...].astype(BF)


def token_both(meta, layer, o_own, o_other, x, wo, norms, d_out, wires):
    count, model = x.shape
    hidden = wires[0].shape[2]
    mine = [pl.BlockSpec((count, o.shape[1]), lambda g, m: (m[3], 0)) for o in o_own + o_other]
    hbm = pl.BlockSpec(memory_space=pl.ANY)
    out_shape = [
        jax.ShapeDtypeStruct((count, model), F32),
        jax.ShapeDtypeStruct((count, model), BF),
        jax.ShapeDtypeStruct((count + NORM_ROWS, model), BF),
        jax.ShapeDtypeStruct((count, model), F32),
        jax.ShapeDtypeStruct((count, model), BF),
    ]
    return pl.pallas_call(
        functools.partial(tokens_both_kernel, layer=layer, chunk=768, groups=len(o_own)),
        out_shape=out_shape,
        grid_spec=pltpu.PrefetchScalarGridSpec(
            num_scalar_prefetch=1,
            grid=(1,),
            in_specs=mine + [
                whole_block(count, model),
                pl.BlockSpec((1, model, model), lambda g, m: (layer, 0, 0)),
                whole_block(4, model),
                whole_block(count, model),
            ] + [hbm] * 12,
            out_specs=[whole_block(*item.shape) for item in out_shape],
            scratch_shapes=[
                pltpu.VMEM((2, 4, model, hidden), BF),
                pltpu.SemaphoreType.DMA((COPIES,)),
                pltpu.VMEM((model, model), BF),
                pltpu.VMEM((count, model), F32),
                pltpu.VMEM((count, 4 * hidden), BF),
                pltpu.VMEM((NORM_ROWS, model), F32),
            ],
        ),
        compiler_params=pltpu.CompilerParams(vmem_limit_bytes=VMEM_LIMIT),
        cost_estimate=cost(16),
        name="token_both",
    )(meta, *o_own, *o_other, x, wo, norms, d_out, *wires)


def hidden_grad_kernel(meta_ref, *refs):
    m_refs, d_refs = refs[:4], refs[4:8]
    wi_ref, wd_ref, keep_ref, give_ref, down_keep, down_give, m_ref, d_ref, mt_ref, dt_ref = refs[8:]
    per = keep_ref.shape[1]
    chunk = wi_ref.shape[2]

    bit, seq = meta_ref[6], meta_ref[4]

    @pl.when(pl.program_id(0) == 0)
    def _():
        for sources, target, transposed, second in ((m_refs, m_ref, mt_ref, False), (d_refs, d_ref, dt_ref, True)):
            for k, source in enumerate(sources):
                count = m_refs[0].shape[0]
                target[k * count : (k + 1) * count, :] = source[:count, :]
                turned = source[:count, :].T
                for n in range(8):
                    s, low = n // 4, n % 2
                    number = 4 * jnp.abs(low - bit) + n // 2 if second else 4 * jnp.abs(s - seq) + n % 4
                    place = pl.ds(pl.multiple_of(number * per, per), per)
                    transposed[place, k * count : (k + 1) * count] = turned[n * per : (n + 1) * per]

    kind = 2 * meta_ref[5] + meta_ref[3]
    count = m_refs[0].shape[0]
    rows = jnp.zeros((NORM_ROWS, d_refs[0].shape[1]), F32)
    for source in d_refs:
        rows = rows + source[count:, :].astype(F32)
    number = lax.broadcasted_iota(jnp.int32, rows.shape, 0)
    norm = jnp.sum(jnp.where((number == kind) | (number == kind + 4), rows, 0.0), axis=0, keepdims=True)
    high = norm.astype(BF).astype(F32)
    norm = jnp.where(lax.broadcasted_iota(jnp.int32, rows.shape, 0) == 0, high, norm - high).astype(BF)

    h = dot(m_ref[...], wi_ref[0])
    cumulative = 0.5 * (1.0 + lax.erf(h * 0.7071067811865476))
    density = jnp.exp(-0.5 * h * h) * 0.3989422804014327
    act = (h * cumulative).astype(BF)
    dh = (dot(d_ref[...], wd_ref[0]) * (cumulative + h * density)).astype(BF)
    half = mt_ref.shape[0] // 2
    for which, (first_out, second_out) in enumerate(((keep_ref, down_keep), (give_ref, down_give))):
        gi = dot(mt_ref[which * half : (which + 1) * half, :], dh).astype(BF)
        gd = dot(dt_ref[which * half : (which + 1) * half, :], act).astype(BF)
        for n in range(4):
            rows = slice(n * per, (n + 1) * per)
            first_out[n] = gi[rows]
            second_out[n // 2, n % 2, :per, :] = gd[rows]
            at = 2 * n * per
            even, odd = norm[:, at : at + per], norm[:, at + per : at + 2 * per]
            piece = jnp.where(bit == which, even.astype(F32), odd.astype(F32)).astype(BF)
            piece = jnp.concatenate([piece, jnp.zeros((NORM_ROWS, 128 - per), BF)], axis=1)
            second_out[n // 2, n % 2, per:, :] = jnp.concatenate([piece] * (chunk // 128), axis=1)


def hidden_grad(meta, layer, rows, d_rows, w_in, w_down):
    count, model = rows[0].shape
    hidden = w_in.shape[2]
    chunk = 256
    shape = (4, model // 8, hidden)
    down = (2, 2, model // 8 + NORM_ROWS, hidden)
    return pl.pallas_call(
        hidden_grad_kernel,
        out_shape=[jax.ShapeDtypeStruct(shape, BF)] * 2 + [jax.ShapeDtypeStruct(down, BF)] * 2,
        grid_spec=pltpu.PrefetchScalarGridSpec(
            num_scalar_prefetch=1,
            grid=(hidden // chunk,),
            in_specs=[whole_block(*a.shape) for a in (*rows, *d_rows)] + [
                pl.BlockSpec((1, model, chunk), lambda g, m: (layer, 0, g)),
                pl.BlockSpec((1, model, chunk), lambda g, m: (layer, 0, g)),
            ],
            out_specs=[pl.BlockSpec(shape[:2] + (chunk,), lambda g, m: (0, 0, g))] * 2
            + [pl.BlockSpec(down[:3] + (chunk,), lambda g, m: (0, 0, 0, g))] * 2,
            scratch_shapes=[pltpu.VMEM((4 * count, model), BF)] * 2 + [pltpu.VMEM((model, 4 * count), BF)] * 2,
        ),
        compiler_params=pltpu.CompilerParams(vmem_limit_bytes=VMEM_LIMIT),
        cost_estimate=cost(10),
        name="hidden_grad",
    )(meta, *rows, *d_rows, w_in, w_down)


def projection_grad_kernel(
    meta_ref, x_own_ref, x_other_ref, d_own_ref, d_other_ref, *rest, length, chunks, pairs, groups, grads,
):
    lists = []
    for size in (groups, groups, grads[0], grads[1], grads[1]):
        lists.append(rest[:size])
        rest = rest[size:]
    o_own = [o.at[:, 128 * k : 128 * (k + 1)] for o in lists[0] for k in range(o.shape[1] // 128)]
    o_other = [o.at[:, 128 * k : 128 * (k + 1)] for o in lists[1] for k in range(o.shape[1] // 128)]
    dqkv, dpos, dpos_other = ([r.at[k] for r in part for k in range(r.shape[0])] for part in lists[2:])
    rel_ref, wq_ref, wk_ref, a_keep, a_give, b_keep, b_give, *rest = rest
    x_ref, d_ref, left_ref, out_ref, right_ref, pos_ref, w_ref = rest
    core = meta_ref[3]
    seq = meta_ref[4]
    y_own = meta_ref[5]
    count = length // 2
    model = x_ref.shape[1]
    buckets = rel_ref.shape[1]
    low = half_of(0)
    zero = jnp.zeros((), BF)
    assemble(x_ref, x_own_ref, x_other_ref, core, count)
    assemble(d_ref, d_own_ref, d_other_ref, core, count)
    left_ref[:, :length] = x_ref[...].T
    left_ref[:, length:] = rel_ref[0].T
    for place, o, dp in ((core, o_own, dpos), (1 - core, o_other, dpos_other)):
        at = 0
        for first, size in head_rows(place):
            rows = pl.ds(pl.multiple_of(first, 64), size)
            p, inner = at // 128, at % 128
            if inner == 0:
                o_t = o[p][...].T
            out_ref[rows, :] = o_t[inner : inner + size]
            for c in range(2):
                pos_ref[c, rows, :] = dp[p][c, inner : inner + size, :]
            at += size
    per = model // chunks
    first_core = core == 0
    half_chunks = chunks // 2
    tile = lambda c, p: dqkv[p][:, 128 * c : 128 * (c + 1)]
    own_pos = [[dpos[p][c].astype(F32).T.astype(BF) for p in range(pairs)] for c in range(2)]
    at = 0
    for first, size in head_rows(core):
        rows = pl.ds(pl.multiple_of(first, 64), size)
        w_ref[0, at : at + size, :] = wq_ref[0, 0, rows, :]
        w_ref[1, at : at + size, :] = wk_ref[0, 0, rows, :]
        at += size
    back = (dot(w_ref[0], pos_ref[0]) + dot(w_ref[1], pos_ref[1])).T
    share = buckets // chunks
    for y in range(2):
        full = 0 if y == 0 else 2
        if y == 0:
            mixed = lambda q, k: jnp.where(low, q, rolled(k))
            v_mix = jnp.where(low, tile(2, 1), zero)
        else:
            mixed = lambda q, k: jnp.where(low, rolled(q), k)
            v_mix = jnp.where(low, rolled(tile(2, 1)), zero)
        right_ref[:length, 0:128] = tile(0, full)
        right_ref[:length, 128:256] = tile(1, full)
        right_ref[:length, 256:384] = mixed(tile(0, 1), tile(1, 1))
        right_ref[length:, 0:128] = own_pos[0][full]
        right_ref[length:, 128:256] = own_pos[1][full]
        right_ref[length:, 256:384] = mixed(own_pos[0][1], own_pos[1][1])
        base = 384 * y
        t0, t1, t2 = (d_ref[:, base + 128 * k : base + 128 * (k + 1)] for k in range(3))
        of = jnp.where(first_core, t0, t2)
        om = jnp.where(low, zero, jnp.where(first_core, rolled(t1), t1))
        one = dot(left_ref[...], right_ref[...])
        two = dot(left_ref[:, :length], jnp.concatenate([tile(2, full), v_mix], axis=1))
        three = dot(out_ref[...], jnp.concatenate([om, of], axis=1))
        rel_full = back[:, 128 * full : 128 * (full + 1)]
        rel_rest = back[:, 128:256] if y == 0 else pltpu.roll(back[:, 128:256], HEAD_DIM, 1)

        def store_a(ref, n, keep):
            rows = slice(n * per, (n + 1) * per)
            ref[keep, :per, :] = one[rows].astype(BF)
            for k in range(3):
                part = slice(n * share + 16 * k, n * share + 16 * (k + 1))
                ref[keep, per:, 128 * k : 128 * (k + 1)] = rel_full[part].astype(BF)

        def store_b(ref, n, keep):
            rows = slice(n * per, (n + 1) * per)
            ref[keep, :per, 0:128] = two[rows, :128].astype(BF)
            ref[keep, :per, 128:256] = (two[rows, 128:] + three[rows, :128]).astype(BF)
            ref[keep, :per, 256:384] = three[rows, 128:].astype(BF)
            ref[keep, per:, 0:128] = rel_full[n * share + 48 : (n + 1) * share].astype(BF)
            for k in range(2):
                a = rel_rest[n * share + 32 * k : n * share + 32 * k + 16]
                b = rel_rest[n * share + 32 * k + 16 : n * share + 32 * k + 32]
                ref[keep, per:, 128 * (k + 1) : 128 * (k + 2)] = jnp.where(low, a, pltpu.roll(b, HEAD_DIM, 1)).astype(BF)

        @pl.when(y_own == y)
        def _():
            for n in range(chunks):
                store_a(a_keep, n, n)

        @pl.when(y_own != y)
        def _():
            for n in range(chunks):
                store_a(a_give, n, n)

        for s in range(2):
            @pl.when(seq == s)
            def _():
                for n in range(chunks):
                    kept = n // half_chunks == s
                    store_b((b_keep if kept else b_give).at[y], n, n % half_chunks)


def projection_grad(meta, layer, x_own, x_other, dqkv, o_own, o_other, d_own, d_other, dpos, dpos_other, rel, qkv_weight):
    count, model = x_own.shape
    length = 2 * count
    buckets = rel.shape[1]
    chunks = 8
    rows = model // chunks + 16
    args = (x_own, x_other, d_own, d_other, *o_own, *o_other, *dqkv, *dpos, *dpos_other)
    return pl.pallas_call(
        functools.partial(
            projection_grad_kernel, length=length, chunks=chunks, pairs=3, groups=len(o_own), grads=(len(dqkv), len(dpos))
        ),
        out_shape=[jax.ShapeDtypeStruct((chunks, rows, model // 2), BF)] * 2
        + [jax.ShapeDtypeStruct((2, chunks // 2, rows, model // 2), BF)] * 2,
        grid_spec=pltpu.PrefetchScalarGridSpec(
            num_scalar_prefetch=1,
            grid=(1,),
            in_specs=[whole_block(*a.shape) for a in args]
            + [
                pl.BlockSpec((1, buckets, model), lambda g, m: (layer, 0, 0)),
                pl.BlockSpec((1, 1, model, model), lambda g, m: (layer, 0, 0, 0)),
                pl.BlockSpec((1, 1, model, model), lambda g, m: (layer, 1, 0, 0)),
            ],
            out_specs=[whole_block(chunks, rows, model // 2)] * 2 + [whole_block(2, chunks // 2, rows, model // 2)] * 2,
            scratch_shapes=[
                pltpu.VMEM((length, model), BF),
                pltpu.VMEM((length, model), BF),
                pltpu.VMEM((model, length + buckets), BF),
                pltpu.VMEM((model, length), BF),
                pltpu.VMEM((length + buckets, 384), BF),
                pltpu.VMEM((2, model, buckets), BF),
                pltpu.VMEM((2, 384, model), BF),
            ],
        ),
        compiler_params=pltpu.CompilerParams(vmem_limit_bytes=VMEM_LIMIT),
        cost_estimate=cost(10),
        name="projection_grad",
    )(meta, *args, rel, qkv_weight, qkv_weight)


class Wires:
    def __init__(self):
        self.seqs, self.rows, self.cols = (lax.axis_size(name) for name in ("seq", "rows", "col"))
        self.seq, self.row, self.col = (lax.axis_index(name) for name in ("seq", "rows", "col"))
        self.core, self.y = self.col % 2, self.col // 2

    def send(self, array, target):
        pairs = []
        for s in range(self.seqs):
            for r in range(self.rows):
                for c in range(self.cols):
                    t = target(s, r, c)
                    pairs.append(((s * self.rows + r) * self.cols + c, (t[0] * self.rows + t[1]) * self.cols + t[2]))
        return lax.ppermute(array, ("seq", "rows", "col"), pairs)

    def turn(self, array):
        return self.send(array, lambda s, r, c: (c % 2, r, c - c % 2 + s))

    def to_core(self, array):
        return self.send(array, lambda s, r, c: (s, r, c ^ 1))

    def to_y(self, array):
        return self.send(array, lambda s, r, c: (s, r, c ^ 2))

    def to_seq(self, array):
        return self.send(array, lambda s, r, c: (1 - s, r, c))

    def to_row(self, array, bit):
        return self.send(array, lambda s, r, c: (s, r ^ (1 << bit), c))


def cut(array, axis, mine):
    shape = array.shape
    pairs = array.reshape(shape[:axis] + (shape[axis] // 2, 2) + shape[axis + 1 :])
    return pick(pairs, axis + 1, mine), pick(pairs, axis + 1, 1 - mine)


def bits_of(count):
    return count.bit_length() - 1


def add(a, b):
    return (a.astype(F32) + b.astype(F32)).astype(a.dtype)


def pick(array, axis, index):
    return lax.dynamic_index_in_dim(array, index, axis, keepdims=False)


def unpack(main, rel, wires):
    t = [main[:, 128 * k : 128 * (k + 1)] for k in range(6)]
    full = [t[0], t[1], t[3], t[5], rel[:, :128]]
    rest = [t[2][:, :64], t[2][:, 64:], t[4][:, :64], t[4][:, 64:], rel[:, 128:]]
    out = []
    for f, r in zip(full, rest):
        out.append(jnp.where(wires.core == 0, jnp.concatenate([f, r], 1), jnp.concatenate([r, f], 1)).astype(F32))
    return out


def after(arrays, *earlier):
    return lax.optimization_barrier((arrays, earlier))[0]


def finer(parts, wires):
    for bit in reversed(range(bits_of(wires.rows) - 2)):
        mine = (wires.row >> bit) & 1
        sums = []
        for v in parts:
            v = v.reshape((2, v.shape[0] // 2) + v.shape[1:])
            sums.append(add(pick(v, 0, mine), wires.to_row(pick(v, 0, 1 - mine), bit)))
        parts = sums
    return parts


def first_flow(keep, give, wires):
    got = yield [(wires.to_seq, give)]
    total = add(keep, got[0])
    low = bits_of(wires.rows) - 2
    for bit in (low, low + 1):
        keep, give = cut(total, 0, (wires.row >> bit) & 1)
        got = yield [(functools.partial(wires.to_row, bit=bit), give)]
        total = add(keep, got[0])
    return finer([total[0]], wires)[0].astype(F32)


def second_flow(keep, give, wires):
    low = bits_of(wires.rows) - 2
    got = yield [(functools.partial(wires.to_row, bit=low), give)]
    keep, give = cut(add(keep, got[0]), 1, (wires.row >> (low + 1)) & 1)
    got = yield [(functools.partial(wires.to_row, bit=low + 1), give)]
    total = add(keep, got[0])[:, 0]
    got = yield [(wires.to_seq, pick(total, 0, 1 - wires.seq))]
    total = add(pick(total, 0, wires.seq), got[0])
    per = total.shape[0] - NORM_ROWS
    down, norm = finer([total[:per], total[per : per + 2, :per].T], wires)
    norm = norm.astype(F32)
    return down.astype(F32), norm[:, 0] + norm[:, 1]


def projection_flow(a_keep, a_give, b_keep, b_give, wires):
    got = yield [(wires.to_y, a_give), (wires.to_seq, b_give)]
    a = add(a_keep, got[0]).reshape((2, 4) + a_keep.shape[1:])
    b = add(b_keep, got[1])
    got = yield [(wires.to_seq, pick(a, 0, 1 - wires.seq)), (wires.to_y, pick(b, 0, 1 - wires.y))]
    both = jnp.stack([add(pick(a, 0, wires.seq), got[0]), add(pick(b, 0, wires.y), got[1])])
    low = bits_of(wires.rows) - 2
    for bit in (low, low + 1):
        keep, give = cut(both, 1, (wires.row >> bit) & 1)
        got = yield [(functools.partial(wires.to_row, bit=bit), give)]
        both = add(keep, got[0])
    both = both[:, 0]
    main = jnp.concatenate([both[0, :-16], both[1, :-16]], axis=1)
    tail = jnp.concatenate([both[0, -16:], both[1, -16:]], axis=1)
    full = jnp.concatenate([tail[:, 128 * k : 128 * (k + 1)] for k in range(4)], axis=0)
    rest = jnp.concatenate([tail[:, 512 + 64 * k : 576 + 64 * k] for k in range(4)], axis=0)
    rel = jnp.concatenate([full, rest], axis=1)
    main, rel = finer([main, rel], wires)
    return unpack(main, rel, wires)


class Flow:
    def __init__(self, steps):
        self.steps, self.value = steps, None
        self.take(next(steps))

    def take(self, sends):
        self.ready = [array for _, array in sends]
        self.under_way = [send(array) for send, array in sends]

    def step(self, *earlier):
        if self.under_way is None:
            return
        arrived = after(self.under_way, earlier) if earlier else self.under_way
        try:
            self.take(self.steps.send(arrived))
        except StopIteration as stop:
            self.ready, self.under_way, self.value = stop.value, None, stop.value

    def finish(self, *earlier):
        while self.under_way is not None:
            self.step(*earlier)
        return self.value


def gather_start(rows, wires):
    return rows, wires.to_core(rows), wires.to_y(rows)


def gather_end(gathered, wires, *earlier):
    rows, other, far = gathered
    return rows, other, far, wires.to_core(after(far, earlier))


def per_device(tokens, lengths, qkv_weight, out_weight, rel_table, ffn_in, ffn_out, norm_params, cotangent):
    wires = Wires()
    core = wires.core
    count, model = tokens.shape[1:]
    length = 2 * count
    layers = qkv_weight.shape[0]
    table_np = bucket_table()
    tables = jnp.asarray(np.stack([table_np, table_np[::-1]]), BF)
    rev = jnp.asarray(np.eye(length)[::-1], BF)
    split = [(0, 2), (2, 1)]

    weights = (ffn_in, ffn_out)
    near, far, core_near, core_far = ([[None, None], [None, None]] for _ in range(4))
    core_own = [None, None]
    start = wires.turn(tokens[0])
    other_lengths = wires.to_core(lengths)
    pieces = [weight_pieces(wires.seq, 0, ffn_in, ffn_out), None]
    done = (pieces[0], start, other_lengths)
    lengths = jnp.where(core == wires.seq, lengths, after(other_lengths, done))
    ends = jnp.cumsum(lengths[0]).astype(jnp.int32)
    low_bit = (wires.row >> (bits_of(wires.rows) - 2)) & 1
    meta = jnp.concatenate([ends[:3], jnp.stack([core, wires.seq, wires.y, low_bit])]).astype(jnp.int32)
    xb = start
    near[0] = [wires.to_y(after(piece, done)) for piece in pieces[0]]
    xb_other = wires.to_core(after(start, done))
    core_own[0] = wires.to_core(after(ffn_in, done))

    place = jnp.stack([core, wires.seq]).astype(jnp.int32)
    prepared = [prepare(after(place, done, meta), 0, qkv_weight, rel_table, tables, weights), None]
    prepared[0], pieces[1] = prepared[0][:2], prepared[0][2:]
    done = (pieces[1], near[0][0], xb_other, core_own[0])
    far[0][0] = wires.to_seq(after(near[0][0], done))
    core_near[0][0] = wires.to_core(after(near[0][0], done))
    core_own[1] = wires.to_core(after(ffn_out, done))
    near[1][0] = wires.to_y(after(pieces[1][0], done))

    w_pairs, pe = prepared[0]
    outs = []

    def attend(group, *arrived):
        outs.append(attention(meta, 0, group, after(xb, arrived), xb_other, w_pairs, pe, rev))

    attend(split[0], done)
    done = (outs[0], far[0][0], core_near[0][0], core_own[1], near[0][1])
    far[0][1] = wires.to_seq(after(near[0][1], done))
    core_near[0][1] = wires.to_core(after(near[0][1], done))
    core_far[0][0] = wires.to_core(after(far[0][0], done))
    near[1][1] = wires.to_y(after(pieces[1][1], done))
    attend(split[1], done)
    o_own = [jnp.concatenate([item[0] for item in outs], axis=1)]
    done = (o_own, core_near[0][1], core_far[0][0], near[1][0])
    o_other = [wires.to_core(after(item, done)) for item in o_own]
    core_near[1][0] = wires.to_core(after(near[1][0], done))
    far[1][0] = wires.to_seq(after(near[1][0], done))
    prepared[1] = prepare(after(place, done), 1, qkv_weight, rel_table, tables)
    done = (prepared[1], far[0][1], o_other, core_near[1][0])
    core_far[0][1] = wires.to_core(after(far[0][1], done))

    def wire_args(n):
        return [
            item for m in range(2)
            for item in (weights[m], core_own[m], near[n][m], far[n][m], core_near[n][m], core_far[n][m])
        ]

    x = after(start, done)
    y, yb, mb, resid, pre, slope = token_step(meta, 0, o_own, o_other, x, out_weight, norm_params[0], wire_args(0))
    kept = [(xb, xb_other, outs, o_own, o_other, resid, pre, slope, mb)]

    done = (yb, far[1][0], near[1][1])
    xb, xb_other = yb, wires.to_core(after(yb, done))
    core_far[1][0] = wires.to_core(after(far[1][0], done))
    far[1][1] = wires.to_seq(after(near[1][1], done))
    core_near[1][1] = wires.to_core(after(near[1][1], done))
    d_final = wires.turn(after(cotangent[0], done))
    w_pairs, pe = prepared[1]
    outs = [attention(meta, 1, (0, 3), after(xb, done, xb_other), xb_other, w_pairs, pe, rev)]
    o_own = [outs[0][0]]
    done = (o_own, far[1][1], core_far[1][0], core_near[1][1], d_final)
    o_other = [wires.to_core(after(item, done)) for item in o_own]
    core_far[1][1] = wires.to_core(after(far[1][1], done))
    x = after(y, done, o_other, core_far[1][1])
    y, mb, df, dr, drb = token_both(meta, 1, o_own, o_other, x, out_weight, norm_params[1], d_final, wire_args(1))
    done = (drb,)
    drb_other = wires.to_core(after(drb, done))
    m_rows = [None, gather_start(after(mb, done), wires)]
    d_rows = [None, gather_start(after(df, done), wires)]
    done = (done, drb_other)
    saved, probs = ([item[k] for item in outs] for k in (1, 2))
    dqkv, dpos, dx_mine, dx_theirs = attention_grad(
        meta, 1, after(drb, done), drb_other, out_weight, saved, probs, pe, rev, w_pairs, tables
    )
    done = (dx_mine, d_rows[1][2], d_rows[1][1], m_rows[1][2], m_rows[1][1])
    d_rows[1] = gather_end(d_rows[1], wires, done)
    m_rows[1] = gather_end(m_rows[1], wires, done)
    dx_got = wires.to_core(after(dx_theirs, done))
    dpos_other = wires.to_core(after(dpos, done))
    output = wires.turn(after(y, done))
    m_rows[0] = gather_start(after(kept[0][-1], done), wires)
    keep, give, *down = hidden_grad(after(meta, done), 1, m_rows[1], d_rows[1], ffn_in, ffn_out)
    done = (down, m_rows[0][1], m_rows[0][2], dpos_other, dx_got, output)
    m_rows[0] = gather_end(m_rows[0], wires, done)
    first = [None, Flow(first_flow(keep, after(give, done), wires))]
    second = [None, Flow(second_flow(*after(down, done), wires))]
    projection = [None, None]
    projection_args = (xb, xb_other, [dqkv], o_own, o_other, drb, drb_other, [dpos], [dpos_other], rel_table, qkv_weight)

    xb, xb_other, outs, o_own, o_other, resid, pre, slope, mb = kept[0]
    w_pairs, pe = prepared[0]
    ups = [after(dr, done, second[1].ready), dx_mine, dx_got]
    df, dr, drb = token_grad(meta, 0, ups, pre, resid, slope, norm_params[0], wire_args(0))
    done = (df, m_rows[0][3])
    d_rows[0] = gather_start(after(df, done), wires)
    drb_other = wires.to_core(after(drb, done))
    packed = projection_grad(after(meta, done), 1, *projection_args)
    done = (packed, d_rows[0][2], d_rows[0][1], drb_other, first[1].under_way, second[1].under_way)
    d_rows[0] = gather_end(d_rows[0], wires, done)
    projection[1] = Flow(projection_flow(*after(packed, done), wires))
    first[1].step(done)
    second[1].step(done, first[1].ready)
    keep, give, *down = hidden_grad(after(meta, done, second[1].ready), 0, m_rows[0], d_rows[0], ffn_in, ffn_out)
    done = (down, projection[1].under_way, first[1].under_way, second[1].under_way)
    projection[1].step(done)
    first[1].step(done)
    first[0] = Flow(first_flow(keep, after(give, done, projection[1].ready), wires))
    second[0] = Flow(second_flow(*after(down, done), wires))
    done = (done, projection[1].ready, first[1].ready)
    saved, probs = ([item[k] for item in outs] for k in (1, 2))
    dqkv, dpos, dx_mine, dx_theirs = attention_grad(
        meta, 0, after(drb, done), drb_other, out_weight, saved, probs, pe, rev, w_pairs, tables
    )
    done = (dx_mine, projection[1].under_way, first[0].under_way, second[0].under_way, first[1].under_way)
    dpos_other = wires.to_core(after(dpos, done))
    projection[1].step(done)
    first[0].step(done, projection[1].ready)
    second[1].step(done)
    now = after(meta, done, projection[1].ready, first[0].ready, second[1].ready)
    packed = projection_grad(
        now, 0, xb, xb_other, [dqkv], o_own, o_other, drb, drb_other, [dpos], [dpos_other], rel_table, qkv_weight
    )
    done = (packed, projection[1].under_way, first[0].under_way, second[1].under_way)
    projection[0] = Flow(projection_flow(*after(packed, done), wires))
    projection[1].step(done, projection[0].ready)
    first[0].step(done, projection[1].ready)
    second[0].step(done, first[0].ready)
    first[1].finish(second[0].ready)
    second[1].finish(second[0].ready)
    done = (projection[0].under_way, second[0].ready)
    projection[0].step(done)
    dx_got = wires.to_core(after(dx_theirs, projection[0].ready))
    d_input = wires.turn((dr + dx_mine + dx_got.astype(F32)).astype(BF)).astype(F32)
    done = (projection[0].under_way, projection[1].under_way, first[0].under_way)
    projection[0].step(done)
    projection[1].finish(projection[0].ready)
    first[0].finish(projection[0].ready)
    done = (projection[0].under_way, second[0].under_way)
    projection[0].step(done)
    second[0].step(projection[0].ready)
    parts = [flow.finish() for flow in projection]
    first, second = ([flow.finish() for flow in flows] for flows in (first, second))
    grad_qkv = jnp.stack([jnp.stack(part[:3]) for part in parts])
    grad_out = jnp.stack([part[3] for part in parts])
    grad_rel = jnp.stack([part[4] for part in parts])
    grad_in = jnp.stack(first)
    grad_down, grad_norms = (jnp.stack([item[k] for item in second]) for k in range(2))
    return (output[None], d_input[None], grad_qkv, grad_out, grad_rel, grad_in, grad_down, grad_norms[:, None])


def solution(mesh):
    placed = (
        P(("rows", "col"), "seq", None),
        P(("rows", "col"), None),
        P(),
        P(),
        P(),
        P(None, None, "col"),
        P(None, None, "col"),
        P(),
        P(("rows", "col"), "seq", None),
    )
    return jax.shard_map(
        per_device,
        mesh=mesh,
        in_specs=placed,
        out_specs=(
            P(("rows", "col"), "seq", None),
            P(("rows", "col"), "seq", None),
            P(None, None, ("seq", "rows"), "col"),
            P(None, ("seq", "rows"), "col"),
            P(None, ("seq", "rows"), "col"),
            P(None, ("seq", "rows"), "col"),
            P(None, ("seq", "rows"), "col"),
            P(None, "col", ("seq", "rows")),
        ),
        check_vma=False,
    )
```

```python
import functools

import jax
import jax.numpy as jnp
import numpy as np
from jax import lax
from jax.experimental import pallas as pl
from jax.experimental.pallas import tpu as pltpu
from jax.sharding import PartitionSpec as P

HEAD_DIM = 64
SPAN = 256
MAX_REL = 512
WIDE = 640
HALF = 320
EPSILON = 1e-07
SCALE = (3.0 * HEAD_DIM) ** (-0.5)
LOG2E = 1.4426950408889634
BF = jnp.bfloat16
F32 = jnp.float32
NT = (((1,), (1,)), ((), ()))
NN = (((1,), (0,)), ((), ()))
TN = (((0,), (0,)), ((), ()))
VMEM_LIMIT = 50 << 20
NORM_ROWS = 16


def dot(a, b, dims=NN):
    return lax.dot_general(a, b, dims, preferred_element_type=F32)


def bucket_table():
    relative = HALF - np.arange(WIDE)
    middle = SPAN // 2
    absolute = np.where((relative < middle) & (relative > -middle), middle - 1, np.abs(relative))
    log_position = np.ceil(np.log(absolute / middle) / np.log((MAX_REL - 1) / middle) * (middle - 1)) + middle
    bucket = np.where(absolute <= middle, relative, log_position * np.sign(relative))
    bucket = np.clip(bucket + SPAN, 0, 2 * SPAN - 1).astype(np.int32)
    return (bucket[:, None] == np.arange(2 * SPAN)[None, :]).astype(np.float32)


def assemble(target, own, other, core, count):
    target[pl.ds(pl.multiple_of(core * count, count), count), :] = own[...]
    target[pl.ds(pl.multiple_of((1 - core) * count, count), count), :] = other[...]


class Late:
    def __init__(self, source, target, sem):
        self.target, self.copy = target, pltpu.make_async_copy(source, target, sem)
        self.copy.start()

    def get(self):
        if self.copy is not None:
            self.copy.wait()
            self.copy = None
        return self.target


class Loads:
    def __init__(self, sems):
        self.sems, self.count = sems, 0

    def __call__(self, source, target):
        self.count += 1
        return Late(source, target, self.sems.at[self.count - 1])


def rows_at(number, count):
    return pl.ds(pl.multiple_of(number * count, count), count)


def half_of(head):
    lane = lax.broadcasted_iota(jnp.int32, (1, 128), 1)
    return (lane < HEAD_DIM) if head == 0 else (lane >= HEAD_DIM)


def doc_number(position, meta_ref):
    total = jnp.zeros(position.shape, jnp.int32)
    for k in range(3):
        total = total + (position >= meta_ref[k]).astype(jnp.int32)
    return total


def skew(values, base):
    return pltpu.roll(values, base % WIDE, 1, stride=1, stride_axis=0)


def rolled(values):
    return pltpu.roll(values.astype(F32), HEAD_DIM, 1).astype(values.dtype)


def cost(microseconds):
    return pl.CostEstimate(flops=int(microseconds * 1e8), bytes_accessed=1 << 20, transcendentals=0)


def whole_block(*shape):
    return pl.BlockSpec(shape, lambda g, m: (0,) * len(shape))


def prepare_kernel(meta_ref, first_ref, second_ref, rel_ref, table_ref, *rest):
    if len(rest) > 2:
        in_ref, down_ref, w_ref, pe_ref, in_piece, down_piece = rest
        in_piece[...] = in_ref[0]
        down_piece[...] = down_ref[0]
    else:
        w_ref, pe_ref = rest
    first = meta_ref[0] == 0
    low = half_of(0)

    @pl.when(pl.program_id(0) != 1)
    def _():
        for c in range(3):
            w_ref[0, 0, :, 128 * c : 128 * (c + 1)] = first_ref[0, c]

    @pl.when(pl.program_id(0) == 1)
    def _():
        for c in range(3):
            a, b = first_ref[0, c], second_ref[0, c]
            zero = jnp.where(low, a, rolled(b))
            one = jnp.where(low, rolled(a), b)
            w_ref[0, 0, :, 128 * c : 128 * (c + 1)] = jnp.where(first, zero, one)

    pos = dot(rel_ref[0], w_ref[0, 0, :, :256]).astype(BF)
    ext = dot(table_ref[0], pos).astype(BF)
    pe_ref[0, 0, 0] = ext[:, :128]
    pe_ref[0, 0, 1] = ext[:, 128:]
    pe_ref[0, 0, 2] = dot(table_ref[1], pos[:, 128:]).astype(BF)


def prepare(place, layer, qkv_weight, rel_table, tables, ffn=()):
    hidden = ffn[0].shape[2] if ffn else 0
    rows = qkv_weight.shape[2] // 2
    kinds, model = qkv_weight.shape[1:3]
    pairs, buckets = 3, rel_table.shape[1]
    return pl.pallas_call(
        prepare_kernel,
        out_shape=(
            jax.ShapeDtypeStruct((1, pairs, model, 384), BF),
            jax.ShapeDtypeStruct((1, pairs, 3, WIDE, 128), BF),
        ) + (jax.ShapeDtypeStruct((rows, hidden), BF),) * len(ffn),
        grid_spec=pltpu.PrefetchScalarGridSpec(
            num_scalar_prefetch=1,
            grid=(pairs,),
            in_specs=[
                pl.BlockSpec(
                    (1, kinds, model, 128),
                    lambda g, m: (layer, 0, 0, jnp.where(g == 1, 1, jnp.where(g == 0, 0, 3) + 2 * m[0])),
                ),
                pl.BlockSpec((1, kinds, model, 128), lambda g, m: (layer, 0, 0, 4)),
                pl.BlockSpec((1, buckets, model), lambda g, m: (layer, 0, 0)),
                whole_block(2, WIDE, buckets),
            ] + [pl.BlockSpec((1, rows // pairs, hidden), lambda g, m: (layer + 1, pairs * m[1] + g, 0))] * len(ffn),
            out_specs=(
                pl.BlockSpec((1, 1, model, 384), lambda g, m: (0, g, 0, 0)),
                pl.BlockSpec((1, 1, 3, WIDE, 128), lambda g, m: (0, g, 0, 0, 0)),
            ) + (pl.BlockSpec((rows // pairs, hidden), lambda g, m: (g, 0)),) * len(ffn),
        ),
        compiler_params=pltpu.CompilerParams(vmem_limit_bytes=VMEM_LIMIT),
        cost_estimate=cost(5),
        name="prepare",
    )(place, qkv_weight, qkv_weight, rel_table, tables, *ffn)


def attention_kernel(
    meta_ref, own_ref, other_ref, w_ref, pe_ref, rev_ref, o_ref, sv_ref, p_hbm,
    x_ref, s_ref, t1_ref, t2_ref, bt_ref, sb_ref, pp_ref, pj_ref, sems, *, length, blk, pairs,
):
    assemble(x_ref, own_ref, other_ref, meta_ref[3], length // 2)
    zero = jnp.zeros((), BF)
    ids_j = doc_number(lax.broadcasted_iota(jnp.int32, (1, length), 1), meta_ref)
    blocks = [slice(b, b + blk) for b in range(0, length, blk)]
    copies = []

    def project(p):
        for sl in blocks:
            qkv = dot(x_ref[sl, :], w_ref[0, p]).astype(BF)
            sb_ref[p, sl, :] = qkv
            sv_ref[p, sl, :128] = qkv[:, :128]

    def reverse(p):
        for sl in blocks:
            sv_ref[p, sl, 128:] = dot(rev_ref[sl, :], sb_ref[p, :, 128:]).astype(BF)

    def key_positions(h):
        for sl in blocks:
            kb = jnp.where(half_of(h % 2), sb_ref[h // 2, sl, 128:256], zero)
            t2_ref[h % 2, sl, :] = dot(kb, pe_ref[0, h // 2, 0], NT)

    def key_skew(h):
        for sl in blocks:
            t2 = skew(t2_ref[h % 2, sl, :], sl.start + HALF)[:, :length].astype(BF)
            bt_ref[h % 2, :, sl] = t2.T

    def products(h):
        for sl in blocks:
            qb = jnp.where(half_of(h % 2), sb_ref[h // 2, sl, :128], zero)
            t1_ref[h % 2, sl, :] = dot(qb, pe_ref[0, h // 2, 1], NT)
            s_ref[h % 2, sl, :] = dot(qb, sb_ref[h // 2, :, 128:256], NT)

    def softmax(h):
        for sl in blocks:
            t1 = skew(t1_ref[h % 2, sl, :], sl.start + HALF)[:, :length]
            total = s_ref[h % 2, sl, :] + t1 + bt_ref[h % 2, sl, :].astype(F32)
            ids_i = doc_number(lax.broadcasted_iota(jnp.int32, (blk, 1), 0) + sl.start, meta_ref)
            total = jnp.where(ids_i == ids_j, total, -1e30)
            e = jnp.exp2((total - jnp.max(total, axis=1, keepdims=True)) * (SCALE * LOG2E))
            pp_ref[h % 2, sl, :] = (e * (1.0 / jnp.sum(e, axis=1, keepdims=True))).astype(BF)

    def outputs(h):
        lanes = slice(128 * (h // 2), 128 * (h // 2 + 1))
        for sl in blocks:
            o = dot(pp_ref[h % 2, sl, :], sb_ref[h // 2, :, 256:]).astype(BF)
            o_ref[sl, lanes] = o if h % 2 == 0 else jnp.where(half_of(1), o, o_ref[sl, lanes])
        if h >= 2:
            copies[h - 2].wait()
        for sl in blocks:
            pj_ref[h % 2, sl, :] = dot(pp_ref[h % 2, sl, :], rev_ref[...]).astype(BF)
        copies.append(pltpu.make_async_copy(pj_ref.at[h % 2], p_hbm.at[h], sems.at[h % 2]))
        copies[h].start()

    project(0)
    key_positions(0)
    for h in range(2 * pairs):
        products(h)
        if h > 0:
            outputs(h - 1)
        else:
            reverse(0)
        key_skew(h)
        if h + 1 < 2 * pairs:
            if h % 2 == 1:
                project((h + 1) // 2)
            key_positions(h + 1)
            if h % 2 == 1:
                reverse((h + 1) // 2)
        softmax(h)
    outputs(2 * pairs - 1)
    copies[-2].wait()
    copies[-1].wait()


def attention(meta, layer, group, own, other, w, pe, rev):
    base, pairs = group
    base //= pairs
    count, model = own.shape
    length = 2 * count
    return pl.pallas_call(
        functools.partial(attention_kernel, length=length, blk=256, pairs=pairs),
        out_shape=(
            jax.ShapeDtypeStruct((length, pairs * 128), BF),
            jax.ShapeDtypeStruct((pairs, length, 384), BF),
            jax.ShapeDtypeStruct((2 * pairs, length, length), BF),
        ),
        grid_spec=pltpu.PrefetchScalarGridSpec(
            num_scalar_prefetch=1,
            grid=(1,),
            in_specs=[
                whole_block(count, model),
                whole_block(count, model),
                pl.BlockSpec((1, pairs, model, 384), lambda g, m: (0, base, 0, 0)),
                pl.BlockSpec((1, pairs, 2, WIDE, 128), lambda g, m: (0, base, 0, 0, 0)),
                whole_block(length, length),
            ],
            out_specs=(
                whole_block(length, pairs * 128),
                whole_block(pairs, length, 384),
                pl.BlockSpec(memory_space=pl.ANY),
            ),
            scratch_shapes=[
                pltpu.VMEM((length, model), BF),
                pltpu.VMEM((2, length, length), F32),
                pltpu.VMEM((2, length, WIDE), F32),
                pltpu.VMEM((2, length, WIDE), F32),
                pltpu.VMEM((2, length, length), BF),
                pltpu.VMEM((pairs, length, 384), BF),
                pltpu.VMEM((2, length, length), BF),
                pltpu.VMEM((2, length, length), BF),
                pltpu.SemaphoreType.DMA((2,)),
            ],
        ),
        compiler_params=pltpu.CompilerParams(vmem_limit_bytes=VMEM_LIMIT),
        cost_estimate=cost(5 * pairs),
        name="attention",
    )(meta, own, other, w, pe, rev)


def head_rows(core):
    return ((256 * core, 128), (128 + 64 * core, 64), (512 + 64 * core, 64), (384 + 256 * core, 128))


def attention_grad_kernel(
    meta_ref, own_hbm, other_hbm, wo_hbm, pe_hbm, rev_hbm, w_hbm, table_hbm, *rest, layer, length, blk, base, sizes,
):
    pairs = sum(sizes)
    sv_hbm = [ref.at[k] for ref, size in zip(rest, sizes) for k in range(size)]
    p_hbm = [ref.at[k] for ref, size in zip(rest[len(sizes) :], sizes) for k in range(2 * size)]
    dqkv_ref, dpos_ref, mine_ref, theirs_ref, *rest = rest[2 * len(sizes) :]
    drb_ref, do_ref, p_ref, da_ref, ds_ref, dt_ref, u_ref, v_ref, acc_ref, dx_ref, heads_ref, *rest = rest
    sv_ref, pe_ref, rev_ref, w_ref, table_ref, loads = rest
    core = meta_ref[3]
    count = length // 2
    load = Loads(loads)
    rows = [load(own_hbm, drb_ref.at[rows_at(core, count)]), load(other_hbm, drb_ref.at[rows_at(1 - core, count)])]
    at = 0
    for start, size in head_rows(core):
        place = pl.ds(pl.multiple_of(start, 64), size)
        rows.append(load(wo_hbm.at[layer, place], heads_ref.at[pl.ds(at, size)]))
        at += size
    saved, probs = [], []
    for p in range(pairs):
        saved.append(load(sv_hbm[p], sv_ref.at[p]))
        probs += [load(p_hbm[2 * p + k], p_ref.at[2 * p + k]) for k in range(2)]
        if p == 0:
            pe = load(pe_hbm.at[0, pl.ds(base, pairs)], pe_ref)
            tables = load(table_hbm, table_ref)
            rev = load(rev_hbm, rev_ref)
            w = load(w_hbm.at[0, pl.ds(base, pairs)], w_ref)
    for item in rows:
        item.get()
    sv = [sv_ref.at[p] for p in range(pairs)]
    zero = jnp.zeros((), BF)
    pad = jnp.zeros((blk, WIDE - length), F32)
    blocks = [slice(b, b + blk) for b in range(0, length, blk)]
    half = lambda h: slice(HEAD_DIM * (h % 2), HEAD_DIM * (h % 2 + 1))

    def attended(p):
        rows = slice(128 * (base + p), 128 * (base + p + 1))
        for sl in blocks:
            do_ref[p, sl, :] = dot(drb_ref[sl, :], heads_ref[rows, :], NT).astype(BF)

    def probabilities(h):
        saved[h // 2].get()
        for sl in blocks:
            d_o = jnp.where(half_of(h % 2), do_ref[h // 2, sl, :], zero)
            da_ref[h % 2, sl, :] = dot(d_o, sv[h // 2][:, 256:], NT)

    def scores(h):
        probs[h].get()
        for sl in blocks:
            da = da_ref[h % 2, sl, :]
            p = p_ref[h, sl, :].astype(F32)
            ds = (p * (da - jnp.sum(p * da, axis=1, keepdims=True))).astype(BF)
            ds_ref[h % 2, sl, :] = ds
            dt_ref[h % 2, :, sl] = ds.T

    def query_skew(h):
        for sl in blocks:
            wide = jnp.concatenate([ds_ref[h % 2, sl, :].astype(F32), pad], axis=1)
            u_ref[h % 2, sl, :] = skew(wide, sl.start + WIDE - 192).astype(BF)

    def key_skew(h):
        for sl in blocks:
            wide = jnp.concatenate([dt_ref[h % 2, sl, :].astype(F32), pad], axis=1)
            v_ref[h % 2, sl, :] = skew(wide, sl.start + WIDE - 191).astype(BF)

    def add_to(p, sl, lanes, h, value):
        acc_ref[p % 2, sl, lanes] = value if h % 2 == 0 else acc_ref[p % 2, sl, lanes] + value

    def values(h):
        p = h // 2
        d_o = jnp.where(half_of(h % 2), do_ref[p], zero)
        add_to(p, slice(0, length), slice(256, 384), h, dot(p_ref[h], d_o, TN))

    def queries(h):
        pe.get()
        tables.get()
        p, own = h // 2, half_of(h % 2)
        kr = jnp.where(own, sv[p][:, 128:256], zero)
        pk = jnp.where(own, pe_ref[p, 2], zero)
        for sl in blocks:
            add_to(p, sl, slice(0, 128), h, dot(ds_ref[h % 2, sl, :], kr) + dot(u_ref[h % 2, sl, :], pk))
        d_ext = (dot(sv[p][:, :128].T[half(h)], u_ref[h % 2]) * SCALE).astype(BF)
        dpos_ref[p, 1, half(h), :] = dot(d_ext, table_ref[1]).astype(BF)

    def keys(h):
        p, own = h // 2, half_of(h % 2)
        q = jnp.where(own, sv[p][:, :128], zero)
        pq = jnp.where(own, pe_ref[p, 0], zero)
        for sl in blocks:
            add_to(p, sl, slice(128, 256), h, dot(dt_ref[h % 2, sl, :], q) + dot(v_ref[h % 2, sl, :], pq))
        d_ext = (dot(sv[p][:, 128:256].T[half(h)], v_ref[h % 2]) * SCALE).astype(BF)
        dpos_ref[p, 0, half(h), :] = dot(d_ext, table_ref[0]).astype(BF)

    def inputs(p):
        rev.get()
        w.get()
        acc = acc_ref[p % 2]
        dqkv_ref[p, :, :128] = (acc[:, :128] * SCALE).astype(BF)
        dkv = jnp.concatenate([(acc[:, 128:256] * SCALE).astype(BF), acc[:, 256:].astype(BF)], axis=1)
        for sl in blocks:
            dqkv_ref[p, sl, 128:] = dot(rev_ref[sl, :], dkv).astype(BF)
        for sl in blocks:
            part = dot(dqkv_ref[p, sl, :], w_ref[p], NT)
            if p > 0:
                part = part + dx_ref[sl, :]
            dx_ref[sl, :] = part

    total = 2 * pairs
    attended(0)
    probabilities(0)
    for h in range(total):
        scores(h)
        if h + 1 < total:
            if h % 2 == 1:
                attended((h + 1) // 2)
            probabilities(h + 1)
        values(h)
        query_skew(h)
        if h > 0:
            keys(h - 1)
            if h % 2 == 0:
                inputs(h // 2 - 1)
        key_skew(h)
        queries(h)
    keys(total - 1)
    inputs(pairs - 1)
    mine_ref[...] = dx_ref[rows_at(core, count), :]
    theirs_ref[...] = dx_ref[rows_at(1 - core, count), :].astype(BF)


def attention_grad(meta, layer, own, other, wo, saved, probs, pe, rev, w, tables):
    buckets = tables.shape[2]
    count, model = own.shape
    length = 2 * count
    sizes = tuple(item.shape[0] for item in saved)
    pairs = sum(sizes)
    out_shape = [
        jax.ShapeDtypeStruct((pairs, length, 384), BF),
        jax.ShapeDtypeStruct((pairs, 2, 128, buckets), BF),
        jax.ShapeDtypeStruct((count, model), F32),
        jax.ShapeDtypeStruct((count, model), BF),
    ]
    return pl.pallas_call(
        functools.partial(attention_grad_kernel, layer=layer, length=length, blk=256, base=0, sizes=sizes),
        out_shape=out_shape,
        grid_spec=pltpu.PrefetchScalarGridSpec(
            num_scalar_prefetch=1,
            grid=(1,),
            in_specs=[pl.BlockSpec(memory_space=pl.ANY)] * (7 + 2 * len(sizes)),
            out_specs=[whole_block(*item.shape) for item in out_shape],
            scratch_shapes=[
                pltpu.VMEM((length, model), BF),
                pltpu.VMEM((pairs, length, 128), BF),
                pltpu.VMEM((2 * pairs, length, length), BF),
                pltpu.VMEM((2, length, length), F32),
                pltpu.VMEM((2, length, length), BF),
                pltpu.VMEM((2, length, length), BF),
                pltpu.VMEM((2, length, WIDE), BF),
                pltpu.VMEM((2, length, WIDE), BF),
                pltpu.VMEM((2, length, 384), F32),
                pltpu.VMEM((length, model), F32),
                pltpu.VMEM((model // 2, model), BF),
                pltpu.VMEM((pairs, length, 384), BF),
                pltpu.VMEM((pairs, 3, WIDE, 128), BF),
                pltpu.VMEM((length, length), BF),
                pltpu.VMEM((pairs, model, 384), BF),
                pltpu.VMEM((2, WIDE, buckets), BF),
                pltpu.SemaphoreType.DMA((10 + 3 * pairs,)),
            ],
        ),
        compiler_params=pltpu.CompilerParams(vmem_limit_bytes=VMEM_LIMIT),
        cost_estimate=cost(6 * pairs),
        name="attention_grad",
    )(meta, own, other, wo, pe, rev, w, tables, *saved, *probs)


def pieces_kernel(meta_ref, in_ref, down_ref, in_piece, down_piece):
    in_piece[...] = in_ref[0]
    down_piece[...] = down_ref[0]


def weight_pieces(seq, layer, ffn_in, ffn_out):
    model, hidden = ffn_in.shape[1:]
    rows = model // 2
    steps = 1
    return pl.pallas_call(
        pieces_kernel,
        out_shape=[jax.ShapeDtypeStruct((rows, hidden), BF)] * 2,
        grid_spec=pltpu.PrefetchScalarGridSpec(
            num_scalar_prefetch=1,
            grid=(steps,),
            in_specs=[pl.BlockSpec((1, rows // steps, hidden), lambda g, m: (layer, steps * m[0] + g, 0))] * 2,
            out_specs=[pl.BlockSpec((rows // steps, hidden), lambda g, m: (g, 0))] * 2,
        ),
        cost_estimate=cost(1),
        name="weight_pieces",
    )(seq[None], ffn_in, ffn_out)


def weight_copies(layer, refs, scratch, sems, meta_ref):
    shards = []
    for s in range(4):
        group = []
        for m in range(2):
            own, core_own, near, far, core_near, core_far = refs[m]
            place = scratch.at[m, s]
            if s < 2:
                group.append(((own if s == 0 else core_own).at[layer], place))
            else:
                first, second = (near, far) if s == 2 else (core_near, core_far)
                rows = first.shape[0]
                one = pl.multiple_of(meta_ref[4] * rows, rows)
                two = pl.multiple_of((1 - meta_ref[4]) * rows, rows)
                group.append((first, place.at[pl.ds(one, rows)]))
                group.append((second, place.at[pl.ds(two, rows)]))
        shards.append(group)
    copies, k = [], 0
    for group in shards:
        made = []
        for source, target in group:
            made.append(pltpu.make_async_copy(source, target, sems.at[k]))
            k += 1
        copies.append(made)
    return copies


COPIES = 12


def row_norm(state, gain, bias):
    centered = state - jnp.mean(state, axis=1, keepdims=True)
    inverse = lax.rsqrt(jnp.mean(centered * centered, axis=1, keepdims=True) + EPSILON)
    return centered * inverse * gain + bias


def row_norm_grad(state, gain, d_result):
    centered = state - jnp.mean(state, axis=1, keepdims=True)
    inverse = lax.rsqrt(jnp.mean(centered * centered, axis=1, keepdims=True) + EPSILON)
    unit = centered * inverse
    d_unit = d_result * gain
    d_state = inverse * (
        d_unit
        - jnp.mean(d_unit, axis=1, keepdims=True)
        - unit * jnp.mean(d_unit * unit, axis=1, keepdims=True)
    )
    return d_state, jnp.sum(d_result * unit, axis=0, keepdims=True), jnp.sum(d_result, axis=0, keepdims=True)


def tokens_kernel(meta_ref, *rest, layer, chunk, groups):
    o_refs, rest = rest[: 2 * groups], rest[2 * groups :]
    x_ref, wo_ref, norm_ref, *rest = rest
    wires, rest = rest[:12], rest[12:]
    y_ref, yb_ref, mb_ref, resid_ref, pre_ref, slope_ref, scratch, sems, heads = rest
    copies = weight_copies(layer, (wires[:6], wires[6:]), scratch, sems, meta_ref)
    for group in copies:
        for item in group:
            item.start()
    at = 0
    for core in (meta_ref[3], 1 - meta_ref[3]):
        for first, size in head_rows(core):
            heads[at : at + size] = wo_ref[0, pl.ds(pl.multiple_of(first, 64), size), :]
            at += size
    resid = x_ref[...].astype(F32) + dot(jnp.concatenate([o[...] for o in o_refs], axis=1), heads[...])
    resid_ref[...] = resid
    middle = row_norm(resid, norm_ref[0:1, :], norm_ref[1:2, :])
    mb = middle.astype(BF)
    mb_ref[...] = mb
    pre_ref[...] = middle
    hidden = scratch.shape[3]
    per = hidden // chunk
    total = 4 * per

    def up(k):
        s, c = k // per, k % per
        if c == 0:
            for item in copies[s]:
                item.wait()
        return dot(mb, scratch[0, s, :, c * chunk : (c + 1) * chunk])

    ahead = up(0)
    for k in range(total):
        s, c = k // per, k % per
        h = ahead
        if k + 1 < total:
            ahead = up(k + 1)
        cumulative = 0.5 * (1.0 + lax.erf(h * 0.7071067811865476))
        density = jnp.exp(-0.5 * h * h) * 0.3989422804014327
        slope_ref[:, k * chunk : (k + 1) * chunk] = (cumulative + h * density).astype(BF)
        act = (h * cumulative).astype(BF)
        pre_ref[...] = pre_ref[...] + dot(act, scratch[1, s, :, c * chunk : (c + 1) * chunk], NT)
    y = row_norm(pre_ref[...], norm_ref[2:3, :], norm_ref[3:4, :])
    y_ref[...] = y
    yb_ref[...] = y.astype(BF)


def token_step(meta, layer, o_own, o_other, x, wo, norms, wires):
    count, model = x.shape
    hidden = wires[0].shape[2]
    mine = [pl.BlockSpec((count, o.shape[1]), lambda g, m: (m[3], 0)) for o in o_own + o_other]
    hbm = pl.BlockSpec(memory_space=pl.ANY)
    return pl.pallas_call(
        functools.partial(tokens_kernel, layer=layer, chunk=768, groups=len(o_own)),
        out_shape=(
            jax.ShapeDtypeStruct((count, model), F32),
            jax.ShapeDtypeStruct((count, model), BF),
            jax.ShapeDtypeStruct((count, model), BF),
            jax.ShapeDtypeStruct((count, model), F32),
            jax.ShapeDtypeStruct((count, model), F32),
            jax.ShapeDtypeStruct((count, 4 * hidden), BF),
        ),
        grid_spec=pltpu.PrefetchScalarGridSpec(
            num_scalar_prefetch=1,
            grid=(1,),
            in_specs=mine + [
                whole_block(count, model),
                pl.BlockSpec((1, model, model), lambda g, m: (layer, 0, 0)),
                whole_block(4, model),
            ] + [hbm] * 12,
            out_specs=(
                whole_block(count, model), whole_block(count, model), whole_block(count, model), whole_block(count, model), whole_block(count, model),
                whole_block(count, 4 * hidden),
            ),
            scratch_shapes=[
                pltpu.VMEM((2, 4, model, hidden), BF),
                pltpu.SemaphoreType.DMA((COPIES,)),
                pltpu.VMEM((model, model), BF),
            ],
        ),
        compiler_params=pltpu.CompilerParams(vmem_limit_bytes=VMEM_LIMIT),
        cost_estimate=cost(10),
        name="token_step",
    )(meta, *o_own, *o_other, x, wo, norms, *wires)


def tokens_grad_kernel(meta_ref, *rest, layer, chunk, parts):
    ups, rest = rest[:parts], rest[parts:]
    pre_ref, resid_ref, slope_ref, norm_ref, *rest = rest
    wires, rest = rest[:12], rest[12:]
    df_ref, dr_ref, drb_ref, scratch, sems, dm_ref, dn_ref = rest
    count = dm_ref.shape[0]
    copies = weight_copies(layer, (wires[:6], wires[6:]), scratch, sems, meta_ref)
    for group in copies:
        for item in group:
            item.start()
    dy = ups[0][...].astype(F32)
    for item in ups[1:]:
        dy = dy + item[...].astype(F32)
    dz, dg2, db2 = row_norm_grad(pre_ref[...], norm_ref[2:3, :], dy)
    df = dz.astype(BF)
    df_ref[:count, :] = df
    dm_ref[...] = dz
    hidden = scratch.shape[3]
    per = hidden // chunk
    total = 4 * per

    def down(k):
        s, c = k // per, k % per
        if c == 0:
            for item in copies[s]:
                item.wait()
        return dot(df, scratch[1, s, :, c * chunk : (c + 1) * chunk])

    ahead = down(0)
    for k in range(total):
        s, c = k // per, k % per
        dg = ahead
        if k + 1 < total:
            ahead = down(k + 1)
        dh = (dg * slope_ref[:, k * chunk : (k + 1) * chunk].astype(F32)).astype(BF)
        dm_ref[...] = dm_ref[...] + dot(dh, scratch[0, s, :, c * chunk : (c + 1) * chunk], NT)
    dr, dg1, db1 = row_norm_grad(resid_ref[...], norm_ref[0:1, :], dm_ref[...])
    dr_ref[...] = dr
    drb_ref[...] = dr.astype(BF)
    norm_rows(dn_ref, df_ref, count, (dg1, db1, dg2, db2))


def token_grad(meta, layer, ups, pre, resid, slope, norms, wires):
    count, model = pre.shape
    hidden = wires[0].shape[2]
    hbm = pl.BlockSpec(memory_space=pl.ANY)
    return pl.pallas_call(
        functools.partial(tokens_grad_kernel, layer=layer, chunk=768, parts=len(ups)),
        out_shape=(
            jax.ShapeDtypeStruct((count + NORM_ROWS, model), BF),
            jax.ShapeDtypeStruct((count, model), F32),
            jax.ShapeDtypeStruct((count, model), BF),
        ),
        grid_spec=pltpu.PrefetchScalarGridSpec(
            num_scalar_prefetch=1,
            grid=(1,),
            in_specs=[whole_block(count, model)] * len(ups)
            + [whole_block(count, model), whole_block(count, model), whole_block(count, 4 * hidden), whole_block(4, model)]
            + [hbm] * 12,
            out_specs=(whole_block(count + NORM_ROWS, model), whole_block(count, model), whole_block(count, model)),
            scratch_shapes=[
                pltpu.VMEM((2, 4, model, hidden), BF),
                pltpu.SemaphoreType.DMA((COPIES,)),
                pltpu.VMEM((count, model), F32),
                pltpu.VMEM((NORM_ROWS, model), F32),
            ],
        ),
        compiler_params=pltpu.CompilerParams(vmem_limit_bytes=VMEM_LIMIT),
        cost_estimate=cost(10),
        name="token_grad",
    )(meta, *ups, pre, resid, slope, norms, *wires)


def tokens_both_kernel(meta_ref, *rest, layer, chunk, groups):
    o_refs, rest = rest[: 2 * groups], rest[2 * groups :]
    x_ref, wo_ref, norm_ref, up_ref, *rest = rest
    wires, rest = rest[:12], rest[12:]
    y_ref, mb_ref, df_ref, dr_ref, drb_ref, scratch, sems, heads, pre_ref, slope_ref, dn_ref = rest
    copies = weight_copies(layer, (wires[:6], wires[6:]), scratch, sems, meta_ref)
    for group in copies:
        for item in group:
            item.start()
    at = 0
    for core in (meta_ref[3], 1 - meta_ref[3]):
        for first, size in head_rows(core):
            heads[at : at + size] = wo_ref[0, pl.ds(pl.multiple_of(first, 64), size), :]
            at += size
    resid = x_ref[...].astype(F32) + dot(jnp.concatenate([o[...] for o in o_refs], axis=1), heads[...])
    dr_ref[...] = resid
    middle = row_norm(resid, norm_ref[0:1, :], norm_ref[1:2, :])
    mb = middle.astype(BF)
    mb_ref[...] = mb
    pre_ref[...] = middle
    count, hidden = resid.shape[0], scratch.shape[3]
    per = hidden // chunk
    total = 4 * per

    def up(k):
        s, c = k // per, k % per
        if c == 0:
            for item in copies[s]:
                item.wait()
        return dot(mb, scratch[0, s, :, c * chunk : (c + 1) * chunk])

    ahead = up(0)
    for k in range(total):
        s, c = k // per, k % per
        h = ahead
        if k + 1 < total:
            ahead = up(k + 1)
        cumulative = 0.5 * (1.0 + lax.erf(h * 0.7071067811865476))
        density = jnp.exp(-0.5 * h * h) * 0.3989422804014327
        slope_ref[:, k * chunk : (k + 1) * chunk] = (cumulative + h * density).astype(BF)
        act = (h * cumulative).astype(BF)
        pre_ref[...] = pre_ref[...] + dot(act, scratch[1, s, :, c * chunk : (c + 1) * chunk], NT)
    y_ref[...] = row_norm(pre_ref[...], norm_ref[2:3, :], norm_ref[3:4, :])
    dz, dg2, db2 = row_norm_grad(pre_ref[...], norm_ref[2:3, :], up_ref[...].astype(F32))
    df = dz.astype(BF)
    df_ref[:count, :] = df
    pre_ref[...] = dz

    def down(k):
        s, c = k // per, k % per
        return dot(df, scratch[1, s, :, c * chunk : (c + 1) * chunk])

    ahead = down(0)
    for k in range(total):
        s, c = k // per, k % per
        dg = ahead
        if k + 1 < total:
            ahead = down(k + 1)
        dh = (dg * slope_ref[:, k * chunk : (k + 1) * chunk].astype(F32)).astype(BF)
        pre_ref[...] = pre_ref[...] + dot(dh, scratch[0, s, :, c * chunk : (c + 1) * chunk], NT)
    dr, dg1, db1 = row_norm_grad(dr_ref[...], norm_ref[0:1, :], pre_ref[...])
    dr_ref[...] = dr
    drb_ref[...] = dr.astype(BF)
    norm_rows(dn_ref, df_ref, count, (dg1, db1, dg2, db2))


def norm_rows(dn_ref, df_ref, count, sums):
    dn_ref[...] = jnp.zeros_like(dn_ref)
    for k, row in enumerate(sums):
        high = row.astype(BF)
        dn_ref[k : k + 1, :] = high.astype(F32)
        dn_ref[4 + k : 5 + k, :] = row - high.astype(F32)
    df_ref[count:, :] = dn_ref[...].astype(BF)


def token_both(meta, layer, o_own, o_other, x, wo, norms, d_out, wires):
    count, model = x.shape
    hidden = wires[0].shape[2]
    mine = [pl.BlockSpec((count, o.shape[1]), lambda g, m: (m[3], 0)) for o in o_own + o_other]
    hbm = pl.BlockSpec(memory_space=pl.ANY)
    out_shape = [
        jax.ShapeDtypeStruct((count, model), F32),
        jax.ShapeDtypeStruct((count, model), BF),
        jax.ShapeDtypeStruct((count + NORM_ROWS, model), BF),
        jax.ShapeDtypeStruct((count, model), F32),
        jax.ShapeDtypeStruct((count, model), BF),
    ]
    return pl.pallas_call(
        functools.partial(tokens_both_kernel, layer=layer, chunk=768, groups=len(o_own)),
        out_shape=out_shape,
        grid_spec=pltpu.PrefetchScalarGridSpec(
            num_scalar_prefetch=1,
            grid=(1,),
            in_specs=mine + [
                whole_block(count, model),
                pl.BlockSpec((1, model, model), lambda g, m: (layer, 0, 0)),
                whole_block(4, model),
                whole_block(count, model),
            ] + [hbm] * 12,
            out_specs=[whole_block(*item.shape) for item in out_shape],
            scratch_shapes=[
                pltpu.VMEM((2, 4, model, hidden), BF),
                pltpu.SemaphoreType.DMA((COPIES,)),
                pltpu.VMEM((model, model), BF),
                pltpu.VMEM((count, model), F32),
                pltpu.VMEM((count, 4 * hidden), BF),
                pltpu.VMEM((NORM_ROWS, model), F32),
            ],
        ),
        compiler_params=pltpu.CompilerParams(vmem_limit_bytes=VMEM_LIMIT),
        cost_estimate=cost(16),
        name="token_both",
    )(meta, *o_own, *o_other, x, wo, norms, d_out, *wires)


def hidden_grad_kernel(meta_ref, *refs):
    m_refs, d_refs = refs[:4], refs[4:8]
    wi_ref, wd_ref, keep_ref, give_ref, down_keep, down_give, m_ref, d_ref, mt_ref, dt_ref = refs[8:]
    per = keep_ref.shape[1]
    chunk = wi_ref.shape[2]

    bit, seq = meta_ref[6], meta_ref[4]

    @pl.when(pl.program_id(0) == 0)
    def _():
        for sources, target, transposed, second in ((m_refs, m_ref, mt_ref, False), (d_refs, d_ref, dt_ref, True)):
            for k, source in enumerate(sources):
                count = m_refs[0].shape[0]
                target[k * count : (k + 1) * count, :] = source[:count, :]
                turned = source[:count, :].T
                for n in range(8):
                    s, low = n // 4, n % 2
                    number = 4 * jnp.abs(low - bit) + n // 2 if second else 4 * jnp.abs(s - seq) + n % 4
                    place = pl.ds(pl.multiple_of(number * per, per), per)
                    transposed[place, k * count : (k + 1) * count] = turned[n * per : (n + 1) * per]

    kind = 2 * meta_ref[5] + meta_ref[3]
    count = m_refs[0].shape[0]
    rows = jnp.zeros((NORM_ROWS, d_refs[0].shape[1]), F32)
    for source in d_refs:
        rows = rows + source[count:, :].astype(F32)
    number = lax.broadcasted_iota(jnp.int32, rows.shape, 0)
    norm = jnp.sum(jnp.where((number == kind) | (number == kind + 4), rows, 0.0), axis=0, keepdims=True)
    high = norm.astype(BF).astype(F32)
    norm = jnp.where(lax.broadcasted_iota(jnp.int32, rows.shape, 0) == 0, high, norm - high).astype(BF)

    h = dot(m_ref[...], wi_ref[0])
    cumulative = 0.5 * (1.0 + lax.erf(h * 0.7071067811865476))
    density = jnp.exp(-0.5 * h * h) * 0.3989422804014327
    act = (h * cumulative).astype(BF)
    dh = (dot(d_ref[...], wd_ref[0]) * (cumulative + h * density)).astype(BF)
    half = mt_ref.shape[0] // 2
    for which, (first_out, second_out) in enumerate(((keep_ref, down_keep), (give_ref, down_give))):
        gi = dot(mt_ref[which * half : (which + 1) * half, :], dh).astype(BF)
        gd = dot(dt_ref[which * half : (which + 1) * half, :], act).astype(BF)
        for n in range(4):
            rows = slice(n * per, (n + 1) * per)
            first_out[n] = gi[rows]
            second_out[n // 2, n % 2, :per, :] = gd[rows]
            at = 2 * n * per
            even, odd = norm[:, at : at + per], norm[:, at + per : at + 2 * per]
            piece = jnp.where(bit == which, even.astype(F32), odd.astype(F32)).astype(BF)
            piece = jnp.concatenate([piece, jnp.zeros((NORM_ROWS, 128 - per), BF)], axis=1)
            second_out[n // 2, n % 2, per:, :] = jnp.concatenate([piece] * (chunk // 128), axis=1)


def hidden_grad(meta, layer, rows, d_rows, w_in, w_down):
    count, model = rows[0].shape
    hidden = w_in.shape[2]
    chunk = 256
    shape = (4, model // 8, hidden)
    down = (2, 2, model // 8 + NORM_ROWS, hidden)
    return pl.pallas_call(
        hidden_grad_kernel,
        out_shape=[jax.ShapeDtypeStruct(shape, BF)] * 2 + [jax.ShapeDtypeStruct(down, BF)] * 2,
        grid_spec=pltpu.PrefetchScalarGridSpec(
            num_scalar_prefetch=1,
            grid=(hidden // chunk,),
            in_specs=[whole_block(*a.shape) for a in (*rows, *d_rows)] + [
                pl.BlockSpec((1, model, chunk), lambda g, m: (layer, 0, g)),
                pl.BlockSpec((1, model, chunk), lambda g, m: (layer, 0, g)),
            ],
            out_specs=[pl.BlockSpec(shape[:2] + (chunk,), lambda g, m: (0, 0, g))] * 2
            + [pl.BlockSpec(down[:3] + (chunk,), lambda g, m: (0, 0, 0, g))] * 2,
            scratch_shapes=[pltpu.VMEM((4 * count, model), BF)] * 2 + [pltpu.VMEM((model, 4 * count), BF)] * 2,
        ),
        compiler_params=pltpu.CompilerParams(vmem_limit_bytes=VMEM_LIMIT),
        cost_estimate=cost(10),
        name="hidden_grad",
    )(meta, *rows, *d_rows, w_in, w_down)


def projection_grad_kernel(
    meta_ref, x_own_ref, x_other_ref, d_own_ref, d_other_ref, *rest, length, chunks, pairs, groups, grads,
):
    lists = []
    for size in (groups, groups, grads[0], grads[1], grads[1]):
        lists.append(rest[:size])
        rest = rest[size:]
    o_own = [o.at[:, 128 * k : 128 * (k + 1)] for o in lists[0] for k in range(o.shape[1] // 128)]
    o_other = [o.at[:, 128 * k : 128 * (k + 1)] for o in lists[1] for k in range(o.shape[1] // 128)]
    dqkv, dpos, dpos_other = ([r.at[k] for r in part for k in range(r.shape[0])] for part in lists[2:])
    rel_ref, wq_ref, wk_ref, a_keep, a_give, b_keep, b_give, *rest = rest
    x_ref, d_ref, left_ref, out_ref, right_ref, pos_ref, w_ref = rest
    core = meta_ref[3]
    seq = meta_ref[4]
    y_own = meta_ref[5]
    count = length // 2
    model = x_ref.shape[1]
    buckets = rel_ref.shape[1]
    low = half_of(0)
    zero = jnp.zeros((), BF)
    assemble(x_ref, x_own_ref, x_other_ref, core, count)
    assemble(d_ref, d_own_ref, d_other_ref, core, count)
    left_ref[:, :length] = x_ref[...].T
    left_ref[:, length:] = rel_ref[0].T
    for place, o, dp in ((core, o_own, dpos), (1 - core, o_other, dpos_other)):
        at = 0
        for first, size in head_rows(place):
            rows = pl.ds(pl.multiple_of(first, 64), size)
            p, inner = at // 128, at % 128
            if inner == 0:
                o_t = o[p][...].T
            out_ref[rows, :] = o_t[inner : inner + size]
            for c in range(2):
                pos_ref[c, rows, :] = dp[p][c, inner : inner + size, :]
            at += size
    per = model // chunks
    first_core = core == 0
    half_chunks = chunks // 2
    tile = lambda c, p: dqkv[p][:, 128 * c : 128 * (c + 1)]
    own_pos = [[dpos[p][c].astype(F32).T.astype(BF) for p in range(pairs)] for c in range(2)]
    at = 0
    for first, size in head_rows(core):
        rows = pl.ds(pl.multiple_of(first, 64), size)
        w_ref[0, at : at + size, :] = wq_ref[0, 0, rows, :]
        w_ref[1, at : at + size, :] = wk_ref[0, 0, rows, :]
        at += size
    back = (dot(w_ref[0], pos_ref[0]) + dot(w_ref[1], pos_ref[1])).T
    share = buckets // chunks
    for y in range(2):
        full = 0 if y == 0 else 2
        if y == 0:
            mixed = lambda q, k: jnp.where(low, q, rolled(k))
            v_mix = jnp.where(low, tile(2, 1), zero)
        else:
            mixed = lambda q, k: jnp.where(low, rolled(q), k)
            v_mix = jnp.where(low, rolled(tile(2, 1)), zero)
        right_ref[:length, 0:128] = tile(0, full)
        right_ref[:length, 128:256] = tile(1, full)
        right_ref[:length, 256:384] = mixed(tile(0, 1), tile(1, 1))
        right_ref[length:, 0:128] = own_pos[0][full]
        right_ref[length:, 128:256] = own_pos[1][full]
        right_ref[length:, 256:384] = mixed(own_pos[0][1], own_pos[1][1])
        base = 384 * y
        t0, t1, t2 = (d_ref[:, base + 128 * k : base + 128 * (k + 1)] for k in range(3))
        of = jnp.where(first_core, t0, t2)
        om = jnp.where(low, zero, jnp.where(first_core, rolled(t1), t1))
        one = dot(left_ref[...], right_ref[...])
        two = dot(left_ref[:, :length], jnp.concatenate([tile(2, full), v_mix], axis=1))
        three = dot(out_ref[...], jnp.concatenate([om, of], axis=1))
        rel_full = back[:, 128 * full : 128 * (full + 1)]
        rel_rest = back[:, 128:256] if y == 0 else pltpu.roll(back[:, 128:256], HEAD_DIM, 1)

        def store_a(ref, n, keep):
            rows = slice(n * per, (n + 1) * per)
            ref[keep, :per, :] = one[rows].astype(BF)
            for k in range(3):
                part = slice(n * share + 16 * k, n * share + 16 * (k + 1))
                ref[keep, per:, 128 * k : 128 * (k + 1)] = rel_full[part].astype(BF)

        def store_b(ref, n, keep):
            rows = slice(n * per, (n + 1) * per)
            ref[keep, :per, 0:128] = two[rows, :128].astype(BF)
            ref[keep, :per, 128:256] = (two[rows, 128:] + three[rows, :128]).astype(BF)
            ref[keep, :per, 256:384] = three[rows, 128:].astype(BF)
            ref[keep, per:, 0:128] = rel_full[n * share + 48 : (n + 1) * share].astype(BF)
            for k in range(2):
                a = rel_rest[n * share + 32 * k : n * share + 32 * k + 16]
                b = rel_rest[n * share + 32 * k + 16 : n * share + 32 * k + 32]
                ref[keep, per:, 128 * (k + 1) : 128 * (k + 2)] = jnp.where(low, a, pltpu.roll(b, HEAD_DIM, 1)).astype(BF)

        @pl.when(y_own == y)
        def _():
            for n in range(chunks):
                store_a(a_keep, n, n)

        @pl.when(y_own != y)
        def _():
            for n in range(chunks):
                store_a(a_give, n, n)

        for s in range(2):
            @pl.when(seq == s)
            def _():
                for n in range(chunks):
                    kept = n // half_chunks == s
                    store_b((b_keep if kept else b_give).at[y], n, n % half_chunks)


def projection_grad(meta, layer, x_own, x_other, dqkv, o_own, o_other, d_own, d_other, dpos, dpos_other, rel, qkv_weight):
    count, model = x_own.shape
    length = 2 * count
    buckets = rel.shape[1]
    chunks = 8
    rows = model // chunks + 16
    args = (x_own, x_other, d_own, d_other, *o_own, *o_other, *dqkv, *dpos, *dpos_other)
    return pl.pallas_call(
        functools.partial(
            projection_grad_kernel, length=length, chunks=chunks, pairs=3, groups=len(o_own), grads=(len(dqkv), len(dpos))
        ),
        out_shape=[jax.ShapeDtypeStruct((chunks, rows, model // 2), BF)] * 2
        + [jax.ShapeDtypeStruct((2, chunks // 2, rows, model // 2), BF)] * 2,
        grid_spec=pltpu.PrefetchScalarGridSpec(
            num_scalar_prefetch=1,
            grid=(1,),
            in_specs=[whole_block(*a.shape) for a in args]
            + [
                pl.BlockSpec((1, buckets, model), lambda g, m: (layer, 0, 0)),
                pl.BlockSpec((1, 1, model, model), lambda g, m: (layer, 0, 0, 0)),
                pl.BlockSpec((1, 1, model, model), lambda g, m: (layer, 1, 0, 0)),
            ],
            out_specs=[whole_block(chunks, rows, model // 2)] * 2 + [whole_block(2, chunks // 2, rows, model // 2)] * 2,
            scratch_shapes=[
                pltpu.VMEM((length, model), BF),
                pltpu.VMEM((length, model), BF),
                pltpu.VMEM((model, length + buckets), BF),
                pltpu.VMEM((model, length), BF),
                pltpu.VMEM((length + buckets, 384), BF),
                pltpu.VMEM((2, model, buckets), BF),
                pltpu.VMEM((2, 384, model), BF),
            ],
        ),
        compiler_params=pltpu.CompilerParams(vmem_limit_bytes=VMEM_LIMIT),
        cost_estimate=cost(10),
        name="projection_grad",
    )(meta, *args, rel, qkv_weight, qkv_weight)


class Wires:
    def __init__(self):
        self.seqs, self.rows, self.cols = (lax.axis_size(name) for name in ("seq", "rows", "col"))
        self.seq, self.row, self.col = (lax.axis_index(name) for name in ("seq", "rows", "col"))
        self.core, self.y = self.col % 2, self.col // 2

    def send(self, array, target):
        pairs = []
        for s in range(self.seqs):
            for r in range(self.rows):
                for c in range(self.cols):
                    t = target(s, r, c)
                    pairs.append(((s * self.rows + r) * self.cols + c, (t[0] * self.rows + t[1]) * self.cols + t[2]))
        return lax.ppermute(array, ("seq", "rows", "col"), pairs)

    def turn(self, array):
        return self.send(array, lambda s, r, c: (c % 2, r, c - c % 2 + s))

    def to_core(self, array):
        return self.send(array, lambda s, r, c: (s, r, c ^ 1))

    def to_y(self, array):
        return self.send(array, lambda s, r, c: (s, r, c ^ 2))

    def to_seq(self, array):
        return self.send(array, lambda s, r, c: (1 - s, r, c))

    def to_row(self, array, bit):
        return self.send(array, lambda s, r, c: (s, r ^ (1 << bit), c))


def cut(array, axis, mine):
    shape = array.shape
    pairs = array.reshape(shape[:axis] + (shape[axis] // 2, 2) + shape[axis + 1 :])
    return pick(pairs, axis + 1, mine), pick(pairs, axis + 1, 1 - mine)


def bits_of(count):
    return count.bit_length() - 1


def add(a, b):
    return (a.astype(F32) + b.astype(F32)).astype(a.dtype)


def pick(array, axis, index):
    return lax.dynamic_index_in_dim(array, index, axis, keepdims=False)


def unpack(main, rel, wires):
    t = [main[:, 128 * k : 128 * (k + 1)] for k in range(6)]
    full = [t[0], t[1], t[3], t[5], rel[:, :128]]
    rest = [t[2][:, :64], t[2][:, 64:], t[4][:, :64], t[4][:, 64:], rel[:, 128:]]
    out = []
    for f, r in zip(full, rest):
        out.append(jnp.where(wires.core == 0, jnp.concatenate([f, r], 1), jnp.concatenate([r, f], 1)).astype(F32))
    return out


def after(arrays, *earlier):
    return lax.optimization_barrier((arrays, earlier))[0]


def finer(parts, wires):
    for bit in reversed(range(bits_of(wires.rows) - 2)):
        mine = (wires.row >> bit) & 1
        sums = []
        for v in parts:
            v = v.reshape((2, v.shape[0] // 2) + v.shape[1:])
            sums.append(add(pick(v, 0, mine), wires.to_row(pick(v, 0, 1 - mine), bit)))
        parts = sums
    return parts


def first_flow(keep, give, wires):
    got = yield [(wires.to_seq, give)]
    total = add(keep, got[0])
    low = bits_of(wires.rows) - 2
    for bit in (low, low + 1):
        keep, give = cut(total, 0, (wires.row >> bit) & 1)
        got = yield [(functools.partial(wires.to_row, bit=bit), give)]
        total = add(keep, got[0])
    return finer([total[0]], wires)[0].astype(F32)


def second_flow(keep, give, wires):
    low = bits_of(wires.rows) - 2
    got = yield [(functools.partial(wires.to_row, bit=low), give)]
    keep, give = cut(add(keep, got[0]), 1, (wires.row >> (low + 1)) & 1)
    got = yield [(functools.partial(wires.to_row, bit=low + 1), give)]
    total = add(keep, got[0])[:, 0]
    got = yield [(wires.to_seq, pick(total, 0, 1 - wires.seq))]
    total = add(pick(total, 0, wires.seq), got[0])
    per = total.shape[0] - NORM_ROWS
    down, norm = finer([total[:per], total[per : per + 2, :per].T], wires)
    norm = norm.astype(F32)
    return down.astype(F32), norm[:, 0] + norm[:, 1]


def projection_flow(a_keep, a_give, b_keep, b_give, wires):
    got = yield [(wires.to_y, a_give), (wires.to_seq, b_give)]
    a = add(a_keep, got[0]).reshape((2, 4) + a_keep.shape[1:])
    b = add(b_keep, got[1])
    got = yield [(wires.to_seq, pick(a, 0, 1 - wires.seq)), (wires.to_y, pick(b, 0, 1 - wires.y))]
    both = jnp.stack([add(pick(a, 0, wires.seq), got[0]), add(pick(b, 0, wires.y), got[1])])
    low = bits_of(wires.rows) - 2
    for bit in (low, low + 1):
        keep, give = cut(both, 1, (wires.row >> bit) & 1)
        got = yield [(functools.partial(wires.to_row, bit=bit), give)]
        both = add(keep, got[0])
    both = both[:, 0]
    main = jnp.concatenate([both[0, :-16], both[1, :-16]], axis=1)
    tail = jnp.concatenate([both[0, -16:], both[1, -16:]], axis=1)
    full = jnp.concatenate([tail[:, 128 * k : 128 * (k + 1)] for k in range(4)], axis=0)
    rest = jnp.concatenate([tail[:, 512 + 64 * k : 576 + 64 * k] for k in range(4)], axis=0)
    rel = jnp.concatenate([full, rest], axis=1)
    main, rel = finer([main, rel], wires)
    return unpack(main, rel, wires)


class Flow:
    def __init__(self, steps):
        self.steps, self.value = steps, None
        self.take(next(steps))

    def take(self, sends):
        self.ready = [array for _, array in sends]
        self.under_way = [send(array) for send, array in sends]

    def step(self, *earlier):
        if self.under_way is None:
            return
        arrived = after(self.under_way, earlier) if earlier else self.under_way
        try:
            self.take(self.steps.send(arrived))
        except StopIteration as stop:
            self.ready, self.under_way, self.value = stop.value, None, stop.value

    def finish(self, *earlier):
        while self.under_way is not None:
            self.step(*earlier)
        return self.value


def gather_start(rows, wires):
    return rows, wires.to_core(rows), wires.to_y(rows)


def gather_end(gathered, wires, *earlier):
    rows, other, far = gathered
    return rows, other, far, wires.to_core(after(far, earlier))


def per_device(tokens, lengths, qkv_weight, out_weight, rel_table, ffn_in, ffn_out, norm_params, cotangent):
    wires = Wires()
    core = wires.core
    count, model = tokens.shape[1:]
    length = 2 * count
    layers = qkv_weight.shape[0]
    table_np = bucket_table()
    tables = jnp.asarray(np.stack([table_np, table_np[::-1]]), BF)
    rev = jnp.asarray(np.eye(length)[::-1], BF)
    split = [(0, 2), (2, 1)]

    weights = (ffn_in, ffn_out)
    near, far, core_near, core_far = ([[None, None], [None, None]] for _ in range(4))
    core_own = [None, None]
    start = wires.turn(tokens[0])
    other_lengths = wires.to_core(lengths)
    pieces = [weight_pieces(wires.seq, 0, ffn_in, ffn_out), None]
    done = (pieces[0], start, other_lengths)
    lengths = jnp.where(core == wires.seq, lengths, after(other_lengths, done))
    ends = jnp.cumsum(lengths[0]).astype(jnp.int32)
    low_bit = (wires.row >> (bits_of(wires.rows) - 2)) & 1
    meta = jnp.concatenate([ends[:3], jnp.stack([core, wires.seq, wires.y, low_bit])]).astype(jnp.int32)
    xb = start
    near[0] = [wires.to_y(after(piece, done)) for piece in pieces[0]]
    xb_other = wires.to_core(after(start, done))
    core_own[0] = wires.to_core(after(ffn_in, done))

    place = jnp.stack([core, wires.seq]).astype(jnp.int32)
    prepared = [prepare(after(place, done, meta), 0, qkv_weight, rel_table, tables, weights), None]
    prepared[0], pieces[1] = prepared[0][:2], prepared[0][2:]
    done = (pieces[1], near[0][0], xb_other, core_own[0])
    far[0][0] = wires.to_seq(after(near[0][0], done))
    core_near[0][0] = wires.to_core(after(near[0][0], done))
    core_own[1] = wires.to_core(after(ffn_out, done))
    near[1][0] = wires.to_y(after(pieces[1][0], done))

    w_pairs, pe = prepared[0]
    outs = []

    def attend(group, *arrived):
        outs.append(attention(meta, 0, group, after(xb, arrived), xb_other, w_pairs, pe, rev))

    attend(split[0], done)
    done = (outs[0], far[0][0], core_near[0][0], core_own[1], near[0][1])
    far[0][1] = wires.to_seq(after(near[0][1], done))
    core_near[0][1] = wires.to_core(after(near[0][1], done))
    core_far[0][0] = wires.to_core(after(far[0][0], done))
    near[1][1] = wires.to_y(after(pieces[1][1], done))
    attend(split[1], done)
    o_own = [jnp.concatenate([item[0] for item in outs], axis=1)]
    done = (o_own, core_near[0][1], core_far[0][0], near[1][0])
    o_other = [wires.to_core(after(item, done)) for item in o_own]
    core_near[1][0] = wires.to_core(after(near[1][0], done))
    far[1][0] = wires.to_seq(after(near[1][0], done))
    prepared[1] = prepare(after(place, done), 1, qkv_weight, rel_table, tables)
    done = (prepared[1], far[0][1], o_other, core_near[1][0])
    core_far[0][1] = wires.to_core(after(far[0][1], done))

    def wire_args(n):
        return [
            item for m in range(2)
            for item in (weights[m], core_own[m], near[n][m], far[n][m], core_near[n][m], core_far[n][m])
        ]

    x = after(start, done)
    y, yb, mb, resid, pre, slope = token_step(meta, 0, o_own, o_other, x, out_weight, norm_params[0], wire_args(0))
    kept = [(xb, xb_other, outs, o_own, o_other, resid, pre, slope, mb)]

    done = (yb, far[1][0], near[1][1])
    xb, xb_other = yb, wires.to_core(after(yb, done))
    core_far[1][0] = wires.to_core(after(far[1][0], done))
    far[1][1] = wires.to_seq(after(near[1][1], done))
    core_near[1][1] = wires.to_core(after(near[1][1], done))
    d_final = wires.turn(after(cotangent[0], done))
    w_pairs, pe = prepared[1]
    outs = [attention(meta, 1, (0, 3), after(xb, done, xb_other), xb_other, w_pairs, pe, rev)]
    o_own = [outs[0][0]]
    done = (o_own, far[1][1], core_far[1][0], core_near[1][1], d_final)
    o_other = [wires.to_core(after(item, done)) for item in o_own]
    core_far[1][1] = wires.to_core(after(far[1][1], done))
    x = after(y, done, o_other, core_far[1][1])
    y, mb, df, dr, drb = token_both(meta, 1, o_own, o_other, x, out_weight, norm_params[1], d_final, wire_args(1))
    done = (drb,)
    drb_other = wires.to_core(after(drb, done))
    m_rows = [None, gather_start(after(mb, done), wires)]
    d_rows = [None, gather_start(after(df, done), wires)]
    done = (done, drb_other)
    saved, probs = ([item[k] for item in outs] for k in (1, 2))
    dqkv, dpos, dx_mine, dx_theirs = attention_grad(
        meta, 1, after(drb, done), drb_other, out_weight, saved, probs, pe, rev, w_pairs, tables
    )
    done = (dx_mine, d_rows[1][2], d_rows[1][1], m_rows[1][2], m_rows[1][1])
    d_rows[1] = gather_end(d_rows[1], wires, done)
    m_rows[1] = gather_end(m_rows[1], wires, done)
    dx_got = wires.to_core(after(dx_theirs, done))
    dpos_other = wires.to_core(after(dpos, done))
    output = wires.turn(after(y, done))
    m_rows[0] = gather_start(after(kept[0][-1], done), wires)
    keep, give, *down = hidden_grad(after(meta, done), 1, m_rows[1], d_rows[1], ffn_in, ffn_out)
    done = (down, m_rows[0][1], m_rows[0][2], dpos_other, dx_got, output)
    m_rows[0] = gather_end(m_rows[0], wires, done)
    first = [None, Flow(first_flow(keep, after(give, done), wires))]
    second = [None, Flow(second_flow(*after(down, done), wires))]
    projection = [None, None]
    projection_args = (xb, xb_other, [dqkv], o_own, o_other, drb, drb_other, [dpos], [dpos_other], rel_table, qkv_weight)

    xb, xb_other, outs, o_own, o_other, resid, pre, slope, mb = kept[0]
    w_pairs, pe = prepared[0]
    ups = [after(dr, done, second[1].ready), dx_mine, dx_got]
    df, dr, drb = token_grad(meta, 0, ups, pre, resid, slope, norm_params[0], wire_args(0))
    done = (df, m_rows[0][3])
    d_rows[0] = gather_start(after(df, done), wires)
    drb_other = wires.to_core(after(drb, done))
    packed = projection_grad(after(meta, done), 1, *projection_args)
    done = (packed, d_rows[0][2], d_rows[0][1], drb_other, first[1].under_way, second[1].under_way)
    d_rows[0] = gather_end(d_rows[0], wires, done)
    projection[1] = Flow(projection_flow(*after(packed, done), wires))
    first[1].step(done)
    second[1].step(done, first[1].ready)
    keep, give, *down = hidden_grad(after(meta, done, second[1].ready), 0, m_rows[0], d_rows[0], ffn_in, ffn_out)
    done = (down, projection[1].under_way, first[1].under_way, second[1].under_way)
    projection[1].step(done)
    first[1].step(done)
    first[0] = Flow(first_flow(keep, after(give, done, projection[1].ready), wires))
    second[0] = Flow(second_flow(*after(down, done), wires))
    done = (done, projection[1].ready, first[1].ready)
    saved, probs = ([item[k] for item in outs] for k in (1, 2))
    dqkv, dpos, dx_mine, dx_theirs = attention_grad(
        meta, 0, after(drb, done), drb_other, out_weight, saved, probs, pe, rev, w_pairs, tables
    )
    done = (dx_mine, projection[1].under_way, first[0].under_way, second[0].under_way, first[1].under_way)
    dpos_other = wires.to_core(after(dpos, done))
    projection[1].step(done)
    first[0].step(done, projection[1].ready)
    second[1].step(done)
    now = after(meta, done, projection[1].ready, first[0].ready, second[1].ready)
    packed = projection_grad(
        now, 0, xb, xb_other, [dqkv], o_own, o_other, drb, drb_other, [dpos], [dpos_other], rel_table, qkv_weight
    )
    done = (packed, projection[1].under_way, first[0].under_way, second[1].under_way)
    projection[0] = Flow(projection_flow(*after(packed, done), wires))
    projection[1].step(done, projection[0].ready)
    first[0].step(done, projection[1].ready)
    second[0].step(done, first[0].ready)
    first[1].finish(second[0].ready)
    second[1].finish(second[0].ready)
    done = (projection[0].under_way, second[0].ready)
    projection[0].step(done)
    dx_got = wires.to_core(after(dx_theirs, projection[0].ready))
    d_input = wires.turn((dr + dx_mine + dx_got.astype(F32)).astype(BF)).astype(F32)
    done = (projection[0].under_way, projection[1].under_way, first[0].under_way)
    projection[0].step(done)
    projection[1].finish(projection[0].ready)
    first[0].finish(projection[0].ready)
    done = (projection[0].under_way, second[0].under_way)
    projection[0].step(done)
    second[0].step(projection[0].ready)
    parts = [flow.finish() for flow in projection]
    first, second = ([flow.finish() for flow in flows] for flows in (first, second))
    grad_qkv = jnp.stack([jnp.stack(part[:3]) for part in parts])
    grad_out = jnp.stack([part[3] for part in parts])
    grad_rel = jnp.stack([part[4] for part in parts])
    grad_in = jnp.stack(first)
    grad_down, grad_norms = (jnp.stack([item[k] for item in second]) for k in range(2))
    return (output[None], d_input[None], grad_qkv, grad_out, grad_rel, grad_in, grad_down, grad_norms[:, None])


def solution(mesh):
    placed = (
        P(("rows", "col"), "seq", None),
        P(("rows", "col"), None),
        P(),
        P(),
        P(),
        P(None, None, "col"),
        P(None, None, "col"),
        P(),
        P(("rows", "col"), "seq", None),
    )
    return jax.shard_map(
        per_device,
        mesh=mesh,
        in_specs=placed,
        out_specs=(
            P(("rows", "col"), "seq", None),
            P(("rows", "col"), "seq", None),
            P(None, None, ("seq", "rows"), "col"),
            P(None, ("seq", "rows"), "col"),
            P(None, ("seq", "rows"), "col"),
            P(None, ("seq", "rows"), "col"),
            P(None, ("seq", "rows"), "col"),
            P(None, "col", ("seq", "rows")),
        ),
        check_vma=False,
    )
```
